256 devices in a mesh: row: 32 (over z, y), col: 8 (over x, core).
Axes of the slice: x: 4, y: 4, z: 8, core: 2. Of those that a mesh axis runs over, the one named last changes fastest.
Arguments:
- features: bfloat16 [256, 128, 640], P('row', 'col'), may hold values from -6 to 6
- cotangent: bfloat16 [256, 128, 640], P('row', 'col'), may hold values from -8 to 8
- conv_weight: bfloat16 [3, 3, 640, 640], replicated, may hold values from -0.078125 to 0.078125
- gain: float32 [640], replicated, may hold values from 0.25 to 1.75
- shift: float32 [640], replicated, may hold values from -3 to 3
Outputs:
- block_input_gradient: bfloat16 [256, 128, 640], P('row', 'col')
- weight_grad: float32 [3, 3, 640, 640], P(None, None, 'row', 'col')
- norm_gain_gradient: float32 [640], replicated
- norm_shift_gradient: float32 [640], replicated
- time_bias_grad: float32 [640], replicated
The draws below stay inside these ranges and needn't reach their ends.
All inputs are finite; a program needn't handle non-finite values.
Results may differ from the reference program's by a relative error of at most 0.0095.
Values may be sent and summed in bfloat16 or wider, within the bound.
No kernel may reach another device: no remote copies, remote signals or barrier semaphores. Data moves between devices by JAX's collectives and lax.ppermute only.
A program may use at most 128 MiB of HBM per device.

```python
import jax
import jax.numpy as jnp
from jax import lax

C = 640
GW = 40
GROUPS = 16
TH = 8
NH = 256
NW = 128


def draw_cotangent(key, part):
    key = jax.random.fold_in(key, 11)
    noise_key, factor_key, offset_key = jax.random.split(key, 3)
    tile_count = NH // TH
    noise_part = jax.random.normal(noise_key, (NH, NW, C), jnp.float32)
    channel_offset = 0.3 + 0.6 * jax.random.uniform(offset_key, (C,), jnp.float32)
    tile_factor = jnp.exp(jax.random.uniform(factor_key, (tile_count, C), jnp.float32, -0.7, 0.7))
    pixel_factor = jnp.repeat(tile_factor, TH, axis=0)[:, None, :]
    height_ramp = jnp.arange(NH, dtype=jnp.float32)[:, None, None] / NH
    width_ramp = jnp.arange(NW, dtype=jnp.float32)[None, :, None] / NW
    position_ramp = 0.5 + height_ramp + width_ramp
    values = jnp.clip(noise_part * pixel_factor + position_ramp * channel_offset, -8.0, 8.0)
    return values.astype(jnp.bfloat16)


def shard_levels(rng, extent, shards, least, top_value):
    level, own = 1.0, jax.random.fold_in(rng, 6)
    for axis_at, shards_of in shards:
        heights = jnp.exp(jax.random.uniform(jax.random.fold_in(own, axis_at), (shards_of,), jnp.float32, least / len(shards), top_value / len(shards)))
        level = level * jnp.repeat(heights, extent[axis_at] // shards_of).reshape([-1 if axis == axis_at else 1 for axis in range(len(extent))])
    return level


def gaussian(stream_key, shape, width, most, cuts=(), kind=jnp.bfloat16):
    loudness = shard_levels(stream_key, shape, cuts, -0.22, 0.18) if cuts else 1.0
    drawn = jax.random.normal(stream_key, shape, jnp.float32) * width * loudness
    return jnp.minimum(jnp.maximum(drawn, -most), most).astype(kind)


def setup_inputs(seed: int = 0) -> dict:
    splits = jax.random.split(jax.random.key(seed), 6)
    features = gaussian(splits[0], (NH, NW, C), 1.0, 6.0, ((0, 32), (1, 8)))
    cotangent = draw_cotangent(jax.random.fold_in(splits[5], 71), 0)
    conv_weight = gaussian(splits[2], (3, 3, C, C), (9 * C) ** -0.5, 0.078125)
    gain = jnp.clip(1.0 + 0.15 * jax.random.normal(splits[3], (C,), jnp.float32), 0.25, 1.75)
    shift = gaussian(splits[4], (C,), 0.5, 3.0, (), jnp.float32)
    return dict(features=features, cotangent=cotangent, conv_weight=conv_weight, gain=gain, shift=shift)


def group_total(values):
    return values.reshape(GROUPS, GW).sum(1)

def per_channel(values):
    return jnp.repeat(values, GW)

def reference(features, cotangent, conv_weight, gain, shift):
    element_count = float(NH * NW * GW)
    feat = features.astype(jnp.float32)
    mean = group_total(feat.sum((0, 1))) / element_count
    centered_input = feat - per_channel(mean)
    var = group_total((centered_input * centered_input).sum((0, 1))) / element_count
    inverse_deviation = per_channel(lax.rsqrt(var + 1e-05))
    normalized_input = centered_input * inverse_deviation
    preactivation = normalized_input * gain + shift
    sig = jax.nn.sigmoid(preactivation)
    hidden = (preactivation * sig).astype(jnp.bfloat16)
    grad = cotangent.astype(jnp.float32)
    time_bias_grad = grad.sum((0, 1))
    hid_pad = jnp.pad(hidden.astype(jnp.float32), ((1, 1), (1, 1), (0, 0)))
    grad_pad = jnp.pad(grad, ((1, 1), (1, 1), (0, 0)))
    weight_f = conv_weight.astype(jnp.float32)
    grad_flat = grad.reshape(NH * NW, C)
    taps = []
    back = jnp.zeros((NH * NW, C), jnp.float32)
    for i in range(3):
        row_taps = []
        for j in range(3):
            window = hid_pad[i:i + NH, j:j + NW].reshape(NH * NW, C)
            row_taps.append(jnp.dot(window.T, grad_flat, precision=lax.Precision.HIGHEST))
            moved = grad_pad[2 - i:2 - i + NH, 2 - j:2 - j + NW].reshape(NH * NW, C)
            back = back + jnp.dot(moved, weight_f[i, j].T, precision=lax.Precision.HIGHEST)
        taps.append(jnp.stack(row_taps))
    weight_grad = jnp.stack(taps)
    dh = back.reshape(NH, NW, C)
    preactivation_grad = dh * sig * (1.0 + preactivation * (1.0 - sig))
    norm_shift_gradient = preactivation_grad.sum((0, 1))
    norm_gain_gradient = (preactivation_grad * normalized_input).sum((0, 1))
    first_moment = per_channel(group_total(gain * norm_shift_gradient))
    second_moment = per_channel(group_total(gain * norm_gain_gradient))
    block_input_gradient = inverse_deviation * (preactivation_grad * gain - first_moment / element_count - normalized_input * second_moment / element_count)
    return (block_input_gradient.astype(jnp.bfloat16), weight_grad, norm_gain_gradient, norm_shift_gradient, time_bias_grad)
```

```python
import numpy as np

import jax
import jax.numpy as jnp
from jax import lax
from jax.experimental import pallas as pl
from jax.experimental.pallas import tpu as pltpu
from jax.sharding import Mesh
from jax.sharding import PartitionSpec as P

C = 640
GW = 40
GROUPS = 16
TR, TC = 8, 16
PIX = TR * TC
NZ, NY, NX = 8, 4, 4
PEERS = NY * NX
ROWS = NY * TR
PL, QL = NZ * 32, 128
NQ = 80
TOTAL = float(NZ * PEERS * 2 * PIX * GW)
VMEM_LIMIT = 48 * 1024 * 1024


def feature_columns():
    out = np.full((1, NY * PL), -1, np.int32)
    for y in range(NY):
        for z in range(NZ):
            for k in range(20):
                out[0, y * PL + z * 32 + k] = z * 80 + y * 20 + k
    return out


def cotangent_columns():
    out = np.full((1, NX * QL), -10000, np.int32)
    for x in range(NX):
        out[0, x * QL : x * QL + NQ] = x * 160 + np.arange(NQ)
    return out


def vmem():
    return pl.BlockSpec(memory_space=pltpu.VMEM)


def group_matrix():
    chan = lax.broadcasted_iota(jnp.int32, (C, 128), 0)
    group = lax.broadcasted_iota(jnp.int32, (C, 128), 1)
    low = group * GW
    return jnp.where((chan >= low) & (chan < low + GW), 1.0, 0.0).astype(jnp.float32)


def exact_dot(a, b, dims):
    return lax.dot_general(
        a, b, (dims, ((), ())), precision=lax.Precision.HIGHEST, preferred_element_type=jnp.float32
    )


def pack_kernel(feat_ref, cot_ref, first_ref, second_ref, fcol_ref, ccol_ref, out_ref, stat_ref, bias_ref):
    feat = feat_ref[...]
    x = feat.astype(jnp.float32)
    groups = group_matrix()
    total = jnp.broadcast_to(x.sum(0, keepdims=True), (8, C))
    mean = exact_dot(total, groups, ((1,), (0,))) / float(PIX * GW)
    centre = x - exact_dot(mean, groups, ((1,), (1,)))[:1]
    squares = jnp.broadcast_to((centre * centre).sum(0, keepdims=True), (8, C))
    stat_ref[0] = mean
    stat_ref[1] = exact_dot(squares, groups, ((1,), (0,)))
    bias_ref[...] = jnp.broadcast_to(cot_ref[...].astype(jnp.float32).sum(0, keepdims=True), (8, C))
    rows = lax.broadcasted_iota(jnp.int32, (C, NY * PL), 0)
    pick = (rows == fcol_ref[...]).astype(jnp.float32).astype(jnp.bfloat16)
    moved = jnp.dot(feat, pick, preferred_element_type=jnp.float32).astype(jnp.bfloat16)
    rows = lax.broadcasted_iota(jnp.int32, (C, NX * QL), 0)
    pick = (rows == ccol_ref[...]).astype(jnp.float32).astype(jnp.bfloat16)
    first = jnp.dot(first_ref[...], pick, preferred_element_type=jnp.float32).astype(jnp.bfloat16)
    second = jnp.dot(second_ref[...], pick, preferred_element_type=jnp.float32).astype(jnp.bfloat16)
    for y in range(NY):
        for xx in range(NX):
            p = y * NX + xx
            out_ref[p, :, :PL] = moved[:, y * PL : (y + 1) * PL]
            out_ref[p, :, PL : PL + QL] = first[:, xx * QL : (xx + 1) * QL]
            out_ref[p, :, PL + QL :] = second[:, xx * QL : (xx + 1) * QL]


def back_kernel(top_ref, cot_ref, bottom_ref, left_ref, right_ref, w_ref, out_ref, shifted, acc):
    step = pl.program_id(0)
    rows = (TR + 2) * TC

    @pl.when(step == 0)
    def _():
        full = jnp.concatenate([top_ref[...], cot_ref[...], bottom_ref[...]], axis=0)
        shifted[1] = full
        wide = full.astype(jnp.float32)
        col = lax.broadcasted_iota(jnp.int32, (rows, C), 0) % TC
        left = left_ref[...].astype(jnp.float32)
        right = right_ref[...].astype(jnp.float32)
        left = jnp.broadcast_to(left[:, None, :], (TR + 2, TC, C)).reshape(rows, C)
        right = jnp.broadcast_to(right[:, None, :], (TR + 2, TC, C)).reshape(rows, C)
        shifted[0] = jnp.where(col == 0, left, pltpu.roll(wide, 1, 0)).astype(jnp.bfloat16)
        shifted[2] = jnp.where(col == TC - 1, right, pltpu.roll(wide, rows - 1, 0)).astype(jnp.bfloat16)
        acc[...] = jnp.zeros_like(acc)

    i, j = step // 3, step % 3
    lhs = shifted[2 - j, pl.ds(pl.multiple_of((2 - i) * TC, TC), PIX), :]
    acc[...] += lax.dot_general(
        lhs, w_ref[0, 0], (((1,), (1,)), ((), ())), preferred_element_type=jnp.float32
    )

    @pl.when(step == 8)
    def _():
        out_ref[...] = acc[...]


def terms_kernel(core_ref, own_ref, other_ref, above_ref, below_ref, par_ref, out_ref, hid, strips, cot3):
    core = core_ref[0]
    mean, scale, shift = par_ref[0:1], par_ref[1:2], par_ref[2:3]

    def put(block, peer, side):
        a = (block.astype(jnp.float32) - mean) * scale + shift
        value = (a * jax.nn.sigmoid(a)).astype(jnp.bfloat16)
        y, xx = peer // NX, peer % NX
        for r in range(TR):
            at = (y * TR + r) * 128 + xx * 32 + side * TC
            hid[pl.ds(pl.multiple_of(at, TC), TC), :] = value[r * TC : (r + 1) * TC]

    for peer in range(PEERS):
        put(own_ref[peer, :, :PL], peer, core)
        put(other_ref[peer], peer, 1 - core)
        y, xx = peer // NX, peer % NX
        for side in range(2):
            lanes = slice(PL + side * QL, PL + (side + 1) * QL)
            for r in range(TR):
                at = (y * TR + r + 1) * 128 + xx * 32 + side * TC
                strips[at : at + TC, :] = own_ref[peer, r * TC : (r + 1) * TC, lanes]
    strips[0:128, :] = above_ref[...]
    strips[(ROWS + 1) * 128 :, :] = below_ref[...]
    lane = lax.broadcasted_iota(jnp.int32, (NQ, 128), 1)
    for row in range(ROWS + 2):
        at = slice(row * 128, (row + 1) * 128)
        turned = strips[at, :].astype(jnp.float32).T[:NQ]
        before = jnp.where(lane == 0, 0.0, pltpu.roll(turned, 1, 1))
        after = jnp.where(lane == 127, 0.0, pltpu.roll(turned, 127, 1))
        cot3[0:NQ, at] = after.astype(jnp.bfloat16)
        cot3[NQ : 2 * NQ, at] = turned.astype(jnp.bfloat16)
        cot3[2 * NQ :, at] = before.astype(jnp.bfloat16)
    for i in range(3):
        lhs = cot3[:, (2 - i) * 128 : (2 - i) * 128 + ROWS * 128]
        turned = jnp.dot(lhs, hid[...], preferred_element_type=jnp.float32)
        out_ref[:, i] = turned.T.astype(jnp.bfloat16).reshape(NZ, 32, 3 * NQ)


def merge(stats, count):
    means, squares = stats[:, 0], stats[:, 1]
    mean = means.mean(0)
    return jnp.stack([mean, squares.sum(0) + count * ((means - mean) ** 2).sum(0)])


def flip(value):
    return lax.ppermute(value, "core", [(0, 1), (1, 0)])


def share(value, axes, count):
    return lax.all_to_all(jnp.broadcast_to(value, (count,) + value.shape), axes, 0, 0)


def per_channel(values):
    return jnp.repeat(values, GW)


def group_total(values):
    return values.reshape(GROUPS, GW).sum(1)


def body(features, cotangent, conv_weight, gain, shift):
    f32, bf16 = jnp.float32, jnp.bfloat16
    core, y = lax.axis_index("core"), lax.axis_index("y")
    feat = features.reshape(PIX, C)
    cot = cotangent.reshape(PIX, C)
    cot_other = flip(cot)
    up = [(k, k + 1) for k in range(NZ * NY - 1)]
    top = lax.ppermute(cotangent[TR - 1], ("z", "y"), up)
    bottom = lax.ppermute(cotangent[0], ("z", "y"), [(b, a) for a, b in up])
    edges = jnp.concatenate([top[None], cotangent, bottom[None]], axis=0)
    side = [(k, k + 1) for k in range(2 * NX - 1)]
    left = lax.ppermute(edges[:, TC - 1], ("x", "core"), side)
    right = lax.ppermute(edges[:, 0], ("x", "core"), [(b, a) for a, b in side])

    first = jnp.where(core == 0, cot, cot_other)
    second = jnp.where(core == 0, cot_other, cot)
    fcol = jnp.asarray(feature_columns())
    ccol = jnp.asarray(cotangent_columns()) + core * NQ
    packed, stats, bias = pl.pallas_call(
        pack_kernel,
        out_shape=(
            jax.ShapeDtypeStruct((PEERS, PIX, PL + 2 * QL), bf16),
            jax.ShapeDtypeStruct((2, 8, 128), f32),
            jax.ShapeDtypeStruct((8, C), f32),
        ),
        in_specs=[vmem()] * 6,
        out_specs=(vmem(), vmem(), vmem()),
        compiler_params=pltpu.CompilerParams(vmem_limit_bytes=VMEM_LIMIT),
        name="pack",
    )(feat, cot, first, second, fcol, ccol)

    stats = merge(share(stats[:, 0], ("y", "x"), PEERS), float(PIX * GW))
    slab = lax.all_to_all(packed, ("y", "x"), 0, 0)
    slab_other = flip(slab[:, :, :PL])
    stats = merge(share(stats, "z", NZ), float(PEERS * PIX * GW))
    stats = merge(jnp.stack([stats, flip(stats)]), float(NZ * PEERS * PIX * GW))
    mean = per_channel(stats[0, :GROUPS])
    rstd = per_channel(lax.rsqrt(stats[1, :GROUPS] / TOTAL + 1e-05))

    slab_cot = slab[:, :, PL:].reshape(NY, NX, TR, TC, 2, QL)
    last_row = slab_cot[NY - 1, :, TR - 1].transpose(0, 2, 1, 3).reshape(128, QL)
    first_row = slab_cot[0, :, 0].transpose(0, 2, 1, 3).reshape(128, QL)
    slabs = [(k, k + 1) for k in range(NZ - 1)]
    above = lax.ppermute(last_row, "z", slabs)
    below = lax.ppermute(first_row, "z", [(b, a) for a, b in slabs])

    back = pl.pallas_call(
        back_kernel,
        grid=(9,),
        out_shape=jax.ShapeDtypeStruct((PIX, C), f32),
        in_specs=[vmem()] * 5 + [pl.BlockSpec((1, 1, C, C), lambda t: (t // 3, t % 3, 0, 0))],
        out_specs=vmem(),
        scratch_shapes=[
            pltpu.VMEM((3, (TR + 2) * TC, C), bf16),
            pltpu.VMEM((PIX, C), f32),
        ],
        compiler_params=pltpu.CompilerParams(vmem_limit_bytes=VMEM_LIMIT),
        cost_estimate=pl.CostEstimate(flops=2 * PIX * 9 * C * C, bytes_accessed=18 * C * C, transcendentals=0),
        name="back",
    )(top, cot, bottom, left, right, conv_weight)

    xhat = (feat.astype(f32) - mean) * rstd
    act = xhat * gain + shift
    sig = jax.nn.sigmoid(act)
    da = back * sig * (1.0 + act * (1.0 - sig))
    sums = jnp.stack([da.sum(0), (da * xhat).sum(0), bias[0]])
    sums = sums + flip(sums)
    sums = share(sums, ("y", "x"), PEERS).sum(0)

    params = jnp.stack([mean, rstd * gain, shift]).reshape(3, NZ, NY, 20)
    params = lax.dynamic_index_in_dim(params, y, 2, keepdims=False)
    params = jnp.pad(params, ((0, 5), (0, 0), (0, 12))).reshape(8, PL)
    terms = pl.pallas_call(
        terms_kernel,
        out_shape=jax.ShapeDtypeStruct((NZ, 3, 32, 3 * NQ), bf16),
        in_specs=[pl.BlockSpec(memory_space=pltpu.SMEM)] + [vmem()] * 5,
        out_specs=vmem(),
        scratch_shapes=[
            pltpu.VMEM((ROWS * 128, PL), bf16),
            pltpu.VMEM(((ROWS + 2) * 128, QL), bf16),
            pltpu.VMEM((3 * NQ, (ROWS + 2) * 128), bf16),
        ],
        compiler_params=pltpu.CompilerParams(vmem_limit_bytes=VMEM_LIMIT),
        cost_estimate=pl.CostEstimate(
            flops=2 * PIX * 9 * C * C, bytes_accessed=4 << 20, transcendentals=ROWS * 128 * PL
        ),
        name="terms",
    )(core.reshape(1), slab, slab_other, above, below, params)
    pieces = lax.all_to_all(terms, "z", 0, 0)
    weight_grad = pieces.astype(f32).sum(0)[:, :20].reshape(3, 20, 3, NQ).transpose(0, 2, 1, 3)

    sums = share(sums, "z", NZ).sum(0)
    shift_grad, gain_grad, bias_grad = sums[0], sums[1], sums[2]
    moment1 = per_channel(group_total(gain * shift_grad))
    moment2 = per_channel(group_total(gain * gain_grad))
    grad = rstd * (da * gain - moment1 / TOTAL - xhat * moment2 / TOTAL)
    return grad.astype(bf16).reshape(features.shape), weight_grad, gain_grad, shift_grad, bias_grad


def solution(mesh):
    grid = Mesh(mesh.devices.reshape(NZ, NY, NX, 2), ("z", "y", "x", "core"))
    rows, cols = ("z", "y"), ("x", "core")
    tiled = P(rows, cols, None)
    return jax.shard_map(
        body,
        mesh=grid,
        in_specs=(tiled, tiled, P(), P(), P()),
        out_specs=(tiled, P(None, None, rows, cols), P(), P(), P()),
        check_vma=False,
    )
```

```python
import numpy as np

import jax
import jax.numpy as jnp
from jax import lax
from jax.experimental import pallas as pl
from jax.experimental.pallas import tpu as pltpu
from jax.sharding import Mesh
from jax.sharding import PartitionSpec as P

C = 640
GW = 40
TR, TC = 8, 16
PIX = TR * TC
NZ, NY, NX = 8, 4, 4
PEERS = NY * NX
ROWS = NY * TR
NQ = 80
CHIP = float(2 * PIX * GW)
TOTAL = float(NZ * PEERS) * CHIP
VMEM_LIMIT = 48 * 1024 * 1024
F_ROWS, C_ROWS, S_ROWS = 160, 160, 16
G_ROWS = F_ROWS + C_ROWS + S_ROWS
W_ROWS, V_ROWS = 64, 32
f32, bf16 = jnp.float32, jnp.bfloat16


def slab_channels(y):
    z, k = np.arange(NZ)[:, None], np.arange(20)[None]
    chans = z * 80 + y * 20 + k
    return chans[:, :16].reshape(-1), chans[:, 16:].reshape(-1)


def feature_columns():
    parts = [slab_channels(y) for y in range(NY)]
    return np.concatenate([p[0] for p in parts] + [p[1] for p in parts])[None].astype(np.int32)


def cotangent_columns(side):
    out = np.full((1, C), -10000, np.int32)
    for x in range(NX):
        out[0, x * 128 + side * 64 : x * 128 + side * 64 + 64] = x * 160 + np.arange(64)
        at = 512 + x * 32 + side * 16
        out[0, at : at + 16] = x * 160 + 64 + np.arange(16)
    return out


def term_columns():
    main, rest = slab_channels(0)
    return np.concatenate([main] + [rest] * 4)[None].astype(np.int32)


def vmem():
    return pl.BlockSpec(memory_space=pltpu.VMEM)


def smem():
    return pl.BlockSpec(memory_space=pltpu.SMEM)


def params(**kw):
    return pltpu.CompilerParams(vmem_limit_bytes=VMEM_LIMIT, **kw)


def group_matrix():
    chan = lax.broadcasted_iota(jnp.int32, (C, 128), 0)
    low = lax.broadcasted_iota(jnp.int32, (C, 128), 1) * GW
    return jnp.where((chan >= low) & (chan < low + GW), 1.0, 0.0).astype(f32)


def exact_dot(a, b, over):
    return lax.dot_general(
        a, b, (((1,), (over,)), ((), ())), precision=lax.Precision.HIGHEST, preferred_element_type=f32
    )


def rows8(row):
    return jnp.broadcast_to(row, (8, row.shape[1]))


def pick(columns):
    rows = lax.broadcasted_iota(jnp.int32, (C, columns.shape[1]), 0)
    return (rows == columns).astype(f32)


def three(value):
    high = value.astype(bf16).astype(f32)
    rest = value - high
    middle = rest.astype(bf16).astype(f32)
    return high, middle, rest - middle


def lanes32(value):
    group = lax.broadcasted_iota(jnp.int32, (32, 128), 1) // 32
    out = []
    for a in range(4):
        acc = jnp.zeros((32, 128), f32)
        for g in range(4):
            moved = pltpu.roll(value[32 * g : 32 * g + 32], (32 * (g - a)) % 128, 1)
            acc = jnp.where(group == g, moved, acc)
        out.append(acc)
    return out


def pack_kernel(core_ref, feat_ref, cot_ref, feat2_ref, cot2_ref, fcol_ref, c0_ref, c1_ref, out_ref, bias_ref):
    core = core_ref[0]
    feat, cot = feat_ref[...], cot_ref[...]
    x, x2 = feat.astype(f32), feat2_ref[...].astype(f32)
    groups = group_matrix()
    total = x.sum(0, keepdims=True) + x2.sum(0, keepdims=True)
    mean = exact_dot(rows8(total), groups, 0) / CHIP
    wide = exact_dot(mean, groups, 1)[:1]
    squares = ((x - wide) ** 2).sum(0, keepdims=True) + ((x2 - wide) ** 2).sum(0, keepdims=True)
    squares = exact_dot(rows8(squares), groups, 0)
    pieces = three(mean[:1]) + three(squares[:1])
    row = lax.broadcasted_iota(jnp.int32, (S_ROWS, 128), 0)
    stats = jnp.zeros((S_ROWS, 128), f32)
    for k in range(6):
        stats = jnp.where(row == k, pieces[k], stats)
    stats = stats.astype(bf16)
    bias_ref[...] = rows8(cot.astype(f32).sum(0, keepdims=True))

    moved = jnp.dot(feat, pick(fcol_ref[...]).astype(bf16), preferred_element_type=f32)
    own = jnp.where(core == 0, c0_ref[...], c1_ref[...]) + core * NQ
    other = jnp.where(core == 0, c1_ref[...], c0_ref[...]) + core * NQ
    terms = jnp.dot(cot, pick(own).astype(bf16), preferred_element_type=f32)
    terms = terms + jnp.dot(cot2_ref[...], pick(other).astype(bf16), preferred_element_type=f32)
    moved_rest = lanes32(moved[:, 512:])
    terms_rest = lanes32(terms[:, 512:])
    for y in range(NY):
        for xx in range(NX):
            p = y * NX + xx
            out_ref[p, 0:128] = moved[:, y * 128 : (y + 1) * 128].astype(bf16)
            out_ref[p, 128:160] = moved_rest[y].astype(bf16)
            out_ref[p, 160:288] = terms[:, xx * 128 : (xx + 1) * 128].astype(bf16)
            out_ref[p, 288:320] = terms_rest[xx].astype(bf16)
            out_ref[p, 320:336] = stats


def merge(means, squares, count):
    n = means.shape[0]
    mean = means.sum(0, keepdims=True) / n
    return mean, squares.sum(0, keepdims=True) + count * ((means - mean) ** 2).sum(0, keepdims=True)


def stats_kernel(slab_ref, out_ref):
    got = slab_ref[...].astype(f32)
    mean, squares = merge(
        got[:, 0] + got[:, 1] + got[:, 2], got[:, 3] + got[:, 4] + got[:, 5], CHIP
    )
    row = lax.broadcasted_iota(jnp.int32, (8, 128), 0)
    block = jnp.where(row == 0, mean, jnp.where(row == 1, squares, 0.0))
    for z in range(NZ):
        out_ref[z] = block


def cot_rows(main, rest, g, side):
    lane = lax.broadcasted_iota(jnp.int32, main.shape, 1)
    main = pltpu.roll(main, 64, 1) if side else main
    return jnp.where(lane < 64, main, pltpu.roll(rest, (64 - 32 * g - 16 * side) % 128, 1))


def split_kernel(slab_ref, feat_ref, first_ref, last_ref):
    feat_ref[...] = slab_ref[:, :F_ROWS]
    for xx in range(NX):
        for side in range(2):
            at = slice(xx * 32 + side * TC, xx * 32 + (side + 1) * TC)
            peer = xx
            block = cot_rows(slab_ref[peer, 160:176].astype(f32), slab_ref[peer, 288:304].astype(f32), 0, side)
            first_ref[at] = block.astype(bf16)
            peer = (NY - 1) * NX + xx
            block = cot_rows(slab_ref[peer, 272:288].astype(f32), slab_ref[peer, 304:320].astype(f32), 3, side)
            last_ref[at] = block.astype(bf16)


def back_kernel(core_ref, cot_ref, cot2_ref, mine_ref, theirs_ref, outer_ref, w_ref, out_ref, shifted, acc):
    step = pl.program_id(0)
    rows = (TR + 2) * TC

    @pl.when(step == 0)
    def _():
        lower = core_ref[0] == 0
        mine, theirs = mine_ref[...].astype(f32), theirs_ref[...].astype(f32)
        top, bottom = jnp.where(lower, mine, theirs), jnp.where(lower, theirs, mine)
        own_top, other_top = jnp.where(lower, top[:TC], top[TC:]), jnp.where(lower, top[TC:], top[:TC])
        own_bot, other_bot = jnp.where(lower, bottom[:TC], bottom[TC:]), jnp.where(lower, bottom[TC:], bottom[:TC])
        wide = jnp.concatenate([own_top, cot_ref[...].astype(f32), own_bot], axis=0)
        near = jnp.concatenate([other_top, cot2_ref[...].astype(f32), other_bot], axis=0)
        near = near.reshape(TR + 2, TC, C)
        inner = jnp.where(lower, near[:, :1], near[:, TC - 1 :])
        outer = outer_ref[...].astype(f32)[:, None, :]
        left, right = jnp.where(lower, outer, inner), jnp.where(lower, inner, outer)
        left = jnp.broadcast_to(left, (TR + 2, TC, C)).reshape(rows, C)
        right = jnp.broadcast_to(right, (TR + 2, TC, C)).reshape(rows, C)
        col = lax.broadcasted_iota(jnp.int32, (rows, C), 0) % TC
        shifted[0] = jnp.where(col == 0, left, pltpu.roll(wide, 1, 0)).astype(bf16)
        shifted[1] = wide.astype(bf16)
        shifted[2] = jnp.where(col == TC - 1, right, pltpu.roll(wide, rows - 1, 0)).astype(bf16)
        acc[...] = jnp.zeros_like(acc)

    i, j = step // 3, step % 3
    lhs = shifted[2 - j, pl.ds(pl.multiple_of((2 - i) * TC, TC), PIX), :]
    acc[...] += lax.dot_general(lhs, w_ref[0, 0], (((1,), (1,)), ((), ())), preferred_element_type=f32)

    @pl.when(step == 8)
    def _():
        out_ref[...] = acc[...]


def sums_kernel(y_ref, stat_ref, feat_ref, back_ref, gain_ref, shift_ref, bias_ref, col_ref,
                row_ref, da_ref, par_ref, out_ref, block):
    got = stat_ref[...]
    mean, squares = merge(got[:, 0], got[:, 1], PEERS * CHIP)
    groups = group_matrix()
    rstd = exact_dot(rows8(lax.rsqrt(squares / TOTAL + 1e-05)), groups, 1)[:1]
    mean = exact_dot(rows8(mean), groups, 1)[:1]
    gain, shift = gain_ref[...], shift_ref[...]
    row = lax.broadcasted_iota(jnp.int32, (8, C), 0)
    row_ref[...] = jnp.where(row == 0, mean, rstd)
    table = jnp.where(row == 0, mean, jnp.where(row == 1, rstd * gain, jnp.where(row == 2, shift, 0.0)))
    par_ref[...] = exact_dot(table, pick(col_ref[...] + y_ref[0] * 20), 0)
    xhat = (feat_ref[...].astype(f32) - mean) * rstd
    act = xhat * gain + shift
    sig = jax.nn.sigmoid(act)
    da = back_ref[...] * sig * (1.0 + act * (1.0 - sig))
    da_ref[...] = da
    sums = (da.sum(0, keepdims=True), (da * xhat).sum(0, keepdims=True), bias_ref[:1])
    block[...] = jnp.zeros_like(block)
    for s in range(3):
        for t in range(5):
            block[5 * s + t : 5 * s + t + 1] = sums[s][:, 128 * t : 128 * t + 128]
    value = block[...]
    for p in range(2 * PEERS):
        out_ref[p] = value


def terms_kernel(core_ref, own_ref, other_ref, above_ref, below_ref, par_ref, out_ref, hid, strips, cot3, rest):
    core = core_ref[0]

    def put(block, peer, side):
        y, xx = peer // NX, peer % NX

        def silu(x, lanes):
            a = (x.astype(f32) - par_ref[0:1, lanes]) * par_ref[1:2, lanes] + par_ref[2:3, lanes]
            return a * jax.nn.sigmoid(a)

        main = silu(block[:128], slice(0, 128)).astype(bf16)
        tail = silu(block[128:], slice(128, 256))
        for g in range(4):
            low = pltpu.roll(tail, (128 - 32 * g) % 128, 1).astype(bf16)
            for h in range(2):
                r = 2 * g + h
                at = pl.ds(pl.multiple_of((y * TR + r) * 128 + xx * 32 + side * TC, TC), TC)
                hid[at, 0:128] = main[r * TC : (r + 1) * TC]
                hid[at, 128:256] = low[h * TC : (h + 1) * TC]

    for peer in range(PEERS):
        put(own_ref[peer, :F_ROWS], peer, core)
        put(other_ref[peer], peer, 1 - core)
        y, xx = peer // NX, peer % NX
        tail = own_ref[peer, 288:320].astype(f32)
        for g in range(4):
            main = own_ref[peer, 160 + 32 * g : 192 + 32 * g].astype(f32)
            for side in range(2):
                value = cot_rows(main, tail, g, side).astype(bf16)
                for h in range(2):
                    at = (y * TR + 2 * g + h + 1) * 128 + xx * 32 + side * TC
                    strips[at : at + TC] = value[h * TC : (h + 1) * TC]
    strips[0:128] = above_ref[...]
    strips[(ROWS + 1) * 128 :] = below_ref[...]
    lane = lax.broadcasted_iota(jnp.int32, (NQ, 128), 1)
    for row in range(ROWS + 2):
        at = slice(row * 128, (row + 1) * 128)
        turned = strips[at].astype(f32).T[:NQ]
        before = jnp.where(lane == 0, 0.0, pltpu.roll(turned, 1, 1))
        after = jnp.where(lane == 127, 0.0, pltpu.roll(turned, 127, 1))
        cot3[0:NQ, at] = after.astype(bf16)
        cot3[NQ : 2 * NQ, at] = turned.astype(bf16)
        cot3[2 * NQ : 3 * NQ, at] = before.astype(bf16)
    cot3[3 * NQ :] = jnp.zeros((16, (ROWS + 2) * 128), bf16)
    rest[...] = jnp.zeros_like(rest)
    for i in range(3):
        lhs = cot3[:, (2 - i) * 128 : (2 - i) * 128 + ROWS * 128]
        turned = jnp.dot(lhs, hid[...], preferred_element_type=f32).T
        for z in range(NZ):
            out_ref[z, 16 * i : 16 * i + 16] = turned[16 * z : 16 * z + 16].astype(bf16)
            rest[z, 4 * i : 4 * i + 4] = turned[128 + 4 * z : 132 + 4 * z]
    for z in range(NZ):
        out_ref[z, 48:64] = rest[z].astype(bf16)


def join_kernel(sums_ref, terms_ref, out_ref):
    value = sums_ref[0]
    for p in range(1, 2 * PEERS):
        value = value + sums_ref[p]
    high, middle, low = three(value)
    zero = jnp.zeros_like(value)
    block = jnp.concatenate(
        [jnp.concatenate([high, middle], axis=1), jnp.concatenate([low, zero], axis=1)], axis=0
    ).astype(bf16)
    for z in range(NZ):
        out_ref[z, :W_ROWS] = terms_ref[z]
        out_ref[z, W_ROWS:] = block


def final_kernel(got_ref, feat_ref, da_ref, row_ref, gain_ref,
                 grad_ref, weight_ref, gain_grad_ref, shift_grad_ref, bias_ref):
    total = jnp.zeros((16, 128), f32)
    for z in range(NZ):
        upper, lower = got_ref[z, 64:80].astype(f32), got_ref[z, 80:96].astype(f32)
        total = total + (upper[:, :128] + upper[:, 128:] + lower[:, :128])
    sums = [jnp.concatenate([total[5 * s + t : 5 * s + t + 1] for t in range(5)], axis=1) for s in range(3)]
    shift_grad_ref[...], gain_grad_ref[...], bias_ref[...] = sums
    groups = group_matrix()
    gain, mean, rstd = gain_ref[...], row_ref[0:1], row_ref[1:2]

    def moment(value):
        return exact_dot(exact_dot(rows8(gain * value), groups, 0), groups, 1)[:1] / TOTAL

    first, second = moment(sums[0]), moment(sums[1])
    xhat = (feat_ref[...].astype(f32) - mean) * rstd
    grad_ref[...] = (rstd * (da_ref[...] * gain - first - xhat * second)).astype(bf16)
    weight = got_ref[0, :W_ROWS].astype(f32)
    for z in range(1, NZ):
        weight = weight + got_ref[z, :W_ROWS].astype(f32)
    for i in range(3):
        for j in range(3):
            lanes = slice(j * NQ, (j + 1) * NQ)
            weight_ref[i, j, 0:16] = weight[16 * i : 16 * i + 16, lanes]
            weight_ref[i, j, 16:20] = weight[48 + 4 * i : 52 + 4 * i, lanes]


def flip(value):
    return lax.ppermute(value, "core", [(0, 1), (1, 0)])


def shape(dims, dtype):
    return jax.ShapeDtypeStruct(dims, dtype)


def body(features, cotangent, conv_weight, gain, shift):
    core, y = lax.axis_index("core"), lax.axis_index("y")
    at_core, at_y = core.reshape(1), y.reshape(1)
    feat, cot = features.reshape(PIX, C), cotangent.reshape(PIX, C)
    gain, shift = gain.reshape(1, C), shift.reshape(1, C)
    cot2, feat2 = flip(cot), flip(feat)

    edge = jnp.where(
        core == 0,
        jnp.concatenate([cot[PIX - TC :], cot2[PIX - TC :]]),
        jnp.concatenate([cot2[:TC], cot[:TC]]),
    )
    count = NZ * NY
    ways = [(2 * k, 2 * k + 2) for k in range(count - 1)] + [(2 * k + 3, 2 * k + 1) for k in range(count - 1)]
    mine = lax.ppermute(edge, ("z", "y", "core"), ways)
    theirs = flip(mine)

    packed, bias = pl.pallas_call(
        pack_kernel,
        out_shape=(shape((PEERS, G_ROWS, 128), bf16), shape((8, C), f32)),
        in_specs=[smem()] + [vmem()] * 7,
        out_specs=(vmem(), vmem()),
        compiler_params=params(),
        name="pack",
    )(
        at_core, feat, cot, feat2, cot2, jnp.asarray(feature_columns()),
        jnp.asarray(cotangent_columns(0)), jnp.asarray(cotangent_columns(1)),
    )
    slab = lax.all_to_all(packed, ("y", "x"), 0, 0)

    top = jnp.where(core == 0, mine[0], theirs[2 * TC - 1])
    bottom = jnp.where(core == 0, theirs[0], mine[2 * TC - 1])
    column = jnp.where(core == 0, cotangent[:, 0], cotangent[:, TC - 1])
    column = jnp.concatenate([top[None], column, bottom[None]])
    pairs = [(2 * k + 1, 2 * k + 2) for k in range(NX - 1)]
    outer = lax.ppermute(column, ("x", "core"), pairs + [(b, a) for a, b in pairs])
    back = pl.pallas_call(
        back_kernel,
        grid=(9,),
        out_shape=shape((PIX, C), f32),
        in_specs=[smem()] + [vmem()] * 5 + [pl.BlockSpec((1, 1, C, C), lambda t: (t // 3, t % 3, 0, 0))],
        out_specs=vmem(),
        scratch_shapes=[pltpu.VMEM((3, (TR + 2) * TC, C), bf16), pltpu.VMEM((PIX, C), f32)],
        compiler_params=params(),
        cost_estimate=pl.CostEstimate(flops=2 * PIX * 9 * C * C, bytes_accessed=18 * C * C, transcendentals=0),
        name="back",
    )(at_core, cot, cot2, mine, theirs, outer, conv_weight)

    stats = pl.pallas_call(
        stats_kernel,
        grid=(1,),
        out_shape=shape((NZ, 8, 128), f32),
        in_specs=[pl.BlockSpec((PEERS, S_ROWS, 128), lambda t: (0, (F_ROWS + C_ROWS) // S_ROWS, 0))],
        out_specs=vmem(),
        compiler_params=params(),
        name="stats",
    )(slab)
    stats = lax.all_to_all(stats, "z", 0, 0)
    slab_feat, first_row, last_row = pl.pallas_call(
        split_kernel,
        out_shape=(shape((PEERS, F_ROWS, 128), bf16), shape((128, 128), bf16), shape((128, 128), bf16)),
        in_specs=[vmem()],
        out_specs=(vmem(), vmem(), vmem()),
        compiler_params=params(),
        name="split",
    )(slab)
    slab_other = flip(slab_feat)
    slabs = [(k, k + 1) for k in range(NZ - 1)]
    above = lax.ppermute(last_row, "z", slabs)
    below = lax.ppermute(first_row, "z", [(b, a) for a, b in slabs])

    row, da, table, sums = pl.pallas_call(
        sums_kernel,
        out_shape=(shape((8, C), f32), shape((PIX, C), f32), shape((8, 256), f32), shape((2 * PEERS, 16, 128), f32)),
        in_specs=[smem()] + [vmem()] * 7,
        out_specs=(vmem(), vmem(), vmem(), vmem()),
        scratch_shapes=[pltpu.VMEM((16, 128), f32)],
        compiler_params=params(),
        name="sums",
    )(at_y, stats, feat, back, gain, shift, bias, jnp.asarray(term_columns()))
    sums = lax.all_to_all(sums, ("y", "x", "core"), 0, 0)

    terms = pl.pallas_call(
        terms_kernel,
        out_shape=shape((NZ, W_ROWS, 256), bf16),
        in_specs=[smem()] + [vmem()] * 5,
        out_specs=vmem(),
        scratch_shapes=[
            pltpu.VMEM((ROWS * 128, 256), bf16),
            pltpu.VMEM(((ROWS + 2) * 128, 128), bf16),
            pltpu.VMEM((256, (ROWS + 2) * 128), bf16),
            pltpu.VMEM((NZ, 16, 256), f32),
        ],
        compiler_params=params(),
        cost_estimate=pl.CostEstimate(
            flops=2 * PIX * 9 * C * C, bytes_accessed=4 << 20, transcendentals=ROWS * 128 * 256
        ),
        name="terms",
    )(at_core, slab, slab_other, above, below, table)

    joined = pl.pallas_call(
        join_kernel,
        out_shape=shape((NZ, W_ROWS + V_ROWS, 256), bf16),
        in_specs=[vmem()] * 2,
        out_specs=vmem(),
        compiler_params=params(),
        name="join",
    )(sums, terms)
    joined = lax.all_to_all(joined, "z", 0, 0)
    grad, weight_grad, gain_grad, shift_grad, bias_grad = pl.pallas_call(
        final_kernel,
        out_shape=(
            shape((PIX, C), bf16),
            shape((3, 3, 20, NQ), f32),
            shape((1, C), f32),
            shape((1, C), f32),
            shape((1, C), f32),
        ),
        in_specs=[vmem()] * 5,
        out_specs=(vmem(),) * 5,
        compiler_params=params(),
        name="final",
    )(joined, feat, da, row, gain)
    return (
        grad.reshape(features.shape),
        weight_grad,
        gain_grad.reshape(C),
        shift_grad.reshape(C),
        bias_grad.reshape(C),
    )


def solution(mesh):
    grid = Mesh(mesh.devices.reshape(NZ, NY, NX, 2), ("z", "y", "x", "core"))
    rows, cols = ("z", "y"), ("x", "core")
    tiled = P(rows, cols, None)
    return jax.shard_map(
        body,
        mesh=grid,
        in_specs=(tiled, tiled, P(), P(), P()),
        out_specs=(tiled, P(None, None, rows, cols), P(), P(), P()),
        check_vma=False,
    )
```

```python
import jax
import jax.numpy as jnp
from jax import lax
from jax.experimental import pallas as pl
from jax.experimental.pallas import tpu as pltpu
from jax.sharding import Mesh
from jax.sharding import PartitionSpec as P

C = 640
GW = 40
TR, TC = 8, 16
PIX = TR * TC
NZ, NY, NX = 8, 4, 4
PEERS = NY * NX
ROWS = NY * TR
NQ = 80
CHIP = float(2 * PIX * GW)
TOTAL = float(NZ * PEERS) * CHIP
VMEM_LIMIT = 48 * 1024 * 1024
F_ROWS, C_ROWS, S_ROWS = 160, 160, 16
G_ROWS = F_ROWS + C_ROWS + S_ROWS
W_ROWS = 64
f32, bf16 = jnp.float32, jnp.bfloat16


def lanes(count):
    return lax.broadcasted_iota(jnp.int32, (1, count), 1)


def slab_channel(main, at):
    z = jnp.where(main, at >> 4, at >> 2)
    return z * 80 + jnp.where(main, at & 15, 16 + (at & 3))


def feature_columns():
    lane = lanes(C)
    main = lane < 512
    y = jnp.where(main, lane >> 7, (lane - 512) >> 5)
    return slab_channel(main, jnp.where(main, lane & 127, lane & 31)) + y * 20


def cotangent_columns(core, side):
    lane = lanes(C)
    main = lane < 512
    x = jnp.where(main, lane >> 7, (lane - 512) >> 5)
    at = jnp.where(main, lane & 127, lane & 31)
    q = jnp.where(main, at & 63, 64 + (at & 15))
    mine = jnp.where(main, at >> 6, at >> 4) == side
    return jnp.where(mine, x * 160 + core * NQ + q, -1)


def term_columns(y):
    lane = lanes(256)
    main = lane < 128
    return slab_channel(main, jnp.where(main, lane, lane & 31)) + y * 20


def vmem():
    return pl.BlockSpec(memory_space=pltpu.VMEM)


def smem():
    return pl.BlockSpec(memory_space=pltpu.SMEM)


def params(**kw):
    return pltpu.CompilerParams(vmem_limit_bytes=VMEM_LIMIT, **kw)


def whole(*dims):
    return pl.BlockSpec(dims, lambda t: (0,) * len(dims))


def group_matrix():
    chan = lax.broadcasted_iota(jnp.int32, (C, 128), 0)
    low = lax.broadcasted_iota(jnp.int32, (C, 128), 1) * GW
    return jnp.where((chan >= low) & (chan < low + GW), 1.0, 0.0).astype(bf16)


def exact_dot(value, matrix, over):
    high, middle, low = three(value)
    stacked = jnp.concatenate([high, middle, low, jnp.zeros_like(low)], axis=0).astype(bf16)
    out = lax.dot_general(stacked, matrix, (((1,), (over,)), ((), ())), preferred_element_type=f32)
    return out[0:8] + out[8:16] + out[16:24]


def rows8(row):
    return jnp.broadcast_to(row, (8, row.shape[1]))


def pick(columns):
    rows = lax.broadcasted_iota(jnp.int32, (C, columns.shape[1]), 0)
    return (rows == columns).astype(f32).astype(bf16)


def three(value):
    high = value.astype(bf16).astype(f32)
    rest = value - high
    middle = rest.astype(bf16).astype(f32)
    return high, middle, rest - middle


def lanes32(value):
    group = lax.broadcasted_iota(jnp.int32, (32, 128), 1) // 32
    out = []
    for a in range(4):
        acc = jnp.zeros((32, 128), f32)
        for g in range(4):
            moved = pltpu.roll(value[32 * g : 32 * g + 32], (32 * (g - a)) % 128, 1)
            acc = jnp.where(group == g, moved, acc)
        out.append(acc)
    return out


def pack_kernel(core_ref, feat_ref, cot_ref, feat2_ref, cot2_ref, out_ref, bias_ref):
    core = core_ref[0]
    feat, cot = feat_ref[...], cot_ref[...]
    x, x2 = feat.astype(f32), feat2_ref[...].astype(f32)
    groups = group_matrix()
    total = x.sum(0, keepdims=True) + x2.sum(0, keepdims=True)
    mean = exact_dot(rows8(total), groups, 0) / CHIP
    wide = exact_dot(mean, groups, 1)[:1]
    squares = ((x - wide) ** 2).sum(0, keepdims=True) + ((x2 - wide) ** 2).sum(0, keepdims=True)
    squares = exact_dot(rows8(squares), groups, 0)
    pieces = three(mean[:1]) + three(squares[:1])
    row = lax.broadcasted_iota(jnp.int32, (S_ROWS, 128), 0)
    stats = jnp.zeros((S_ROWS, 128), f32)
    for k in range(6):
        stats = jnp.where(row == k, pieces[k], stats)
    stats = stats.astype(bf16)
    bias_ref[...] = rows8(cot.astype(f32).sum(0, keepdims=True))

    moved = jnp.dot(feat, pick(feature_columns()), preferred_element_type=f32)
    terms = jnp.dot(cot, pick(cotangent_columns(core, core)), preferred_element_type=f32)
    terms = terms + jnp.dot(cot2_ref[...], pick(cotangent_columns(core, 1 - core)), preferred_element_type=f32)
    moved_rest = lanes32(moved[:, 512:])
    terms_rest = lanes32(terms[:, 512:])
    for y in range(NY):
        for xx in range(NX):
            p = y * NX + xx
            out_ref[p, 0:128] = moved[:, y * 128 : (y + 1) * 128].astype(bf16)
            out_ref[p, 128:160] = moved_rest[y].astype(bf16)
            out_ref[p, 160:288] = terms[:, xx * 128 : (xx + 1) * 128].astype(bf16)
            out_ref[p, 288:320] = terms_rest[xx].astype(bf16)
            out_ref[p, 320:336] = stats


def merge(means, squares, count):
    n = means.shape[0]
    mean = means.sum(0, keepdims=True) / n
    return mean, squares.sum(0, keepdims=True) + count * ((means - mean) ** 2).sum(0, keepdims=True)


def stats_kernel(slab_ref, out_ref):
    got = slab_ref[...].astype(f32)
    mean, squares = merge(
        got[:, 0] + got[:, 1] + got[:, 2], got[:, 3] + got[:, 4] + got[:, 5], CHIP
    )
    row = lax.broadcasted_iota(jnp.int32, (8, 128), 0)
    block = jnp.where(row == 0, mean, jnp.where(row == 1, squares, 0.0))
    for z in range(NZ):
        out_ref[z] = block


def cot_rows(main, rest, g, side):
    lane = lax.broadcasted_iota(jnp.int32, main.shape, 1)
    main = pltpu.roll(main, 64, 1) if side else main
    return jnp.where(lane < 64, main, pltpu.roll(rest, (64 - 32 * g - 16 * side) % 128, 1))


def split_kernel(core_ref, slab_ref, feat_ref, keep_ref, give_ref):
    lower = core_ref[0] == 0
    feat_ref[...] = slab_ref[:, :F_ROWS]
    for xx in range(NX):
        for side in range(2):
            at = slice(xx * 32 + side * TC, xx * 32 + (side + 1) * TC)
            peer = (NY - 1) * NX + xx
            first = cot_rows(slab_ref[xx, 160:176].astype(f32), slab_ref[xx, 288:304].astype(f32), 0, side)
            last = cot_rows(slab_ref[peer, 272:288].astype(f32), slab_ref[peer, 304:320].astype(f32), 3, side)
            keep_ref[at] = jnp.where(lower, last, first).astype(bf16)
            give_ref[at] = jnp.where(lower, first, last).astype(bf16)


def back_kernel(core_ref, cot_ref, cot2_ref, mine_ref, theirs_ref, outer_ref, w_hbm, out_ref, shifted, w_ref, sem):
    copies = [pltpu.make_async_copy(w_hbm.at[t // 3, t % 3], w_ref.at[t], sem.at[t]) for t in range(9)]
    for copy in copies:
        copy.start()
    rows = (TR + 2) * TC
    lower = core_ref[0] == 0
    mine, theirs = mine_ref[...].astype(f32), theirs_ref[...].astype(f32)
    top, bottom = jnp.where(lower, mine, theirs), jnp.where(lower, theirs, mine)
    own_top, other_top = jnp.where(lower, top[:TC], top[TC:]), jnp.where(lower, top[TC:], top[:TC])
    own_bot, other_bot = jnp.where(lower, bottom[:TC], bottom[TC:]), jnp.where(lower, bottom[TC:], bottom[:TC])
    wide = jnp.concatenate([own_top, cot_ref[...].astype(f32), own_bot], axis=0)
    near = jnp.concatenate([other_top, cot2_ref[...].astype(f32), other_bot], axis=0)
    near = near.reshape(TR + 2, TC, C)
    inner = jnp.where(lower, near[:, :1], near[:, TC - 1 :])
    outer = outer_ref[...].astype(f32)[:, None, :]
    left, right = jnp.where(lower, outer, inner), jnp.where(lower, inner, outer)
    left = jnp.broadcast_to(left, (TR + 2, TC, C)).reshape(rows, C)
    right = jnp.broadcast_to(right, (TR + 2, TC, C)).reshape(rows, C)
    col = lax.broadcasted_iota(jnp.int32, (rows, C), 0) % TC
    shifted[0] = jnp.where(col == 0, left, pltpu.roll(wide, 1, 0)).astype(bf16)
    shifted[1] = wide.astype(bf16)
    shifted[2] = jnp.where(col == TC - 1, right, pltpu.roll(wide, rows - 1, 0)).astype(bf16)
    total = jnp.zeros((C, PIX), f32)
    for t in range(9):
        i, j = t // 3, t % 3
        copies[t].wait()
        pixels = shifted[2 - j, (2 - i) * TC : (2 - i) * TC + PIX]
        total = total + lax.dot_general(
            w_ref[t], pixels, (((1,), (1,)), ((), ())), preferred_element_type=f32
        )
    out_ref[...] = total.T


def sums_kernel(y_ref, stat_ref, feat_ref, back_ref, gain_ref, shift_ref, bias_ref,
                row_ref, da_ref, par_ref, out_ref, block):
    got = stat_ref[...]
    mean, squares = merge(got[:, 0], got[:, 1], PEERS * CHIP)
    groups = group_matrix()
    both = jnp.concatenate([mean, lax.rsqrt(squares / TOTAL + 1e-05), jnp.zeros((6, 128), f32)], axis=0)
    both = exact_dot(both, groups, 1)
    mean, rstd = both[0:1], both[1:2]
    gain, shift = gain_ref[...], shift_ref[...]
    row = lax.broadcasted_iota(jnp.int32, (8, C), 0)
    row_ref[...] = jnp.where(row == 0, mean, rstd)
    table = jnp.where(row == 0, mean, jnp.where(row == 1, rstd * gain, jnp.where(row == 2, shift, 0.0)))
    par_ref[...] = exact_dot(table, pick(term_columns(y_ref[0])), 0)
    xhat = (feat_ref[...].astype(f32) - mean) * rstd
    act = xhat * gain + shift
    sig = jax.nn.sigmoid(act)
    da = back_ref[...] * sig * (1.0 + act * (1.0 - sig))
    da_ref[...] = da
    sums = (da.sum(0, keepdims=True), (da * xhat).sum(0, keepdims=True), bias_ref[:1])
    block[...] = jnp.zeros_like(block)
    for s in range(3):
        for t in range(5):
            block[5 * s + t : 5 * s + t + 1] = sums[s][:, 128 * t : 128 * t + 128]
    value = block[...]
    for p in range(2 * PEERS):
        out_ref[p] = value


def terms_kernel(core_ref, own_ref, other_ref, edge_ref, swap_ref, par_ref, out_ref, hid, strips, cot3, rest):
    core = core_ref[0]

    def put(block, peer, side):
        y, xx = peer // NX, peer % NX

        def silu(x, lanes):
            a = (x.astype(f32) - par_ref[0:1, lanes]) * par_ref[1:2, lanes] + par_ref[2:3, lanes]
            return a * jax.nn.sigmoid(a)

        main = silu(block[:128], slice(0, 128)).astype(bf16)
        tail = silu(block[128:], slice(128, 256))
        for g in range(4):
            low = pltpu.roll(tail, (128 - 32 * g) % 128, 1).astype(bf16)
            for h in range(2):
                r = 2 * g + h
                at = pl.ds(pl.multiple_of((y * TR + r) * 128 + xx * 32 + side * TC, TC), TC)
                hid[at, 0:128] = main[r * TC : (r + 1) * TC]
                hid[at, 128:256] = low[h * TC : (h + 1) * TC]

    for peer in range(PEERS):
        put(own_ref[peer, :F_ROWS], peer, core)
        put(other_ref[peer], peer, 1 - core)
        y, xx = peer // NX, peer % NX
        tail = own_ref[peer, 288:320].astype(f32)
        for g in range(4):
            main = own_ref[peer, 160 + 32 * g : 192 + 32 * g].astype(f32)
            for side in range(2):
                value = cot_rows(main, tail, g, side).astype(bf16)
                for h in range(2):
                    at = (y * TR + 2 * g + h + 1) * 128 + xx * 32 + side * TC
                    strips[at : at + TC] = value[h * TC : (h + 1) * TC]
    edge, swap = edge_ref[...].astype(f32), swap_ref[...].astype(f32)
    strips[0:128] = jnp.where(core == 0, edge, swap).astype(bf16)
    strips[(ROWS + 1) * 128 :] = jnp.where(core == 0, swap, edge).astype(bf16)
    lane = lax.broadcasted_iota(jnp.int32, (NQ, 128), 1)
    for row in range(ROWS + 2):
        at = slice(row * 128, (row + 1) * 128)
        turned = strips[at].astype(f32).T[:NQ]
        before = jnp.where(lane == 0, 0.0, pltpu.roll(turned, 1, 1))
        after = jnp.where(lane == 127, 0.0, pltpu.roll(turned, 127, 1))
        cot3[0:NQ, at] = after.astype(bf16)
        cot3[NQ : 2 * NQ, at] = turned.astype(bf16)
        cot3[2 * NQ : 3 * NQ, at] = before.astype(bf16)
    cot3[3 * NQ :] = jnp.zeros((16, (ROWS + 2) * 128), bf16)
    rest[...] = jnp.zeros_like(rest)
    for i in range(3):
        lhs = cot3[:, (2 - i) * 128 : (2 - i) * 128 + ROWS * 128]
        turned = jnp.dot(lhs, hid[...], preferred_element_type=f32).T
        for z in range(NZ):
            out_ref[z, 16 * i : 16 * i + 16] = turned[16 * z : 16 * z + 16].astype(bf16)
            rest[z, 4 * i : 4 * i + 4] = turned[128 + 4 * z : 132 + 4 * z]
    for z in range(NZ):
        out_ref[z, 48:64] = rest[z].astype(bf16)


def join_kernel(sums_ref, out_ref):
    value = sums_ref[0]
    for p in range(1, 2 * PEERS):
        value = value + sums_ref[p]
    for z in range(NZ):
        out_ref[z] = value


def final_kernel(sums_ref, got_ref, feat_ref, da_ref, row_ref, gain_ref,
                 grad_ref, weight_ref, gain_grad_ref, shift_grad_ref, bias_ref):
    total = sums_ref[0]
    for z in range(1, NZ):
        total = total + sums_ref[z]
    sums = [jnp.concatenate([total[5 * s + t : 5 * s + t + 1] for t in range(5)], axis=1) for s in range(3)]
    shift_grad_ref[...], gain_grad_ref[...], bias_ref[...] = [value.reshape(C) for value in sums]
    groups = group_matrix()
    gain, mean, rstd = gain_ref[...], row_ref[0:1], row_ref[1:2]

    both = jnp.concatenate([gain * sums[0], gain * sums[1], jnp.zeros((6, C), f32)], axis=0)
    both = exact_dot(exact_dot(both, groups, 0), groups, 1) / TOTAL
    first, second = both[0:1], both[1:2]
    xhat = (feat_ref[...].astype(f32) - mean) * rstd
    grad_ref[...] = (rstd * (da_ref[...] * gain - first - xhat * second)).astype(bf16)
    weight = got_ref[0].astype(f32)
    for z in range(1, NZ):
        weight = weight + got_ref[z].astype(f32)
    for i in range(3):
        for j in range(3):
            at = slice(j * NQ, (j + 1) * NQ)
            weight_ref[i, j, 0:16] = weight[16 * i : 16 * i + 16, at]
            weight_ref[i, j, 16:20] = weight[48 + 4 * i : 52 + 4 * i, at]


def flip(value):
    return lax.ppermute(value, "core", [(0, 1), (1, 0)])


def shape(dims, dtype):
    return jax.ShapeDtypeStruct(dims, dtype)


def body(features, cotangent, conv_weight, gain, shift):
    core, y = lax.axis_index("core"), lax.axis_index("y")
    at_core, at_y = core.reshape(1), y.reshape(1)
    feat, cot = features.reshape(PIX, C), cotangent.reshape(PIX, C)
    gain, shift = gain.reshape(1, C), shift.reshape(1, C)
    cot2, feat2 = flip(cot), flip(feat)

    edge = jnp.where(
        core == 0,
        jnp.concatenate([cot[PIX - TC :], cot2[PIX - TC :]]),
        jnp.concatenate([cot2[:TC], cot[:TC]]),
    )
    count = NZ * NY
    ways = [(2 * k, 2 * k + 2) for k in range(count - 1)] + [(2 * k + 3, 2 * k + 1) for k in range(count - 1)]
    mine = lax.ppermute(edge, ("z", "y", "core"), ways)
    theirs = flip(mine)

    packed, bias = pl.pallas_call(
        pack_kernel,
        grid=(1,),
        out_shape=(shape((PEERS, G_ROWS, 128), bf16), shape((8, C), f32)),
        in_specs=[smem()] + [whole(PIX, C)] * 4,
        out_specs=(vmem(), vmem()),
        compiler_params=params(),
        name="pack",
    )(at_core, feat, cot, feat2, cot2)
    packed, mine = lax.optimization_barrier((packed, mine))
    slab = lax.all_to_all(packed, ("y", "x"), 0, 0)

    top = jnp.where(core == 0, mine[0], theirs[2 * TC - 1])
    bottom = jnp.where(core == 0, theirs[0], mine[2 * TC - 1])
    column = jnp.where(core == 0, cotangent[:, 0], cotangent[:, TC - 1])
    column = jnp.concatenate([top[None], column, bottom[None]])
    pairs = [(2 * k + 1, 2 * k + 2) for k in range(NX - 1)]
    outer = lax.ppermute(column, ("x", "core"), pairs + [(b, a) for a, b in pairs])
    back = pl.pallas_call(
        back_kernel,
        out_shape=shape((PIX, C), f32),
        in_specs=[smem()] + [vmem()] * 5 + [pl.BlockSpec(memory_space=pl.ANY)],
        out_specs=vmem(),
        scratch_shapes=[
            pltpu.VMEM((3, (TR + 2) * TC, C), bf16),
            pltpu.VMEM((9, C, C), bf16),
            pltpu.SemaphoreType.DMA((9,)),
        ],
        compiler_params=params(),
        cost_estimate=pl.CostEstimate(flops=2 * PIX * 9 * C * C, bytes_accessed=18 * C * C, transcendentals=0),
        name="back",
    )(at_core, cot, cot2, mine, theirs, outer, conv_weight)
    slab, back = lax.optimization_barrier((slab, back))

    stats = pl.pallas_call(
        stats_kernel,
        grid=(1,),
        out_shape=shape((NZ, 8, 128), f32),
        in_specs=[pl.BlockSpec((PEERS, S_ROWS, 128), lambda t: (0, (F_ROWS + C_ROWS) // S_ROWS, 0))],
        out_specs=vmem(),
        compiler_params=params(),
        name="stats",
    )(slab)
    stats = lax.all_to_all(stats, "z", 0, 0)
    slab_feat, keep, give = pl.pallas_call(
        split_kernel,
        out_shape=(shape((PEERS, F_ROWS, 128), bf16), shape((128, 128), bf16), shape((128, 128), bf16)),
        in_specs=[smem(), vmem()],
        out_specs=(vmem(), vmem(), vmem()),
        compiler_params=params(),
        name="split",
    )(at_core, slab)
    slab_other = flip(slab_feat)
    ways = [(2 * k, 2 * k + 2) for k in range(NZ - 1)] + [(2 * k + 3, 2 * k + 1) for k in range(NZ - 1)]
    strip = lax.ppermute(jnp.stack([keep, flip(give)]), ("z", "core"), ways)
    edge, swap = strip[0], flip(strip[1])

    row, da, table, sums = pl.pallas_call(
        sums_kernel,
        out_shape=(shape((8, C), f32), shape((PIX, C), f32), shape((8, 256), f32), shape((2 * PEERS, 16, 128), f32)),
        in_specs=[smem()] + [vmem()] * 6,
        out_specs=(vmem(), vmem(), vmem(), vmem()),
        scratch_shapes=[pltpu.VMEM((16, 128), f32)],
        compiler_params=params(),
        name="sums",
    )(at_y, stats, feat, back, gain, shift, bias)
    sums = lax.all_to_all(sums, ("y", "x", "core"), 0, 0)

    terms = pl.pallas_call(
        terms_kernel,
        out_shape=shape((NZ, W_ROWS, 256), bf16),
        in_specs=[smem()] + [vmem()] * 5,
        out_specs=vmem(),
        scratch_shapes=[
            pltpu.VMEM((ROWS * 128, 256), bf16),
            pltpu.VMEM(((ROWS + 2) * 128, 128), bf16),
            pltpu.VMEM((256, (ROWS + 2) * 128), bf16),
            pltpu.VMEM((NZ, 16, 256), f32),
        ],
        compiler_params=params(),
        cost_estimate=pl.CostEstimate(
            flops=2 * PIX * 9 * C * C, bytes_accessed=4 << 20, transcendentals=ROWS * 128 * 256
        ),
        name="terms",
    )(at_core, slab, slab_other, edge, swap, table)

    terms = lax.all_to_all(terms, "z", 0, 0)
    sums = pl.pallas_call(
        join_kernel,
        out_shape=shape((NZ, 16, 128), f32),
        in_specs=[vmem()],
        out_specs=vmem(),
        compiler_params=params(),
        name="join",
    )(sums)
    sums = lax.all_to_all(sums, "z", 0, 0)
    grad, weight_grad, gain_grad, shift_grad, bias_grad = pl.pallas_call(
        final_kernel,
        out_shape=(shape((PIX, C), bf16), shape((3, 3, 20, NQ), f32)) + (shape((C,), f32),) * 3,
        in_specs=[vmem()] * 6,
        out_specs=(vmem(),) * 5,
        compiler_params=params(),
        name="final",
    )(sums, terms, feat, da, row, gain)
    return grad.reshape(features.shape), weight_grad, gain_grad, shift_grad, bias_grad


def solution(mesh):
    grid = Mesh(mesh.devices.reshape(NZ, NY, NX, 2), ("z", "y", "x", "core"))
    rows, cols = ("z", "y"), ("x", "core")
    tiled = P(rows, cols, None)
    return jax.shard_map(
        body,
        mesh=grid,
        in_specs=(tiled, tiled, P(), P(), P()),
        out_specs=(tiled, P(None, None, rows, cols), P(), P(), P()),
        check_vma=False,
    )
```

```python
import jax
import jax.numpy as jnp
from jax import lax
from jax.experimental import pallas as pl
from jax.experimental.pallas import tpu as pltpu
from jax.sharding import Mesh
from jax.sharding import PartitionSpec as P

C = 640
GW = 40
TR, TC = 8, 16
PIX = TR * TC
NZ, NY, NX = 8, 4, 4
PEERS = NY * NX
ROWS = NY * TR
NQ = 80
CHIP = float(2 * PIX * GW)
TOTAL = float(NZ * PEERS) * CHIP
VMEM_LIMIT = 48 * 1024 * 1024
F_ROWS, C_ROWS, H_ROWS, S_ROWS = 160, 160, 32, 16
H_AT = F_ROWS + C_ROWS
S_AT = H_AT + H_ROWS
G_ROWS = S_AT + S_ROWS
W_ROWS, V_ROWS = 64, 16
f32, bf16 = jnp.float32, jnp.bfloat16


def lanes(count):
    return lax.broadcasted_iota(jnp.int32, (1, count), 1)


def slab_channel(main, at):
    z = jnp.where(main, at >> 4, at >> 2)
    return z * 80 + jnp.where(main, at & 15, 16 + (at & 3))


def feature_columns():
    lane = lanes(C)
    main = lane < 512
    y = jnp.where(main, lane >> 7, (lane - 512) >> 5)
    return slab_channel(main, jnp.where(main, lane & 127, lane & 31)) + y * 20


def cotangent_columns(core, side):
    lane = lanes(C)
    main = lane < 512
    x = jnp.where(main, lane >> 7, (lane - 512) >> 5)
    at = jnp.where(main, lane & 127, lane & 31)
    q = jnp.where(main, at & 63, 64 + (at & 15))
    mine = jnp.where(main, at >> 6, at >> 4) == side
    return jnp.where(mine, x * 160 + core * NQ + q, -1)


def term_columns(y):
    lane = lanes(256)
    main = lane < 128
    return slab_channel(main, jnp.where(main, lane, lane & 31)) + y * 20


def vmem():
    return pl.BlockSpec(memory_space=pltpu.VMEM)


def smem():
    return pl.BlockSpec(memory_space=pltpu.SMEM)


def params(**kw):
    return pltpu.CompilerParams(vmem_limit_bytes=VMEM_LIMIT, **kw)


def whole(*dims):
    return pl.BlockSpec(dims, lambda t: (0,) * len(dims))


def group_matrix():
    chan = lax.broadcasted_iota(jnp.int32, (C, 128), 0)
    low = lax.broadcasted_iota(jnp.int32, (C, 128), 1) * GW
    return jnp.where((chan >= low) & (chan < low + GW), 1.0, 0.0).astype(bf16)


def exact_dot(value, matrix, over):
    high, middle, low = three(value)
    stacked = jnp.concatenate([high, middle, low, jnp.zeros_like(low)], axis=0).astype(bf16)
    out = lax.dot_general(stacked, matrix, (((1,), (over,)), ((), ())), preferred_element_type=f32)
    return out[0:8] + out[8:16] + out[16:24]


def rows8(row):
    return jnp.broadcast_to(row, (8, row.shape[1]))


def pick(columns):
    rows = lax.broadcasted_iota(jnp.int32, (C, columns.shape[1]), 0)
    return (rows == columns).astype(f32).astype(bf16)


def three(value):
    high = value.astype(bf16).astype(f32)
    rest = value - high
    middle = rest.astype(bf16).astype(f32)
    return high, middle, rest - middle


def lanes32(value, height):
    group = lax.broadcasted_iota(jnp.int32, (height, 128), 1) // 32
    out = []
    for a in range(4):
        acc = jnp.zeros((height, 128), f32)
        for g in range(4):
            moved = pltpu.roll(value[height * g : height * (g + 1)], (32 * (g - a)) % 128, 1)
            acc = jnp.where(group == g, moved, acc)
        out.append(acc)
    return out


def stats_kernel(feat_hbm, cot_hbm, feat2_ref, out_ref, bias_ref, feat_ref, cot_ref, sem):
    copies = [
        pltpu.make_async_copy(feat_hbm, feat_ref, sem.at[0]),
        pltpu.make_async_copy(cot_hbm, cot_ref, sem.at[1]),
    ]
    for copy in copies:
        copy.start()
    groups = group_matrix()
    for copy in copies:
        copy.wait()
    x, x2 = feat_ref[...].astype(f32), feat2_ref[...].astype(f32)
    total = x.sum(0, keepdims=True) + x2.sum(0, keepdims=True)
    mean = exact_dot(rows8(total), groups, 0) / CHIP
    wide = exact_dot(mean, groups, 1)[:1]
    squares = ((x - wide) ** 2).sum(0, keepdims=True) + ((x2 - wide) ** 2).sum(0, keepdims=True)
    squares = exact_dot(rows8(squares), groups, 0)
    row = lax.broadcasted_iota(jnp.int32, (8, 128), 0)
    block = jnp.where(row == 0, mean, jnp.where(row == 1, squares, 0.0))
    for z in range(NZ):
        out_ref[z] = block
    bias_ref[...] = rows8(cot_ref[...].astype(f32).sum(0, keepdims=True))


def pack_kernel(core_ref, feat_ref, cot_ref, cot2_ref, mine_ref, theirs_ref, out_ref, rest_ref):
    core = core_ref[0]
    lower = core == 0

    def pair(own, other):
        a, b = own[...].astype(f32), other[...].astype(f32)
        return jnp.where(lower, a, b).astype(bf16), jnp.where(lower, b, a).astype(bf16)

    first, second = pair(cot_ref, cot2_ref)
    top, bottom = pair(mine_ref, theirs_ref)
    moved = jnp.dot(feat_ref[...], pick(feature_columns()), preferred_element_type=f32)
    terms = jnp.dot(
        jnp.concatenate([first, top], axis=0), pick(cotangent_columns(core, 0)), preferred_element_type=f32
    ) + jnp.dot(
        jnp.concatenate([second, bottom], axis=0), pick(cotangent_columns(core, 1)), preferred_element_type=f32
    )
    moved_rest = lanes32(moved[:, 512:], 32)
    terms_rest = lanes32(terms[:PIX, 512:], 32)
    halo_rest = lanes32(terms[PIX:, 512:], 8)
    for xx in range(NX):
        rest_ref[xx] = halo_rest[xx]
    for y in range(NY):
        for xx in range(NX):
            p = y * NX + xx
            out_ref[p, 0:128] = moved[:, y * 128 : (y + 1) * 128].astype(bf16)
            out_ref[p, 128:160] = moved_rest[y].astype(bf16)
            out_ref[p, 160:288] = terms[:PIX, xx * 128 : (xx + 1) * 128].astype(bf16)
            out_ref[p, 288:320] = terms_rest[xx].astype(bf16)
            out_ref[p, H_AT:S_AT] = terms[PIX:, xx * 128 : (xx + 1) * 128].astype(bf16)


def merge(means, squares, count):
    n = means.shape[0]
    mean = means.sum(0, keepdims=True) / n
    return mean, squares.sum(0, keepdims=True) + count * ((means - mean) ** 2).sum(0, keepdims=True)


def patch_kernel(stat_ref, rest_ref, packed_ref, out_ref, block, sem):
    got = stat_ref[...]
    mean, squares = merge(got[:, 0], got[:, 1], CHIP)
    pieces = three(mean) + three(squares)
    row = lax.broadcasted_iota(jnp.int32, (8, 128), 0)
    stats = jnp.zeros((8, 128), f32)
    for k in range(6):
        stats = jnp.where(row == k, pieces[k], stats)
    for p in range(PEERS):
        block[p] = jnp.concatenate([stats, rest_ref[p % NX]], axis=0).astype(bf16)
    copy = pltpu.make_async_copy(block, out_ref.at[:, S_AT:, :], sem)
    copy.start()
    copy.wait()


def cot_rows(main, rest, g, side):
    lane = lax.broadcasted_iota(jnp.int32, main.shape, 1)
    main = pltpu.roll(main, 64, 1) if side else main
    return jnp.where(lane < 64, main, pltpu.roll(rest, (64 - 32 * g - 16 * side) % 128, 1))


def back_kernel(core_ref, cot_ref, cot2_ref, mine_ref, theirs_ref, outer_ref, w_hbm, out_ref, shifted, w_ref, sem):
    copies = [pltpu.make_async_copy(w_hbm.at[t // 3, t % 3], w_ref.at[t], sem.at[t]) for t in range(9)]
    for copy in copies:
        copy.start()
    rows = (TR + 2) * TC
    lower = core_ref[0] == 0
    mine, theirs = mine_ref[...].astype(f32), theirs_ref[...].astype(f32)
    top, bottom = jnp.where(lower, mine, theirs), jnp.where(lower, theirs, mine)
    own_top, other_top = jnp.where(lower, top[:TC], top[TC:]), jnp.where(lower, top[TC:], top[:TC])
    own_bot, other_bot = jnp.where(lower, bottom[:TC], bottom[TC:]), jnp.where(lower, bottom[TC:], bottom[:TC])
    wide = jnp.concatenate([own_top, cot_ref[...].astype(f32), own_bot], axis=0)
    near = jnp.concatenate([other_top, cot2_ref[...].astype(f32), other_bot], axis=0)
    near = near.reshape(TR + 2, TC, C)
    inner = jnp.where(lower, near[:, :1], near[:, TC - 1 :])
    outer = outer_ref[...].astype(f32)[:, None, :]
    left, right = jnp.where(lower, outer, inner), jnp.where(lower, inner, outer)
    left = jnp.broadcast_to(left, (TR + 2, TC, C)).reshape(rows, C)
    right = jnp.broadcast_to(right, (TR + 2, TC, C)).reshape(rows, C)
    col = lax.broadcasted_iota(jnp.int32, (rows, C), 0) % TC
    shifted[0] = jnp.where(col == 0, left, pltpu.roll(wide, 1, 0)).astype(bf16)
    shifted[1] = wide.astype(bf16)
    shifted[2] = jnp.where(col == TC - 1, right, pltpu.roll(wide, rows - 1, 0)).astype(bf16)
    total = jnp.zeros((C, PIX), f32)
    for t in range(9):
        i, j = t // 3, t % 3
        copies[t].wait()
        pixels = shifted[2 - j, (2 - i) * TC : (2 - i) * TC + PIX]
        total = total + lax.dot_general(
            w_ref[t], pixels, (((1,), (1,)), ((), ())), preferred_element_type=f32
        )
    out_ref[...] = total.T


def sums_kernel(y_ref, slab_ref, feat_ref, back_ref, gain_ref, shift_ref, bias_ref,
                row_ref, da_ref, par_ref, out_ref, block):
    got = slab_ref[:, S_AT:].astype(f32)
    mean, squares = merge(
        got[:, 0] + got[:, 1] + got[:, 2], got[:, 3] + got[:, 4] + got[:, 5], NZ * CHIP
    )
    groups = group_matrix()
    both = jnp.concatenate([mean, lax.rsqrt(squares / TOTAL + 1e-05), jnp.zeros((6, 128), f32)], axis=0)
    both = exact_dot(both, groups, 1)
    mean, rstd = both[0:1], both[1:2]
    gain, shift = gain_ref[...], shift_ref[...]
    row = lax.broadcasted_iota(jnp.int32, (8, C), 0)
    row_ref[...] = jnp.where(row == 0, mean, rstd)
    table = jnp.where(row == 0, mean, jnp.where(row == 1, rstd * gain, jnp.where(row == 2, shift, 0.0)))
    par_ref[...] = exact_dot(table, pick(term_columns(y_ref[0])), 0)
    xhat = (feat_ref[...].astype(f32) - mean) * rstd
    act = xhat * gain + shift
    sig = jax.nn.sigmoid(act)
    da = back_ref[...] * sig * (1.0 + act * (1.0 - sig))
    da_ref[...] = da
    sums = (da.sum(0, keepdims=True), (da * xhat).sum(0, keepdims=True), bias_ref[:1])
    block[...] = jnp.zeros_like(block)
    for s in range(3):
        for t in range(5):
            block[5 * s + t : 5 * s + t + 1] = sums[s][:, 128 * t : 128 * t + 128]
    for p in range(2 * PEERS):
        out_ref[p] = block[8 * (p % 2) : 8 * (p % 2) + 8]


def terms_kernel(core_ref, own_ref, other_ref, par_ref, out_ref, hid, strips, cot3, rest):
    core = core_ref[0]

    def put(block, peer, side):
        y, xx = peer // NX, peer % NX

        def silu(x, lanes):
            a = (x.astype(f32) - par_ref[0:1, lanes]) * par_ref[1:2, lanes] + par_ref[2:3, lanes]
            return a * jax.nn.sigmoid(a)

        main = silu(block[:128], slice(0, 128)).astype(bf16)
        tail = silu(block[128:], slice(128, 256))
        for g in range(4):
            low = pltpu.roll(tail, (128 - 32 * g) % 128, 1).astype(bf16)
            for h in range(2):
                r = 2 * g + h
                at = pl.ds(pl.multiple_of((y * TR + r) * 128 + xx * 32 + side * TC, TC), TC)
                hid[at, 0:128] = main[r * TC : (r + 1) * TC]
                hid[at, 128:256] = low[h * TC : (h + 1) * TC]

    for peer in range(PEERS):
        put(own_ref[peer, :F_ROWS], peer, core)
        put(other_ref[peer, :F_ROWS], peer, 1 - core)
        y, xx = peer // NX, peer % NX
        tail = own_ref[peer, 288:320].astype(f32)
        for g in range(4):
            main = own_ref[peer, 160 + 32 * g : 192 + 32 * g].astype(f32)
            for side in range(2):
                value = cot_rows(main, tail, g, side).astype(bf16)
                for h in range(2):
                    at = (y * TR + 2 * g + h + 1) * 128 + xx * 32 + side * TC
                    strips[at : at + TC] = value[h * TC : (h + 1) * TC]
    for xx in range(NX):
        for side, peer, start in ((0, xx, 0), (1, (NY - 1) * NX + xx, (ROWS + 1) * 128)):
            tail = own_ref[peer, S_AT:].astype(f32)[8:]
            main = own_ref[peer, H_AT:S_AT].astype(f32)
            value = [cot_rows(main[8 * g : 8 * g + 8], tail, g, side) for g in range(4)]
            at = start + xx * 32
            strips[at : at + 32] = jnp.concatenate(value, axis=0).astype(bf16)
    lane = lax.broadcasted_iota(jnp.int32, (NQ, 128), 1)
    for row in range(ROWS + 2):
        at = slice(row * 128, (row + 1) * 128)
        turned = strips[at].astype(f32).T[:NQ]
        before = jnp.where(lane == 0, 0.0, pltpu.roll(turned, 1, 1))
        after = jnp.where(lane == 127, 0.0, pltpu.roll(turned, 127, 1))
        cot3[0:NQ, at] = after.astype(bf16)
        cot3[NQ : 2 * NQ, at] = turned.astype(bf16)
        cot3[2 * NQ : 3 * NQ, at] = before.astype(bf16)
    cot3[3 * NQ :] = jnp.zeros((16, (ROWS + 2) * 128), bf16)
    rest[...] = jnp.zeros_like(rest)
    for i in range(3):
        lhs = cot3[:, (2 - i) * 128 : (2 - i) * 128 + ROWS * 128]
        turned = jnp.dot(lhs, hid[...], preferred_element_type=f32).T
        for z in range(NZ):
            out_ref[z, 16 * i : 16 * i + 16] = turned[16 * z : 16 * z + 16].astype(bf16)
            rest[z, 4 * i : 4 * i + 4] = turned[128 + 4 * z : 132 + 4 * z]
    for z in range(NZ):
        out_ref[z, 48:64] = rest[z].astype(bf16)


def join_kernel(sums_ref, terms_ref, out_ref):
    value = sums_ref[0]
    for p in range(1, 2 * PEERS):
        value = value + sums_ref[p]
    high, middle, low = three(value)
    block = jnp.concatenate(
        [jnp.concatenate([high, middle], axis=1), jnp.concatenate([low, jnp.zeros_like(low)], axis=1)], axis=0
    ).astype(bf16)
    for z in range(NZ):
        out_ref[z, :W_ROWS] = terms_ref[z]
        out_ref[z, W_ROWS:] = block


def final_kernel(core_ref, got_ref, other_ref, feat_ref, da_ref, row_ref, gain_ref,
                 grad_ref, weight_ref, gain_grad_ref, shift_grad_ref, bias_ref):
    def half(ref):
        total = jnp.zeros((8, 128), f32)
        for z in range(NZ):
            part = ref[z, W_ROWS:].astype(f32)
            total = total + (part[:8, :128] + part[:8, 128:] + part[8:, :128])
        return total

    own, other = half(got_ref), half(other_ref)
    lower = core_ref[0] == 0
    total = jnp.concatenate([jnp.where(lower, own, other), jnp.where(lower, other, own)], axis=0)
    sums = [jnp.concatenate([total[5 * s + t : 5 * s + t + 1] for t in range(5)], axis=1) for s in range(3)]
    shift_grad_ref[...], gain_grad_ref[...], bias_ref[...] = [value.reshape(C) for value in sums]
    groups = group_matrix()
    gain, mean, rstd = gain_ref[...], row_ref[0:1], row_ref[1:2]

    both = jnp.concatenate([gain * sums[0], gain * sums[1], jnp.zeros((6, C), f32)], axis=0)
    both = exact_dot(exact_dot(both, groups, 0), groups, 1) / TOTAL
    first, second = both[0:1], both[1:2]
    xhat = (feat_ref[...].astype(f32) - mean) * rstd
    grad_ref[...] = (rstd * (da_ref[...] * gain - first - xhat * second)).astype(bf16)
    weight = got_ref[0, :W_ROWS].astype(f32)
    for z in range(1, NZ):
        weight = weight + got_ref[z, :W_ROWS].astype(f32)
    for i in range(3):
        for j in range(3):
            at = slice(j * NQ, (j + 1) * NQ)
            weight_ref[i, j, 0:16] = weight[16 * i : 16 * i + 16, at]
            weight_ref[i, j, 16:20] = weight[48 + 4 * i : 52 + 4 * i, at]


def flip(value):
    return lax.ppermute(value, "core", [(0, 1), (1, 0)])


def shape(dims, dtype):
    return jax.ShapeDtypeStruct(dims, dtype)


def body(features, cotangent, conv_weight, gain, shift):
    core, y = lax.axis_index("core"), lax.axis_index("y")
    at_core, at_y = core.reshape(1), y.reshape(1)
    feat, cot = features.reshape(PIX, C), cotangent.reshape(PIX, C)
    gain, shift = gain.reshape(1, C), shift.reshape(1, C)
    cot2, feat2 = flip(cot), flip(feat)

    edge = jnp.where(
        core == 0,
        jnp.concatenate([cot[PIX - TC :], cot2[PIX - TC :]]),
        jnp.concatenate([cot2[:TC], cot[:TC]]),
    )
    count = NZ * NY
    ways = [(2 * k, 2 * k + 2) for k in range(count - 1)] + [(2 * k + 3, 2 * k + 1) for k in range(count - 1)]
    mine = lax.ppermute(edge, ("z", "y", "core"), ways)
    theirs = flip(mine)

    stats, bias = pl.pallas_call(
        stats_kernel,
        out_shape=(shape((NZ, 8, 128), f32), shape((8, C), f32)),
        in_specs=[pl.BlockSpec(memory_space=pltpu.HBM)] * 2 + [vmem()],
        out_specs=(vmem(), vmem()),
        scratch_shapes=[pltpu.VMEM((PIX, C), bf16)] * 2 + [pltpu.SemaphoreType.DMA((2,))],
        compiler_params=params(),
        name="stats",
    )(feat, cot, feat2)
    stats, mine = lax.optimization_barrier((stats, mine))
    stats = lax.all_to_all(stats, "z", 0, 0)
    packed, rest = pl.pallas_call(
        pack_kernel,
        grid=(1,),
        out_shape=(shape((PEERS, G_ROWS, 128), bf16), shape((NX, 8, 128), f32)),
        in_specs=[smem()] + [whole(PIX, C)] * 3 + [vmem()] * 2,
        out_specs=(vmem(), vmem()),
        compiler_params=params(),
        name="pack",
    )(at_core, feat, cot, cot2, mine, theirs)
    top = jnp.where(core == 0, mine[0], theirs[2 * TC - 1])
    bottom = jnp.where(core == 0, theirs[0], mine[2 * TC - 1])
    column = jnp.where(core == 0, cotangent[:, 0], cotangent[:, TC - 1])
    column = jnp.concatenate([top[None], column, bottom[None]])
    pairs = [(2 * k + 1, 2 * k + 2) for k in range(NX - 1)]
    outer = lax.ppermute(column, ("x", "core"), pairs + [(b, a) for a, b in pairs])
    packed, outer = lax.optimization_barrier((packed, outer))
    packed = pl.pallas_call(
        patch_kernel,
        out_shape=shape((PEERS, G_ROWS, 128), bf16),
        in_specs=[vmem(), vmem(), pl.BlockSpec(memory_space=pl.ANY)],
        out_specs=pl.BlockSpec(memory_space=pl.ANY),
        scratch_shapes=[pltpu.VMEM((PEERS, S_ROWS, 128), bf16), pltpu.SemaphoreType.DMA],
        input_output_aliases={2: 0},
        compiler_params=params(),
        name="patch",
    )(stats, rest, packed)
    slab = lax.all_to_all(packed, ("y", "x"), 0, 0)
    slab_other = flip(slab)

    back = pl.pallas_call(
        back_kernel,
        grid=(1,),
        out_shape=shape((PIX, C), f32),
        in_specs=[smem()] + [whole(PIX, C)] * 2 + [vmem()] * 3 + [pl.BlockSpec(memory_space=pl.ANY)],
        out_specs=vmem(),
        scratch_shapes=[
            pltpu.VMEM((3, (TR + 2) * TC, C), bf16),
            pltpu.VMEM((9, C, C), bf16),
            pltpu.SemaphoreType.DMA((9,)),
        ],
        compiler_params=params(),
        cost_estimate=pl.CostEstimate(flops=2 * PIX * 9 * C * C, bytes_accessed=18 * C * C, transcendentals=0),
        name="back",
    )(at_core, cot, cot2, mine, theirs, outer, conv_weight)
    slab, back = lax.optimization_barrier((slab, back))

    row, da, table, sums = pl.pallas_call(
        sums_kernel,
        grid=(1,),
        out_shape=(shape((8, C), f32), shape((PIX, C), f32), shape((8, 256), f32), shape((2 * PEERS, 8, 128), f32)),
        in_specs=[smem(), vmem(), whole(PIX, C), vmem(), whole(1, C), whole(1, C), vmem()],
        out_specs=(vmem(), vmem(), vmem(), vmem()),
        scratch_shapes=[pltpu.VMEM((16, 128), f32)],
        compiler_params=params(),
        name="sums",
    )(at_y, slab, feat, back, gain, shift, bias)
    sums = lax.all_to_all(sums, ("y", "x", "core"), 0, 0)

    terms = pl.pallas_call(
        terms_kernel,
        out_shape=shape((NZ, W_ROWS, 256), bf16),
        in_specs=[smem()] + [vmem()] * 3,
        out_specs=vmem(),
        scratch_shapes=[
            pltpu.VMEM((ROWS * 128, 256), bf16),
            pltpu.VMEM(((ROWS + 2) * 128, 128), bf16),
            pltpu.VMEM((256, (ROWS + 2) * 128), bf16),
            pltpu.VMEM((NZ, 16, 256), f32),
        ],
        compiler_params=params(),
        cost_estimate=pl.CostEstimate(
            flops=2 * PIX * 9 * C * C, bytes_accessed=4 << 20, transcendentals=ROWS * 128 * 256
        ),
        name="terms",
    )(at_core, slab, slab_other, table)

    joined = pl.pallas_call(
        join_kernel,
        out_shape=shape((NZ, W_ROWS + V_ROWS, 256), bf16),
        in_specs=[vmem()] * 2,
        out_specs=vmem(),
        compiler_params=params(),
        name="join",
    )(sums, terms)
    joined = lax.all_to_all(joined, "z", 0, 0)
    grad, weight_grad, gain_grad, shift_grad, bias_grad = pl.pallas_call(
        final_kernel,
        grid=(1,),
        out_shape=(shape((PIX, C), bf16), shape((3, 3, 20, NQ), f32)) + (shape((C,), f32),) * 3,
        in_specs=[smem(), vmem(), vmem(), whole(PIX, C), vmem(), vmem(), whole(1, C)],
        out_specs=(vmem(),) * 5,
        compiler_params=params(),
        name="final",
    )(at_core, joined, flip(joined), feat, da, row, gain)
    return grad.reshape(features.shape), weight_grad, gain_grad, shift_grad, bias_grad


def solution(mesh):
    grid = Mesh(mesh.devices.reshape(NZ, NY, NX, 2), ("z", "y", "x", "core"))
    rows, cols = ("z", "y"), ("x", "core")
    tiled = P(rows, cols, None)
    return jax.shard_map(
        body,
        mesh=grid,
        in_specs=(tiled, tiled, P(), P(), P()),
        out_specs=(tiled, P(None, None, rows, cols), P(), P(), P()),
        check_vma=False,
    )
```

```python
import jax
import jax.numpy as jnp
from jax import lax
from jax.experimental import pallas as pl
from jax.experimental.pallas import tpu as pltpu
from jax.sharding import Mesh
from jax.sharding import PartitionSpec as P

C = 640
GW = 40
TR, TC = 8, 16
PIX = TR * TC
NZ, NY, NX = 8, 4, 4
PEERS = NY * NX
ROWS = NY * TR
NQ = 80
CHIP = float(2 * PIX * GW)
TOTAL = float(NZ * PEERS) * CHIP
VMEM_LIMIT = 48 * 1024 * 1024
F_ROWS, C_ROWS, S_ROWS = 160, 160, 16
S_AT = F_ROWS + C_ROWS
G_ROWS = S_AT + S_ROWS
E_ROWS = 96
W_ROWS, V_ROWS = 64, 16
f32, bf16 = jnp.float32, jnp.bfloat16


def lanes(count):
    return lax.broadcasted_iota(jnp.int32, (1, count), 1)


def slab_channel(main, at):
    z = jnp.where(main, at >> 4, at >> 2)
    return z * 80 + jnp.where(main, at & 15, 16 + (at & 3))


def feature_columns():
    lane = lanes(C)
    main = lane < 512
    y = jnp.where(main, lane >> 7, (lane - 512) >> 5)
    return slab_channel(main, jnp.where(main, lane & 127, lane & 31)) + y * 20


def cotangent_columns(core, side):
    lane = lanes(C)
    main = lane < 512
    x = jnp.where(main, lane >> 7, (lane - 512) >> 5)
    at = jnp.where(main, lane & 127, lane & 31)
    q = jnp.where(main, at & 63, 64 + (at & 15))
    mine = jnp.where(main, at >> 6, at >> 4) == side
    return jnp.where(mine, x * 160 + core * NQ + q, -1)


def term_columns(y):
    lane = lanes(256)
    main = lane < 128
    return slab_channel(main, jnp.where(main, lane, lane & 31)) + y * 20


def vmem():
    return pl.BlockSpec(memory_space=pltpu.VMEM)


def smem():
    return pl.BlockSpec(memory_space=pltpu.SMEM)


def hbm():
    return pl.BlockSpec(memory_space=pltpu.HBM)


def fetch(pairs, sem):
    copies = [pltpu.make_async_copy(src, dst, sem.at[k]) for k, (src, dst) in enumerate(pairs)]
    for copy in copies:
        copy.start()
    return copies


def params(**kw):
    return pltpu.CompilerParams(vmem_limit_bytes=VMEM_LIMIT, **kw)


def group_matrix():
    chan = lax.broadcasted_iota(jnp.int32, (C, 128), 0)
    low = lax.broadcasted_iota(jnp.int32, (C, 128), 1) * GW
    return jnp.where((chan >= low) & (chan < low + GW), 1.0, 0.0).astype(bf16)


def exact_dot(value, matrix, over):
    high, middle, low = three(value)
    stacked = jnp.concatenate([high, middle, low, jnp.zeros_like(low)], axis=0).astype(bf16)
    out = lax.dot_general(stacked, matrix, (((1,), (over,)), ((), ())), preferred_element_type=f32)
    return out[0:8] + out[8:16] + out[16:24]


def rows8(row):
    return jnp.broadcast_to(row, (8, row.shape[1]))


def pick(columns):
    rows = lax.broadcasted_iota(jnp.int32, (C, columns.shape[1]), 0)
    return (rows == columns).astype(f32).astype(bf16)


def three(value):
    high = value.astype(bf16).astype(f32)
    rest = value - high
    middle = rest.astype(bf16).astype(f32)
    return high, middle, rest - middle


def lanes32(value, height):
    group = lax.broadcasted_iota(jnp.int32, (height, 128), 1) // 32
    out = []
    for a in range(4):
        acc = jnp.zeros((height, 128), f32)
        for g in range(4):
            moved = pltpu.roll(value[height * g : height * (g + 1)], (32 * (g - a)) % 128, 1)
            acc = jnp.where(group == g, moved, acc)
        out.append(acc)
    return out


def put_pieces(mean, squares):
    pieces = three(mean) + three(squares)
    row = lax.broadcasted_iota(jnp.int32, (S_ROWS, 128), 0)
    out = jnp.zeros((S_ROWS, 128), f32)
    for k in range(6):
        out = jnp.where(row == k, pieces[k], out)
    return out.astype(bf16)


def merge_pieces(got, count):
    got = got.astype(f32)
    return merge(got[:, 0] + got[:, 1] + got[:, 2], got[:, 3] + got[:, 4] + got[:, 5], count)


def in_order(core, own, other):
    a, b = own[...].astype(f32), other[...].astype(f32)
    return jnp.where(core == 0, a, b).astype(bf16), jnp.where(core == 0, b, a).astype(bf16)


def blocks(core, first, second):
    return jnp.dot(first, pick(cotangent_columns(core, 0)), preferred_element_type=f32) + jnp.dot(
        second, pick(cotangent_columns(core, 1)), preferred_element_type=f32
    )


def pack_kernel(core_ref, both_ref, feat2_ref, cot2_ref, out_ref, bias_ref):
    core = core_ref[0]
    feat_ref, cot_ref = both_ref.at[:PIX], both_ref.at[PIX:]
    x, x2 = feat_ref[...].astype(f32), feat2_ref[...].astype(f32)
    groups = group_matrix()
    total = x.sum(0, keepdims=True) + x2.sum(0, keepdims=True)
    mean = exact_dot(rows8(total), groups, 0) / CHIP
    wide = exact_dot(mean, groups, 1)[:1]
    squares = ((x - wide) ** 2).sum(0, keepdims=True) + ((x2 - wide) ** 2).sum(0, keepdims=True)
    stats = put_pieces(mean[:1], exact_dot(rows8(squares), groups, 0)[:1])
    bias_ref[...] = rows8(cot_ref[...].astype(f32).sum(0, keepdims=True))
    first, second = in_order(core, cot_ref, cot2_ref)
    moved = jnp.dot(feat_ref[...], pick(feature_columns()), preferred_element_type=f32)
    terms = blocks(core, first, second)
    moved_rest = lanes32(moved[:, 512:], 32)
    terms_rest = lanes32(terms[:, 512:], 32)
    for y in range(NY):
        for xx in range(NX):
            p = y * NX + xx
            out_ref[p, 0:128] = moved[:, y * 128 : (y + 1) * 128].astype(bf16)
            out_ref[p, 128:160] = moved_rest[y].astype(bf16)
            out_ref[p, 160:288] = terms[:, xx * 128 : (xx + 1) * 128].astype(bf16)
            out_ref[p, 288:320] = terms_rest[xx].astype(bf16)
            out_ref[p, S_AT:] = stats


def merge(means, squares, count):
    n = means.shape[0]
    mean = means.sum(0, keepdims=True) / n
    return mean, squares.sum(0, keepdims=True) + count * ((means - mean) ** 2).sum(0, keepdims=True)


def cot_rows(main, rest, g, side):
    lane = lax.broadcasted_iota(jnp.int32, main.shape, 1)
    main = pltpu.roll(main, 64, 1) if side else main
    return jnp.where(lane < 64, main, pltpu.roll(rest, (64 - 32 * g - 16 * side) % 128, 1))


def split_kernel(z_ref, slab_ref, out_ref):
    mean, squares = merge_pieces(slab_ref[:, S_AT:], CHIP)
    stats = put_pieces(mean, squares)
    group = lax.broadcasted_iota(jnp.int32, (TC, 128), 1) // 32
    first, last = jnp.zeros((TC, 128), f32), jnp.zeros((TC, 128), f32)
    for xx in range(NX):
        tail = slab_ref[xx, 288:304].astype(f32)
        first = jnp.where(group == xx, pltpu.roll(tail, 32 * xx, 1) if xx else tail, first)
        tail = slab_ref[(NY - 1) * NX + xx, 304:320].astype(f32)
        last = jnp.where(group == xx, pltpu.roll(tail, (32 * xx + 32) % 128, 1) if xx < 3 else tail, last)
    first, last = first.astype(bf16), last.astype(bf16)
    for p in range(NZ):
        out_ref[p, :S_ROWS] = stats

        @pl.when(z_ref[0] < p)
        def _():
            for xx in range(NX):
                out_ref[p, 16 + 16 * xx : 32 + 16 * xx] = slab_ref[(NY - 1) * NX + xx, 272:288]
            out_ref[p, 80:] = last

        @pl.when(z_ref[0] >= p)
        def _():
            for xx in range(NX):
                out_ref[p, 16 + 16 * xx : 32 + 16 * xx] = slab_ref[xx, 160:176]
            out_ref[p, 80:] = first


def back_kernel(core_ref, both_ref, cot2_ref, mine_ref, theirs_ref, outer_ref, w_hbm, out_ref, shifted, w_ref, sem):
    copies = fetch([(w_hbm.at[t // 3, t % 3], w_ref.at[t]) for t in range(9)], sem)
    rows = (TR + 2) * TC
    lower = core_ref[0] == 0
    mine, theirs = mine_ref[...].astype(f32), theirs_ref[...].astype(f32)
    top, bottom = jnp.where(lower, mine, theirs), jnp.where(lower, theirs, mine)
    corner = 2 * TC
    own_top, other_top = jnp.where(lower, top[:TC], top[TC:corner]), jnp.where(lower, top[TC:corner], top[:TC])
    own_bot, other_bot = jnp.where(lower, bottom[:TC], bottom[TC:corner]), jnp.where(lower, bottom[TC:corner], bottom[:TC])
    wide = jnp.concatenate([own_top, both_ref[PIX:].astype(f32), own_bot], axis=0)
    near = jnp.concatenate([other_top, cot2_ref[...].astype(f32), other_bot], axis=0)
    near = near.reshape(TR + 2, TC, C)
    inner = jnp.where(lower, near[:, :1], near[:, TC - 1 :])
    top_corner = jnp.where(lower, top[corner : corner + 1], top[corner + 1 : corner + 2])
    bot_corner = jnp.where(lower, bottom[corner : corner + 1], bottom[corner + 1 : corner + 2])
    outer = jnp.concatenate(
        [top_corner[None], outer_ref[...].astype(f32)[:, None, :], bot_corner[None]], axis=0
    )
    left, right = jnp.where(lower, outer, inner), jnp.where(lower, inner, outer)
    left = jnp.broadcast_to(left, (TR + 2, TC, C)).reshape(rows, C)
    right = jnp.broadcast_to(right, (TR + 2, TC, C)).reshape(rows, C)
    col = lax.broadcasted_iota(jnp.int32, (rows, C), 0) % TC
    shifted[0] = jnp.where(col == 0, left, pltpu.roll(wide, 1, 0)).astype(bf16)
    shifted[1] = wide.astype(bf16)
    shifted[2] = jnp.where(col == TC - 1, right, pltpu.roll(wide, rows - 1, 0)).astype(bf16)
    total = jnp.zeros((C, PIX), f32)
    for t in range(9):
        i, j = t // 3, t % 3
        copies[t].wait()
        pixels = shifted[2 - j, (2 - i) * TC : (2 - i) * TC + PIX]
        total = total + lax.dot_general(
            w_ref[t], pixels, (((1,), (1,)), ((), ())), preferred_element_type=f32
        )
    out_ref[...] = total.T


def sums_kernel(y_ref, stat_ref, feat_hbm, back_ref, gain_ref, shift_ref, bias_ref,
                row_ref, da_ref, par_ref, out_ref, block, feat_ref, sem):
    copies = fetch(((feat_hbm, feat_ref),), sem)
    mean, squares = merge_pieces(stat_ref[:, :S_ROWS], PEERS * CHIP)
    groups = group_matrix()
    both = jnp.concatenate([mean, lax.rsqrt(squares / TOTAL + 1e-05), jnp.zeros((6, 128), f32)], axis=0)
    both = exact_dot(both, groups, 1)
    mean, rstd = both[0:1], both[1:2]
    gain, shift = gain_ref[...], shift_ref[...]
    row = lax.broadcasted_iota(jnp.int32, (8, C), 0)
    row_ref[...] = jnp.where(row == 0, mean, rstd)
    table = jnp.where(row == 0, mean, jnp.where(row == 1, rstd * gain, jnp.where(row == 2, shift, 0.0)))
    par_ref[...] = exact_dot(table, pick(term_columns(y_ref[0])), 0)
    copies[0].wait()
    xhat = (feat_ref[...].astype(f32) - mean) * rstd
    act = xhat * gain + shift
    sig = jax.nn.sigmoid(act)
    da = back_ref[...] * sig * (1.0 + act * (1.0 - sig))
    da_ref[...] = da
    sums = (da.sum(0, keepdims=True), (da * xhat).sum(0, keepdims=True), bias_ref[:1])
    block[...] = jnp.zeros_like(block)
    for s in range(3):
        for t in range(5):
            block[5 * s + t : 5 * s + t + 1] = sums[s][:, 128 * t : 128 * t + 128]
    for p in range(2 * PEERS):
        out_ref[p] = block[8 * (p % 2) : 8 * (p % 2) + 8]


def terms_kernel(core_ref, z_ref, own_ref, other_ref, edge_ref, par_ref, out_ref, hid, strips, cot3, rest):
    core = core_ref[0]

    def put(block, peer, side):
        y, xx = peer // NX, peer % NX

        def silu(x, lanes):
            a = (x.astype(f32) - par_ref[0:1, lanes]) * par_ref[1:2, lanes] + par_ref[2:3, lanes]
            return a * jax.nn.sigmoid(a)

        main = silu(block[:128], slice(0, 128)).astype(bf16)
        tail = silu(block[128:], slice(128, 256))
        for g in range(4):
            low = pltpu.roll(tail, (128 - 32 * g) % 128, 1).astype(bf16)
            for h in range(2):
                r = 2 * g + h
                at = pl.ds(pl.multiple_of((y * TR + r) * 128 + xx * 32 + side * TC, TC), TC)
                hid[at, 0:128] = main[r * TC : (r + 1) * TC]
                hid[at, 128:256] = low[h * TC : (h + 1) * TC]

    for peer in range(PEERS):
        put(own_ref[peer, :F_ROWS], peer, core)
        put(other_ref[peer, :F_ROWS], peer, 1 - core)
        y, xx = peer // NX, peer % NX
        tail = own_ref[peer, 288:320].astype(f32)
        for g in range(4):
            main = own_ref[peer, 160 + 32 * g : 192 + 32 * g].astype(f32)
            for side in range(2):
                value = cot_rows(main, tail, g, side).astype(bf16)
                for h in range(2):
                    at = (y * TR + 2 * g + h + 1) * 128 + xx * 32 + side * TC
                    strips[at : at + TC] = value[h * TC : (h + 1) * TC]
    z = z_ref[0]
    for start, peer, there in ((0, jnp.maximum(z - 1, 0), z > 0),
                               ((ROWS + 1) * 128, jnp.minimum(z + 1, NZ - 1), z < NZ - 1)):
        got = jnp.where(there, edge_ref[peer].astype(f32), 0.0)
        for xx in range(NX):
            for side in range(2):
                at = start + xx * 32 + side * TC
                value = cot_rows(got[16 + 16 * xx : 32 + 16 * xx], got[80:], xx, side)
                strips[at : at + TC] = value.astype(bf16)
    lane = lax.broadcasted_iota(jnp.int32, (NQ, 128), 1)
    for row in range(ROWS + 2):
        at = slice(row * 128, (row + 1) * 128)
        turned = strips[at].astype(f32).T[:NQ]
        before = jnp.where(lane == 0, 0.0, pltpu.roll(turned, 1, 1))
        after = jnp.where(lane == 127, 0.0, pltpu.roll(turned, 127, 1))
        cot3[0:NQ, at] = after.astype(bf16)
        cot3[NQ : 2 * NQ, at] = turned.astype(bf16)
        cot3[2 * NQ : 3 * NQ, at] = before.astype(bf16)
    cot3[3 * NQ :] = jnp.zeros((16, (ROWS + 2) * 128), bf16)
    rest[...] = jnp.zeros_like(rest)
    for i in range(3):
        lhs = cot3[:, (2 - i) * 128 : (2 - i) * 128 + ROWS * 128]
        turned = jnp.dot(lhs, hid[...], preferred_element_type=f32).T
        for z in range(NZ):
            out_ref[z, 16 * i : 16 * i + 16] = turned[16 * z : 16 * z + 16].astype(bf16)
            rest[z, 4 * i : 4 * i + 4] = turned[128 + 4 * z : 132 + 4 * z]
    for z in range(NZ):
        out_ref[z, 48:64] = rest[z].astype(bf16)


def join_kernel(sums_ref, terms_ref, out_ref):
    value = sums_ref[0]
    for p in range(1, 2 * PEERS):
        value = value + sums_ref[p]
    high, middle, low = three(value)
    block = jnp.concatenate(
        [jnp.concatenate([high, middle], axis=1), jnp.concatenate([low, jnp.zeros_like(low)], axis=1)], axis=0
    ).astype(bf16)
    for z in range(NZ):
        out_ref[z, :W_ROWS] = terms_ref[z]
        out_ref[z, W_ROWS:] = block


def final_kernel(core_ref, got_ref, other_ref, feat_hbm, da_ref, row_ref, gain_ref,
                 grad_ref, weight_ref, gain_grad_ref, shift_grad_ref, bias_ref, feat_ref, sem):
    copies = fetch(((feat_hbm, feat_ref),), sem)

    def half(ref):
        total = jnp.zeros((8, 128), f32)
        for z in range(NZ):
            part = ref[z, W_ROWS:].astype(f32)
            total = total + (part[:8, :128] + part[:8, 128:] + part[8:, :128])
        return total

    own, other = half(got_ref), half(other_ref)
    lower = core_ref[0] == 0
    total = jnp.concatenate([jnp.where(lower, own, other), jnp.where(lower, other, own)], axis=0)
    sums = [jnp.concatenate([total[5 * s + t : 5 * s + t + 1] for t in range(5)], axis=1) for s in range(3)]
    shift_grad_ref[...], gain_grad_ref[...], bias_ref[...] = [value.reshape(C) for value in sums]
    groups = group_matrix()
    gain, mean, rstd = gain_ref[...], row_ref[0:1], row_ref[1:2]

    both = jnp.concatenate([gain * sums[0], gain * sums[1], jnp.zeros((6, C), f32)], axis=0)
    both = exact_dot(exact_dot(both, groups, 0), groups, 1) / TOTAL
    first, second = both[0:1], both[1:2]
    copies[0].wait()
    xhat = (feat_ref[...].astype(f32) - mean) * rstd
    grad_ref[...] = (rstd * (da_ref[...] * gain - first - xhat * second)).astype(bf16)
    weight = got_ref[0, :W_ROWS].astype(f32)
    for z in range(1, NZ):
        weight = weight + got_ref[z, :W_ROWS].astype(f32)
    for i in range(3):
        for j in range(3):
            at = slice(j * NQ, (j + 1) * NQ)
            weight_ref[i, j, 0:16] = weight[16 * i : 16 * i + 16, at]
            weight_ref[i, j, 16:20] = weight[48 + 4 * i : 52 + 4 * i, at]


def flip(value):
    return lax.ppermute(value, "core", [(0, 1), (1, 0)])


def shape(dims, dtype):
    return jax.ShapeDtypeStruct(dims, dtype)


def body(features, cotangent, conv_weight, gain, shift):
    core, y, z = lax.axis_index("core"), lax.axis_index("y"), lax.axis_index("z")
    at_core, at_y, at_z = core.reshape(1), y.reshape(1), z.reshape(1)
    feat, cot = features.reshape(PIX, C), cotangent.reshape(PIX, C)
    gain, shift = gain.reshape(1, C), shift.reshape(1, C)
    cot2, feat2 = flip(cot), flip(feat)
    both = jnp.concatenate([feat, cot])
    column = jnp.where(core == 0, cotangent[:, 0], cotangent[:, TC - 1])
    pairs = [(2 * k + 1, 2 * k + 2) for k in range(NX - 1)]
    outer = lax.ppermute(column, ("x", "core"), pairs + [(b, a) for a, b in pairs])
    outer2 = flip(outer)
    spare = jnp.zeros((6, C), bf16)
    edge = jnp.where(
        core == 0,
        jnp.concatenate([cot[PIX - TC :], cot2[PIX - TC :], outer[TR - 1 :], outer2[TR - 1 :], spare]),
        jnp.concatenate([cot2[:TC], cot[:TC], outer2[:1], outer[:1], spare]),
    )
    count = NZ * NY
    ways = [(2 * k, 2 * k + 2) for k in range(count - 1)] + [(2 * k + 3, 2 * k + 1) for k in range(count - 1)]
    mine = lax.ppermute(edge, ("z", "y", "core"), ways)

    packed, bias = pl.pallas_call(
        pack_kernel,
        out_shape=(shape((PEERS, G_ROWS, 128), bf16), shape((8, C), f32)),
        in_specs=[smem()] + [vmem()] * 3,
        out_specs=(vmem(), vmem()),
        compiler_params=params(),
        cost_estimate=pl.CostEstimate(flops=1 << 28, bytes_accessed=2 << 20, transcendentals=0),
        name="pack",
    )(at_core, both, feat2, cot2)
    packed, outer = lax.optimization_barrier((packed, outer))
    slab = lax.all_to_all(packed, ("y", "x"), 0, 0)
    slab, mine = lax.optimization_barrier((slab, mine))
    edges = pl.pallas_call(
        split_kernel,
        out_shape=shape((NZ, E_ROWS, 128), bf16),
        in_specs=[smem(), vmem()],
        out_specs=vmem(),
        compiler_params=params(),
        name="split",
    )(at_z, slab)
    slab_other = flip(slab)
    edges = lax.all_to_all(edges, "z", 0, 0)
    theirs = flip(mine)
    back = pl.pallas_call(
        back_kernel,
        out_shape=shape((PIX, C), f32),
        in_specs=[smem()] + [vmem()] * 5 + [hbm()],
        out_specs=vmem(),
        scratch_shapes=[
            pltpu.VMEM((3, (TR + 2) * TC, C), bf16),
            pltpu.VMEM((9, C, C), bf16),
            pltpu.SemaphoreType.DMA((9,)),
        ],
        compiler_params=params(),
        cost_estimate=pl.CostEstimate(flops=2 * PIX * 9 * C * C, bytes_accessed=18 * C * C, transcendentals=0),
        name="back",
    )(at_core, both, cot2, mine, theirs, outer, conv_weight)


    row, da, table, sums = pl.pallas_call(
        sums_kernel,
        out_shape=(shape((8, C), f32), shape((PIX, C), f32), shape((8, 256), f32), shape((2 * PEERS, 8, 128), f32)),
        in_specs=[smem(), vmem(), hbm(), vmem(), vmem(), vmem(), vmem()],
        out_specs=(vmem(), vmem(), vmem(), vmem()),
        scratch_shapes=[
            pltpu.VMEM((16, 128), f32),
            pltpu.VMEM((PIX, C), bf16),
            pltpu.SemaphoreType.DMA((1,)),
        ],
        compiler_params=params(),
        name="sums",
    )(at_y, edges, feat, back, gain, shift, bias)
    sums = lax.all_to_all(sums, ("y", "x", "core"), 0, 0)

    terms = pl.pallas_call(
        terms_kernel,
        out_shape=shape((NZ, W_ROWS, 256), bf16),
        in_specs=[smem()] * 2 + [vmem()] * 4,
        out_specs=vmem(),
        scratch_shapes=[
            pltpu.VMEM((ROWS * 128, 256), bf16),
            pltpu.VMEM(((ROWS + 2) * 128, 128), bf16),
            pltpu.VMEM((256, (ROWS + 2) * 128), bf16),
            pltpu.VMEM((NZ, 16, 256), f32),
        ],
        compiler_params=params(),
        cost_estimate=pl.CostEstimate(
            flops=2 * PIX * 9 * C * C, bytes_accessed=4 << 20, transcendentals=ROWS * 128 * 256
        ),
        name="terms",
    )(at_core, at_z, slab, slab_other, edges, table)

    joined = pl.pallas_call(
        join_kernel,
        out_shape=shape((NZ, W_ROWS + V_ROWS, 256), bf16),
        in_specs=[vmem()] * 2,
        out_specs=vmem(),
        compiler_params=params(),
        name="join",
    )(sums, terms)
    joined = lax.all_to_all(joined, "z", 0, 0)
    grad, weight_grad, gain_grad, shift_grad, bias_grad = pl.pallas_call(
        final_kernel,
        out_shape=(shape((PIX, C), bf16), shape((3, 3, 20, NQ), f32)) + (shape((C,), f32),) * 3,
        in_specs=[smem(), vmem(), vmem(), hbm(), vmem(), vmem(), vmem()],
        out_specs=(vmem(),) * 5,
        scratch_shapes=[pltpu.VMEM((PIX, C), bf16), pltpu.SemaphoreType.DMA((1,))],
        compiler_params=params(),
        name="final",
    )(at_core, joined, flip(joined), feat, da, row, gain)
    return grad.reshape(features.shape), weight_grad, gain_grad, shift_grad, bias_grad


def solution(mesh):
    grid = Mesh(mesh.devices.reshape(NZ, NY, NX, 2), ("z", "y", "x", "core"))
    rows, cols = ("z", "y"), ("x", "core")
    tiled = P(rows, cols, None)
    return jax.shard_map(
        body,
        mesh=grid,
        in_specs=(tiled, tiled, P(), P(), P()),
        out_specs=(tiled, P(None, None, rows, cols), P(), P(), P()),
        check_vma=False,
    )
```

```python
import jax
import jax.numpy as jnp
from jax import lax
from jax.experimental import pallas as pl
from jax.experimental.pallas import tpu as pltpu
from jax.sharding import Mesh
from jax.sharding import PartitionSpec as P

C = 640
GW = 40
TR, TC = 8, 16
PIX = TR * TC
NZ, NY, NX = 8, 4, 4
PEERS = NY * NX
ROWS = NY * TR
NQ = 80
CHIP = float(2 * PIX * GW)
TOTAL = float(NZ * PEERS) * CHIP
VMEM_LIMIT = 48 * 1024 * 1024
F_ROWS, C_ROWS, S_ROWS = 160, 160, 16
S_AT = F_ROWS + C_ROWS
G_ROWS = S_AT + S_ROWS
E_ROWS = 96
W_ROWS, V_ROWS = 64, 16
f32, bf16 = jnp.float32, jnp.bfloat16


def lanes(count):
    return lax.broadcasted_iota(jnp.int32, (1, count), 1)


def slab_channel(main, at):
    z = jnp.where(main, at >> 4, at >> 2)
    return z * 80 + jnp.where(main, at & 15, 16 + (at & 3))


def feature_columns():
    lane = lanes(C)
    main = lane < 512
    y = jnp.where(main, lane >> 7, (lane - 512) >> 5)
    return slab_channel(main, jnp.where(main, lane & 127, lane & 31)) + y * 20


def cotangent_columns(core, side):
    lane = lanes(C)
    main = lane < 512
    x = jnp.where(main, lane >> 7, (lane - 512) >> 5)
    at = jnp.where(main, lane & 127, lane & 31)
    q = jnp.where(main, at & 63, 64 + (at & 15))
    mine = jnp.where(main, at >> 6, at >> 4) == side
    return jnp.where(mine, x * 160 + core * NQ + q, -1)


def term_columns(y):
    lane = lanes(256)
    main = lane < 128
    return slab_channel(main, jnp.where(main, lane, lane & 31)) + y * 20


def vmem():
    return pl.BlockSpec(memory_space=pltpu.VMEM)


def smem():
    return pl.BlockSpec(memory_space=pltpu.SMEM)


def hbm():
    return pl.BlockSpec(memory_space=pltpu.HBM)


def fetch(pairs, sem):
    copies = [pltpu.make_async_copy(src, dst, sem.at[k]) for k, (src, dst) in enumerate(pairs)]
    for copy in copies:
        copy.start()
    return copies


def params(**kw):
    return pltpu.CompilerParams(vmem_limit_bytes=VMEM_LIMIT, **kw)


def group_matrix():
    chan = lax.broadcasted_iota(jnp.int32, (C, 128), 0)
    low = lax.broadcasted_iota(jnp.int32, (C, 128), 1) * GW
    return jnp.where((chan >= low) & (chan < low + GW), 1.0, 0.0).astype(bf16)


def exact_dot(value, matrix, over):
    high, middle, low = three(value)
    stacked = jnp.concatenate([high, middle, low, jnp.zeros_like(low)], axis=0).astype(bf16)
    out = lax.dot_general(stacked, matrix, (((1,), (over,)), ((), ())), preferred_element_type=f32)
    return out[0:8] + out[8:16] + out[16:24]


def rows8(row):
    return jnp.broadcast_to(row, (8, row.shape[1]))


def pick(columns):
    rows = lax.broadcasted_iota(jnp.int32, (C, columns.shape[1]), 0)
    return (rows == columns).astype(f32).astype(bf16)


def three(value):
    high = value.astype(bf16).astype(f32)
    rest = value - high
    middle = rest.astype(bf16).astype(f32)
    return high, middle, rest - middle


def lanes32(value, height):
    group = lax.broadcasted_iota(jnp.int32, (height, 128), 1) // 32
    out = []
    for a in range(4):
        acc = jnp.zeros((height, 128), f32)
        for g in range(4):
            moved = pltpu.roll(value[height * g : height * (g + 1)], (32 * (g - a)) % 128, 1)
            acc = jnp.where(group == g, moved, acc)
        out.append(acc)
    return out


def put_pieces(mean, squares):
    pieces = three(mean) + three(squares)
    row = lax.broadcasted_iota(jnp.int32, (S_ROWS, 128), 0)
    out = jnp.zeros((S_ROWS, 128), f32)
    for k in range(6):
        out = jnp.where(row == k, pieces[k], out)
    return out.astype(bf16)


def merge_pieces(got, count):
    got = got.astype(f32)
    return merge(got[:, 0] + got[:, 1] + got[:, 2], got[:, 3] + got[:, 4] + got[:, 5], count)


def in_order(core, own, other):
    a, b = own[...].astype(f32), other[...].astype(f32)
    return jnp.where(core == 0, a, b).astype(bf16), jnp.where(core == 0, b, a).astype(bf16)


def blocks(core, first, second):
    return jnp.dot(first, pick(cotangent_columns(core, 0)), preferred_element_type=f32) + jnp.dot(
        second, pick(cotangent_columns(core, 1)), preferred_element_type=f32
    )


def pack_kernel(core_ref, both_ref, feat2_ref, cot2_ref, out_hbm, bias_ref, out_ref, sem):
    core = core_ref[0]
    feat_ref, cot_ref = both_ref.at[:PIX], both_ref.at[PIX:]
    x, x2 = feat_ref[...].astype(f32), feat2_ref[...].astype(f32)
    groups = group_matrix()
    total = x.sum(0, keepdims=True) + x2.sum(0, keepdims=True)
    mean = exact_dot(rows8(total), groups, 0) / CHIP
    wide = exact_dot(mean, groups, 1)[:1]
    squares = ((x - wide) ** 2).sum(0, keepdims=True) + ((x2 - wide) ** 2).sum(0, keepdims=True)
    stats = put_pieces(mean[:1], exact_dot(rows8(squares), groups, 0)[:1])
    bias_ref[...] = rows8(cot_ref[...].astype(f32).sum(0, keepdims=True))
    moved = jnp.dot(feat_ref[...], pick(feature_columns()), preferred_element_type=f32)
    moved_rest = lanes32(moved[:, 512:], 32)
    for p in range(PEERS):
        y = p // NX
        out_ref[p, 0:128] = moved[:, y * 128 : (y + 1) * 128].astype(bf16)
        out_ref[p, 128:160] = moved_rest[y].astype(bf16)
    copies = fetch(((out_ref.at[:, :F_ROWS, :], out_hbm.at[:, :F_ROWS, :]),), sem.at[0:1])
    first, second = in_order(core, cot_ref, cot2_ref)
    terms = blocks(core, first, second)
    terms_rest = lanes32(terms[:, 512:], 32)
    for p in range(PEERS):
        xx = p % NX
        out_ref[p, 160:288] = terms[:, xx * 128 : (xx + 1) * 128].astype(bf16)
        out_ref[p, 288:320] = terms_rest[xx].astype(bf16)
        out_ref[p, S_AT:] = stats
    copies += fetch(((out_ref.at[:, F_ROWS:, :], out_hbm.at[:, F_ROWS:, :]),), sem.at[1:2])
    for copy in copies:
        copy.wait()


def merge(means, squares, count):
    n = means.shape[0]
    mean = means.sum(0, keepdims=True) / n
    return mean, squares.sum(0, keepdims=True) + count * ((means - mean) ** 2).sum(0, keepdims=True)


def cot_rows(main, rest, g, side):
    lane = lax.broadcasted_iota(jnp.int32, main.shape, 1)
    main = pltpu.roll(main, 64, 1) if side else main
    return jnp.where(lane < 64, main, pltpu.roll(rest, (64 - 32 * g - 16 * side) % 128, 1))


def split_kernel(z_ref, slab_ref, out_ref):
    mean, squares = merge_pieces(slab_ref[:, S_AT:], CHIP)
    stats = put_pieces(mean, squares)
    group = lax.broadcasted_iota(jnp.int32, (TC, 128), 1) // 32
    first, last = jnp.zeros((TC, 128), f32), jnp.zeros((TC, 128), f32)
    for xx in range(NX):
        tail = slab_ref[xx, 288:304].astype(f32)
        first = jnp.where(group == xx, pltpu.roll(tail, 32 * xx, 1) if xx else tail, first)
        tail = slab_ref[(NY - 1) * NX + xx, 304:320].astype(f32)
        last = jnp.where(group == xx, pltpu.roll(tail, (32 * xx + 32) % 128, 1) if xx < 3 else tail, last)
    first, last = first.astype(bf16), last.astype(bf16)
    for p in range(NZ):
        out_ref[p, :S_ROWS] = stats

        @pl.when(z_ref[0] < p)
        def _():
            for xx in range(NX):
                out_ref[p, 16 + 16 * xx : 32 + 16 * xx] = slab_ref[(NY - 1) * NX + xx, 272:288]
            out_ref[p, 80:] = last

        @pl.when(z_ref[0] >= p)
        def _():
            for xx in range(NX):
                out_ref[p, 16 + 16 * xx : 32 + 16 * xx] = slab_ref[xx, 160:176]
            out_ref[p, 80:] = first


def back_kernel(core_ref, both_ref, cot2_ref, mine_ref, theirs_ref, beside_ref, w_hbm, out_ref, shifted, w_ref, sem):
    copies = fetch([(w_hbm.at[t // 3, t % 3], w_ref.at[t]) for t in range(9)], sem)
    rows = (TR + 2) * TC
    lower = core_ref[0] == 0
    mine, theirs = mine_ref[...].astype(f32), theirs_ref[...].astype(f32)
    top, bottom = jnp.where(lower, mine, theirs), jnp.where(lower, theirs, mine)
    corner = 2 * TC
    own_top, other_top = jnp.where(lower, top[:TC], top[TC:corner]), jnp.where(lower, top[TC:corner], top[:TC])
    own_bot, other_bot = jnp.where(lower, bottom[:TC], bottom[TC:corner]), jnp.where(lower, bottom[TC:corner], bottom[:TC])
    wide = jnp.concatenate([own_top, both_ref[PIX:].astype(f32), own_bot], axis=0)
    near = jnp.concatenate([other_top, cot2_ref[...].astype(f32), other_bot], axis=0)
    near = near.reshape(TR + 2, TC, C)
    inner = jnp.where(lower, near[:, :1], near[:, TC - 1 :])
    top_corner = jnp.where(lower, top[corner : corner + 1], top[corner + 1 : corner + 2])
    bot_corner = jnp.where(lower, bottom[corner : corner + 1], bottom[corner + 1 : corner + 2])
    beside = beside_ref[...].astype(f32).reshape(TR, TC, C)
    outer = jnp.where(lower, beside[:, TC - 1 :], beside[:, :1])
    outer = jnp.concatenate([top_corner[None], outer, bot_corner[None]], axis=0)
    left, right = jnp.where(lower, outer, inner), jnp.where(lower, inner, outer)
    left = jnp.broadcast_to(left, (TR + 2, TC, C)).reshape(rows, C)
    right = jnp.broadcast_to(right, (TR + 2, TC, C)).reshape(rows, C)
    col = lax.broadcasted_iota(jnp.int32, (rows, C), 0) % TC
    shifted[0] = jnp.where(col == 0, left, pltpu.roll(wide, 1, 0)).astype(bf16)
    shifted[1] = wide.astype(bf16)
    shifted[2] = jnp.where(col == TC - 1, right, pltpu.roll(wide, rows - 1, 0)).astype(bf16)
    total = jnp.zeros((C, PIX), f32)
    for t in range(9):
        i, j = t // 3, t % 3
        copies[t].wait()
        pixels = shifted[2 - j, (2 - i) * TC : (2 - i) * TC + PIX]
        total = total + lax.dot_general(
            w_ref[t], pixels, (((1,), (1,)), ((), ())), preferred_element_type=f32
        )
    out_ref[...] = total.T


def sums_kernel(y_ref, stat_ref, both_ref, back_ref, gain_ref, shift_ref, bias_ref,
                row_ref, da_ref, par_ref, out_ref, block):
    mean, squares = merge_pieces(stat_ref[:, :S_ROWS], PEERS * CHIP)
    groups = group_matrix()
    both = jnp.concatenate([mean, lax.rsqrt(squares / TOTAL + 1e-05), jnp.zeros((6, 128), f32)], axis=0)
    both = exact_dot(both, groups, 1)
    mean, rstd = both[0:1], both[1:2]
    gain, shift = gain_ref[...], shift_ref[...]
    row = lax.broadcasted_iota(jnp.int32, (8, C), 0)
    row_ref[...] = jnp.where(row == 0, mean, rstd)
    table = jnp.where(row == 0, mean, jnp.where(row == 1, rstd * gain, jnp.where(row == 2, shift, 0.0)))
    par_ref[...] = exact_dot(table, pick(term_columns(y_ref[0])), 0)
    xhat = (both_ref[:PIX].astype(f32) - mean) * rstd
    act = xhat * gain + shift
    sig = jax.nn.sigmoid(act)
    da = back_ref[...] * sig * (1.0 + act * (1.0 - sig))
    da_ref[...] = da
    sums = (da.sum(0, keepdims=True), (da * xhat).sum(0, keepdims=True), bias_ref[:1])
    block[...] = jnp.zeros_like(block)
    for s in range(3):
        for t in range(5):
            block[5 * s + t : 5 * s + t + 1] = sums[s][:, 128 * t : 128 * t + 128]
    for p in range(2 * PEERS):
        out_ref[p] = block[8 * (p % 2) : 8 * (p % 2) + 8]


def terms_kernel(core_ref, z_ref, own_ref, other_hbm, edge_ref, par_ref, out_ref,
                 hid, strips, cot3, rest, other_ref, sem):
    copies = fetch(((other_hbm.at[:, :F_ROWS, :], other_ref),), sem)
    core = core_ref[0]

    def put(block, peer, side):
        y, xx = peer // NX, peer % NX

        def silu(x, lanes):
            a = (x.astype(f32) - par_ref[0:1, lanes]) * par_ref[1:2, lanes] + par_ref[2:3, lanes]
            return a * jax.nn.sigmoid(a)

        main = silu(block[:128], slice(0, 128)).astype(bf16)
        tail = silu(block[128:], slice(128, 256))
        for g in range(4):
            low = pltpu.roll(tail, (128 - 32 * g) % 128, 1).astype(bf16)
            for h in range(2):
                r = 2 * g + h
                at = pl.ds(pl.multiple_of((y * TR + r) * 128 + xx * 32 + side * TC, TC), TC)
                hid[at, 0:128] = main[r * TC : (r + 1) * TC]
                hid[at, 128:256] = low[h * TC : (h + 1) * TC]

    for peer in range(PEERS):
        put(own_ref[peer, :F_ROWS], peer, core)
        y, xx = peer // NX, peer % NX
        tail = own_ref[peer, 288:320].astype(f32)
        for g in range(4):
            main = own_ref[peer, 160 + 32 * g : 192 + 32 * g].astype(f32)
            for side in range(2):
                value = cot_rows(main, tail, g, side).astype(bf16)
                for h in range(2):
                    at = (y * TR + 2 * g + h + 1) * 128 + xx * 32 + side * TC
                    strips[at : at + TC] = value[h * TC : (h + 1) * TC]
    copies[0].wait()
    for peer in range(PEERS):
        put(other_ref[peer], peer, 1 - core)
    z = z_ref[0]
    for start, peer, there in ((0, jnp.maximum(z - 1, 0), z > 0),
                               ((ROWS + 1) * 128, jnp.minimum(z + 1, NZ - 1), z < NZ - 1)):
        got = jnp.where(there, edge_ref[peer].astype(f32), 0.0)
        for xx in range(NX):
            for side in range(2):
                at = start + xx * 32 + side * TC
                value = cot_rows(got[16 + 16 * xx : 32 + 16 * xx], got[80:], xx, side)
                strips[at : at + TC] = value.astype(bf16)
    lane = lax.broadcasted_iota(jnp.int32, (NQ, 128), 1)
    for row in range(ROWS + 2):
        at = slice(row * 128, (row + 1) * 128)
        turned = strips[at].astype(f32).T[:NQ]
        before = jnp.where(lane == 0, 0.0, pltpu.roll(turned, 1, 1))
        after = jnp.where(lane == 127, 0.0, pltpu.roll(turned, 127, 1))
        cot3[0:NQ, at] = after.astype(bf16)
        cot3[NQ : 2 * NQ, at] = turned.astype(bf16)
        cot3[2 * NQ : 3 * NQ, at] = before.astype(bf16)
    cot3[3 * NQ :] = jnp.zeros((16, (ROWS + 2) * 128), bf16)
    rest[...] = jnp.zeros_like(rest)
    for i in range(3):
        lhs = cot3[:, (2 - i) * 128 : (2 - i) * 128 + ROWS * 128]
        turned = jnp.dot(lhs, hid[...], preferred_element_type=f32).T
        for z in range(NZ):
            out_ref[z, 16 * i : 16 * i + 16] = turned[16 * z : 16 * z + 16].astype(bf16)
            rest[z, 4 * i : 4 * i + 4] = turned[128 + 4 * z : 132 + 4 * z]
    for z in range(NZ):
        out_ref[z, 48:64] = rest[z].astype(bf16)


def join_kernel(sums_ref, terms_ref, out_ref):
    value = sums_ref[0]
    for p in range(1, 2 * PEERS):
        value = value + sums_ref[p]
    high, middle, low = three(value)
    block = jnp.concatenate(
        [jnp.concatenate([high, middle], axis=1), jnp.concatenate([low, jnp.zeros_like(low)], axis=1)], axis=0
    ).astype(bf16)
    for z in range(NZ):
        out_ref[z, :W_ROWS] = terms_ref[z]
        out_ref[z, W_ROWS:] = block


def final_kernel(core_ref, got_ref, other_ref, both_ref, da_ref, row_ref, gain_ref,
                 grad_ref, gain_grad_ref, shift_grad_ref, bias_ref):

    def half(ref):
        total = jnp.zeros((8, 128), f32)
        for z in range(NZ):
            part = ref[z, W_ROWS:].astype(f32)
            total = total + (part[:8, :128] + part[:8, 128:] + part[8:, :128])
        return total

    own, other = half(got_ref), half(other_ref)
    lower = core_ref[0] == 0
    total = jnp.concatenate([jnp.where(lower, own, other), jnp.where(lower, other, own)], axis=0)
    sums = [jnp.concatenate([total[5 * s + t : 5 * s + t + 1] for t in range(5)], axis=1) for s in range(3)]
    shift_grad_ref[...], gain_grad_ref[...], bias_ref[...] = [value.reshape(C) for value in sums]
    groups = group_matrix()
    gain, mean, rstd = gain_ref[...], row_ref[0:1], row_ref[1:2]

    both = jnp.concatenate([gain * sums[0], gain * sums[1], jnp.zeros((6, C), f32)], axis=0)
    both = exact_dot(exact_dot(both, groups, 0), groups, 1) / TOTAL
    first, second = both[0:1], both[1:2]
    xhat = (both_ref[:PIX].astype(f32) - mean) * rstd
    grad_ref[...] = (rstd * (da_ref[...] * gain - first - xhat * second)).astype(bf16)


def gather_kernel(got_ref, weight_ref):
    weight = got_ref[0, :W_ROWS].astype(f32)
    for z in range(1, NZ):
        weight = weight + got_ref[z, :W_ROWS].astype(f32)
    for i in range(3):
        for j in range(3):
            at = slice(j * NQ, (j + 1) * NQ)
            weight_ref[i, j, 0:16] = weight[16 * i : 16 * i + 16, at]
            weight_ref[i, j, 16:20] = weight[48 + 4 * i : 52 + 4 * i, at]


def flip(value):
    return lax.ppermute(value, "core", [(0, 1), (1, 0)])


def shape(dims, dtype):
    return jax.ShapeDtypeStruct(dims, dtype)


def body(features, cotangent, conv_weight, gain, shift):
    core, y, z = lax.axis_index("core"), lax.axis_index("y"), lax.axis_index("z")
    at_core, at_y, at_z = core.reshape(1), y.reshape(1), z.reshape(1)
    feat, cot = features.reshape(PIX, C), cotangent.reshape(PIX, C)
    gain, shift = gain.reshape(1, C), shift.reshape(1, C)
    cot2, feat2 = flip(cot), flip(feat)
    both = jnp.concatenate([feat, cot])
    pairs = [(2 * k + 1, 2 * k + 2) for k in range(NX - 1)]
    beside = lax.ppermute(cot, ("x", "core"), pairs + [(b, a) for a, b in pairs])
    upper = jnp.where(core == 0, beside[TC - 1 : TC], beside[:1])
    lower = jnp.where(core == 0, beside[PIX - 1 :], beside[PIX - TC : PIX - TC + 1])
    corners = flip(jnp.concatenate([upper, lower]))
    spare = jnp.zeros((6, C), bf16)
    edge = jnp.where(
        core == 0,
        jnp.concatenate([cot[PIX - TC :], cot2[PIX - TC :], lower, corners[1:], spare]),
        jnp.concatenate([cot2[:TC], cot[:TC], corners[:1], upper, spare]),
    )
    count = NZ * NY
    ways = [(2 * k, 2 * k + 2) for k in range(count - 1)] + [(2 * k + 3, 2 * k + 1) for k in range(count - 1)]
    mine = lax.ppermute(edge, ("z", "y", "core"), ways)

    packed, bias = pl.pallas_call(
        pack_kernel,
        out_shape=(shape((PEERS, G_ROWS, 128), bf16), shape((8, C), f32)),
        in_specs=[smem()] + [vmem()] * 3,
        out_specs=(hbm(), vmem()),
        scratch_shapes=[pltpu.VMEM((PEERS, G_ROWS, 128), bf16), pltpu.SemaphoreType.DMA((2,))],
        compiler_params=params(),
        cost_estimate=pl.CostEstimate(flops=1 << 28, bytes_accessed=2 << 20, transcendentals=0),
        name="pack",
    )(at_core, both, feat2, cot2)
    packed, beside = lax.optimization_barrier((packed, beside))
    slab = lax.all_to_all(packed, ("y", "x"), 0, 0)
    slab, mine = lax.optimization_barrier((slab, mine))
    edges = pl.pallas_call(
        split_kernel,
        out_shape=shape((NZ, E_ROWS, 128), bf16),
        in_specs=[smem(), vmem()],
        out_specs=vmem(),
        compiler_params=params(),
        name="split",
    )(at_z, slab)
    slab_other = flip(slab)
    edges = lax.all_to_all(edges, "z", 0, 0)
    theirs = flip(mine)
    back = pl.pallas_call(
        back_kernel,
        out_shape=shape((PIX, C), f32),
        in_specs=[smem()] + [vmem()] * 5 + [hbm()],
        out_specs=vmem(),
        scratch_shapes=[
            pltpu.VMEM((3, (TR + 2) * TC, C), bf16),
            pltpu.VMEM((9, C, C), bf16),
            pltpu.SemaphoreType.DMA((9,)),
        ],
        compiler_params=params(),
        cost_estimate=pl.CostEstimate(flops=2 * PIX * 9 * C * C, bytes_accessed=18 * C * C, transcendentals=0),
        name="back",
    )(at_core, both, cot2, mine, theirs, beside, conv_weight)


    row, da, table, sums = pl.pallas_call(
        sums_kernel,
        out_shape=(shape((8, C), f32), shape((PIX, C), f32), shape((8, 256), f32), shape((2 * PEERS, 8, 128), f32)),
        in_specs=[smem()] + [vmem()] * 6,
        out_specs=(vmem(), vmem(), vmem(), vmem()),
        scratch_shapes=[pltpu.VMEM((16, 128), f32)],
        compiler_params=params(),
        name="sums",
    )(at_y, edges, both, back, gain, shift, bias)
    sums = lax.all_to_all(sums, ("y", "x", "core"), 0, 0)

    terms = pl.pallas_call(
        terms_kernel,
        out_shape=shape((NZ, W_ROWS, 256), bf16),
        in_specs=[smem()] * 2 + [vmem(), hbm(), vmem(), vmem()],
        out_specs=vmem(),
        scratch_shapes=[
            pltpu.VMEM((ROWS * 128, 256), bf16),
            pltpu.VMEM(((ROWS + 2) * 128, 128), bf16),
            pltpu.VMEM((256, (ROWS + 2) * 128), bf16),
            pltpu.VMEM((NZ, 16, 256), f32),
            pltpu.VMEM((PEERS, F_ROWS, 128), bf16),
            pltpu.SemaphoreType.DMA((1,)),
        ],
        compiler_params=params(),
        cost_estimate=pl.CostEstimate(
            flops=2 * PIX * 9 * C * C, bytes_accessed=4 << 20, transcendentals=ROWS * 128 * 256
        ),
        name="terms",
    )(at_core, at_z, slab, slab_other, edges, table)

    joined = pl.pallas_call(
        join_kernel,
        out_shape=shape((NZ, W_ROWS + V_ROWS, 256), bf16),
        in_specs=[vmem()] * 2,
        out_specs=vmem(),
        compiler_params=params(),
        name="join",
    )(sums, terms)
    joined = lax.all_to_all(joined, "z", 0, 0)
    weight_grad = pl.pallas_call(
        gather_kernel,
        out_shape=shape((3, 3, 20, NQ), f32),
        in_specs=[vmem()],
        out_specs=vmem(),
        compiler_params=params(),
        cost_estimate=pl.CostEstimate(flops=1 << 22, bytes_accessed=1 << 20, transcendentals=0),
        name="gather",
    )(joined)
    grad, gain_grad, shift_grad, bias_grad = pl.pallas_call(
        final_kernel,
        out_shape=(shape((PIX, C), bf16),) + (shape((C,), f32),) * 3,
        in_specs=[smem()] + [vmem()] * 6,
        out_specs=(vmem(),) * 4,
        compiler_params=params(),
        name="final",
    )(at_core, joined, flip(joined), both, da, row, gain)
    return grad.reshape(features.shape), weight_grad, gain_grad, shift_grad, bias_grad


def solution(mesh):
    grid = Mesh(mesh.devices.reshape(NZ, NY, NX, 2), ("z", "y", "x", "core"))
    rows, cols = ("z", "y"), ("x", "core")
    tiled = P(rows, cols, None)
    return jax.shard_map(
        body,
        mesh=grid,
        in_specs=(tiled, tiled, P(), P(), P()),
        out_specs=(tiled, P(None, None, rows, cols), P(), P(), P()),
        check_vma=False,
    )
```

```python
import jax
import jax.numpy as jnp
from jax import lax
from jax.experimental import pallas as pl
from jax.experimental.pallas import tpu as pltpu
from jax.sharding import Mesh
from jax.sharding import PartitionSpec as P

C = 640
GW = 40
TR, TC = 8, 16
PIX = TR * TC
NZ, NY, NX = 8, 4, 4
PEERS = NY * NX
ROWS = NY * TR
NQ = 80
CHIP = float(2 * PIX * GW)
TOTAL = float(NZ * PEERS) * CHIP
VMEM_LIMIT = 48 * 1024 * 1024
F_ROWS, C_ROWS, S_ROWS = 160, 160, 16
S_AT = F_ROWS + C_ROWS
G_ROWS = S_AT + S_ROWS
E_ROWS = 96
W_ROWS, V_ROWS = 64, 16
f32, bf16 = jnp.float32, jnp.bfloat16


def lanes(count):
    return lax.broadcasted_iota(jnp.int32, (1, count), 1)


def slab_channel(main, at):
    z = jnp.where(main, at >> 4, at >> 2)
    return z * 80 + jnp.where(main, at & 15, 16 + (at & 3))


def feature_columns():
    lane = lanes(C)
    main = lane < 512
    y = jnp.where(main, lane >> 7, (lane - 512) >> 5)
    return slab_channel(main, jnp.where(main, lane & 127, lane & 31)) + y * 20


def cotangent_columns(core, side):
    lane = lanes(C)
    main = lane < 512
    x = jnp.where(main, lane >> 7, (lane - 512) >> 5)
    at = jnp.where(main, lane & 127, lane & 31)
    q = jnp.where(main, at & 63, 64 + (at & 15))
    mine = jnp.where(main, at >> 6, at >> 4) == side
    return jnp.where(mine, x * 160 + core * NQ + q, -1)


def term_columns(y):
    lane = lanes(256)
    main = lane < 128
    return slab_channel(main, jnp.where(main, lane, lane & 31)) + y * 20


def vmem():
    return pl.BlockSpec(memory_space=pltpu.VMEM)


def smem():
    return pl.BlockSpec(memory_space=pltpu.SMEM)


def hbm():
    return pl.BlockSpec(memory_space=pltpu.HBM)


def fetch(pairs, sem):
    copies = [pltpu.make_async_copy(src, dst, sem.at[k]) for k, (src, dst) in enumerate(pairs)]
    for copy in copies:
        copy.start()
    return copies


def params(**kw):
    return pltpu.CompilerParams(vmem_limit_bytes=VMEM_LIMIT, **kw)


def group_matrix():
    chan = lax.broadcasted_iota(jnp.int32, (C, 128), 0)
    low = lax.broadcasted_iota(jnp.int32, (C, 128), 1) * GW
    return jnp.where((chan >= low) & (chan < low + GW), 1.0, 0.0).astype(bf16)


def exact_dot(value, matrix, over):
    high, middle, low = three(value)
    stacked = jnp.concatenate([high, middle, low, jnp.zeros_like(low)], axis=0).astype(bf16)
    out = lax.dot_general(stacked, matrix, (((1,), (over,)), ((), ())), preferred_element_type=f32)
    return out[0:8] + out[8:16] + out[16:24]


def rows8(row):
    return jnp.broadcast_to(row, (8, row.shape[1]))


def pick(columns):
    rows = lax.broadcasted_iota(jnp.int32, (C, columns.shape[1]), 0)
    return (rows == columns).astype(f32).astype(bf16)


def three(value):
    high = value.astype(bf16).astype(f32)
    rest = value - high
    middle = rest.astype(bf16).astype(f32)
    return high, middle, rest - middle


def lanes32(value, height):
    group = lax.broadcasted_iota(jnp.int32, (height, 128), 1) // 32
    out = []
    for a in range(4):
        acc = jnp.zeros((height, 128), f32)
        for g in range(4):
            moved = pltpu.roll(value[height * g : height * (g + 1)], (32 * (g - a)) % 128, 1)
            acc = jnp.where(group == g, moved, acc)
        out.append(acc)
    return out


def put_pieces(mean, squares):
    pieces = three(mean) + three(squares)
    row = lax.broadcasted_iota(jnp.int32, (S_ROWS, 128), 0)
    out = jnp.zeros((S_ROWS, 128), f32)
    for k in range(6):
        out = jnp.where(row == k, pieces[k], out)
    return out.astype(bf16)


def merge_pieces(got, count):
    got = got.astype(f32)
    return merge(got[:, 0] + got[:, 1] + got[:, 2], got[:, 3] + got[:, 4] + got[:, 5], count)


def in_order(core, own, other):
    a, b = own[...].astype(f32), other[...].astype(f32)
    return jnp.where(core == 0, a, b).astype(bf16), jnp.where(core == 0, b, a).astype(bf16)


def blocks(core, first, second):
    return jnp.dot(first, pick(cotangent_columns(core, 0)), preferred_element_type=f32) + jnp.dot(
        second, pick(cotangent_columns(core, 1)), preferred_element_type=f32
    )


def pack_kernel(core_ref, both_ref, feat2_ref, cot2_ref, out_hbm, bias_ref, out_ref, sem):
    core = core_ref[0]
    feat_ref, cot_ref = both_ref.at[:PIX], both_ref.at[PIX:]
    x, x2 = feat_ref[...].astype(f32), feat2_ref[...].astype(f32)
    groups = group_matrix()
    total = x.sum(0, keepdims=True) + x2.sum(0, keepdims=True)
    mean = exact_dot(rows8(total), groups, 0) / CHIP
    wide = exact_dot(mean, groups, 1)[:1]
    squares = ((x - wide) ** 2).sum(0, keepdims=True) + ((x2 - wide) ** 2).sum(0, keepdims=True)
    stats = put_pieces(mean[:1], exact_dot(rows8(squares), groups, 0)[:1])
    bias_ref[...] = rows8(cot_ref[...].astype(f32).sum(0, keepdims=True))
    moved = jnp.dot(feat_ref[...], pick(feature_columns()), preferred_element_type=f32)
    moved_rest = lanes32(moved[:, 512:], 32)
    for p in range(PEERS):
        y = p // NX
        out_ref[p, 0:128] = moved[:, y * 128 : (y + 1) * 128].astype(bf16)
        out_ref[p, 128:160] = moved_rest[y].astype(bf16)
    copies = fetch(((out_ref.at[:, :F_ROWS, :], out_hbm.at[:, :F_ROWS, :]),), sem.at[0:1])
    first, second = in_order(core, cot_ref, cot2_ref)
    terms = blocks(core, first, second)
    terms_rest = lanes32(terms[:, 512:], 32)
    for p in range(PEERS):
        xx = p % NX
        out_ref[p, 160:288] = terms[:, xx * 128 : (xx + 1) * 128].astype(bf16)
        out_ref[p, 288:320] = terms_rest[xx].astype(bf16)
        out_ref[p, S_AT:] = stats
    copies += fetch(((out_ref.at[:, F_ROWS:, :], out_hbm.at[:, F_ROWS:, :]),), sem.at[1:2])
    for copy in copies:
        copy.wait()


def merge(means, squares, count):
    n = means.shape[0]
    mean = means.sum(0, keepdims=True) / n
    return mean, squares.sum(0, keepdims=True) + count * ((means - mean) ** 2).sum(0, keepdims=True)


def cot_rows(main, rest, g, side):
    lane = lax.broadcasted_iota(jnp.int32, main.shape, 1)
    main = pltpu.roll(main, 64, 1) if side else main
    return jnp.where(lane < 64, main, pltpu.roll(rest, (64 - 32 * g - 16 * side) % 128, 1))


def split_kernel(z_ref, slab_ref, out_ref):
    mean, squares = merge_pieces(slab_ref[:, S_AT:], CHIP)
    stats = put_pieces(mean, squares)
    group = lax.broadcasted_iota(jnp.int32, (TC, 128), 1) // 32
    first, last = jnp.zeros((TC, 128), f32), jnp.zeros((TC, 128), f32)
    for xx in range(NX):
        tail = slab_ref[xx, 288:304].astype(f32)
        first = jnp.where(group == xx, pltpu.roll(tail, 32 * xx, 1) if xx else tail, first)
        tail = slab_ref[(NY - 1) * NX + xx, 304:320].astype(f32)
        last = jnp.where(group == xx, pltpu.roll(tail, (32 * xx + 32) % 128, 1) if xx < 3 else tail, last)
    first, last = first.astype(bf16), last.astype(bf16)
    for p in range(NZ):
        out_ref[p, :S_ROWS] = stats

        @pl.when(z_ref[0] < p)
        def _():
            for xx in range(NX):
                out_ref[p, 16 + 16 * xx : 32 + 16 * xx] = slab_ref[(NY - 1) * NX + xx, 272:288]
            out_ref[p, 80:] = last

        @pl.when(z_ref[0] >= p)
        def _():
            for xx in range(NX):
                out_ref[p, 16 + 16 * xx : 32 + 16 * xx] = slab_ref[xx, 160:176]
            out_ref[p, 80:] = first


def back_kernel(core_ref, both_ref, cot2_ref, mine_ref, theirs_ref, w_hbm, out_ref, shifted, w_ref, sem):
    copies = fetch([(w_hbm.at[t // 3, t % 3], w_ref.at[t]) for t in range(9)], sem)
    rows = (TR + 2) * TC
    lower = core_ref[0] == 0
    mine, theirs = mine_ref[...].astype(f32), theirs_ref[...].astype(f32)
    top, bottom = jnp.where(lower, mine, theirs), jnp.where(lower, theirs, mine)
    own_top, other_top = jnp.where(lower, top[:TC], top[TC:]), jnp.where(lower, top[TC:], top[:TC])
    own_bot, other_bot = jnp.where(lower, bottom[:TC], bottom[TC:]), jnp.where(lower, bottom[TC:], bottom[:TC])
    wide = jnp.concatenate([own_top, both_ref[PIX:].astype(f32), own_bot], axis=0)
    near = jnp.concatenate([other_top, cot2_ref[...].astype(f32), other_bot], axis=0)
    near = near.reshape(TR + 2, TC, C)
    inner = jnp.where(lower, near[:, :1], near[:, TC - 1 :])
    left, right = jnp.where(lower, 0.0, inner), jnp.where(lower, inner, 0.0)
    left = jnp.broadcast_to(left, (TR + 2, TC, C)).reshape(rows, C)
    right = jnp.broadcast_to(right, (TR + 2, TC, C)).reshape(rows, C)
    col = lax.broadcasted_iota(jnp.int32, (rows, C), 0) % TC
    shifted[0] = jnp.where(col == 0, left, pltpu.roll(wide, 1, 0)).astype(bf16)
    shifted[1] = wide.astype(bf16)
    shifted[2] = jnp.where(col == TC - 1, right, pltpu.roll(wide, rows - 1, 0)).astype(bf16)
    total = jnp.zeros((C, PIX), f32)
    for t in range(9):
        i, j = t // 3, t % 3
        copies[t].wait()
        pixels = shifted[2 - j, (2 - i) * TC : (2 - i) * TC + PIX]
        total = total + lax.dot_general(
            w_ref[t], pixels, (((1,), (1,)), ((), ())), preferred_element_type=f32
        )
    out_ref[...] = total.T


def side_kernel(core_ref, both_ref, mine_ref, theirs_ref, w_hbm, out_ref, w_ref, sem):
    j = 2 * core_ref[0]
    copies = fetch([(w_hbm.at[i, j], w_ref.at[i]) for i in range(3)], sem)
    lower = core_ref[0] == 0
    tile = both_ref[PIX:].astype(f32).reshape(TR, TC, C)
    tile = jnp.where(lower, tile[:, :1], tile[:, TC - 1 :])
    mine, theirs = mine_ref[...].astype(f32), theirs_ref[...].astype(f32)
    mine = jnp.where(lower, mine[:1], mine[2 * TC - 1 :])
    theirs = jnp.where(lower, theirs[:1], theirs[2 * TC - 1 :])
    top, bottom = jnp.where(lower, mine, theirs), jnp.where(lower, theirs, mine)
    column = jnp.concatenate([top[None], tile, bottom[None]], axis=0)
    total = jnp.zeros((TR, C), f32)
    for i in range(3):
        copies[i].wait()
        pixels = column[2 - i : 2 - i + TR].reshape(TR, C).astype(bf16)
        total = total + lax.dot_general(
            pixels, w_ref[i], (((1,), (1,)), ((), ())), preferred_element_type=f32
        )
    out_ref[...] = total


def sums_kernel(core_ref, y_ref, stat_ref, both_ref, back_ref, side_ref, gain_ref, shift_ref, bias_ref,
                row_ref, da_ref, par_ref, out_ref, block):
    mean, squares = merge_pieces(stat_ref[:, :S_ROWS], PEERS * CHIP)
    groups = group_matrix()
    both = jnp.concatenate([mean, lax.rsqrt(squares / TOTAL + 1e-05), jnp.zeros((6, 128), f32)], axis=0)
    both = exact_dot(both, groups, 1)
    mean, rstd = both[0:1], both[1:2]
    gain, shift = gain_ref[...], shift_ref[...]
    row = lax.broadcasted_iota(jnp.int32, (8, C), 0)
    row_ref[...] = jnp.where(row == 0, mean, rstd)
    table = jnp.where(row == 0, mean, jnp.where(row == 1, rstd * gain, jnp.where(row == 2, shift, 0.0)))
    par_ref[...] = exact_dot(table, pick(term_columns(y_ref[0])), 0)
    xhat = (both_ref[:PIX].astype(f32) - mean) * rstd
    act = xhat * gain + shift
    sig = jax.nn.sigmoid(act)
    column = lax.broadcasted_iota(jnp.int32, (TR, TC, C), 1)
    side = jnp.broadcast_to(side_ref[...][:, None, :], (TR, TC, C))
    side = jnp.where(column == core_ref[0] * (TC - 1), side, 0.0).reshape(PIX, C)
    da = (back_ref[...] + side) * sig * (1.0 + act * (1.0 - sig))
    da_ref[...] = da
    sums = (da.sum(0, keepdims=True), (da * xhat).sum(0, keepdims=True), bias_ref[:1])
    block[...] = jnp.zeros_like(block)
    for s in range(3):
        for t in range(5):
            block[5 * s + t : 5 * s + t + 1] = sums[s][:, 128 * t : 128 * t + 128]
    for p in range(2 * PEERS):
        out_ref[p] = block[8 * (p % 2) : 8 * (p % 2) + 8]


def terms_kernel(core_ref, z_ref, own_ref, other_hbm, edge_ref, par_ref, out_ref,
                 hid, strips, cot3, rest, other_ref, sem):
    copies = fetch(((other_hbm.at[:, :F_ROWS, :], other_ref),), sem)
    core = core_ref[0]

    def put(block, peer, side):
        y, xx = peer // NX, peer % NX

        def silu(x, lanes):
            a = (x.astype(f32) - par_ref[0:1, lanes]) * par_ref[1:2, lanes] + par_ref[2:3, lanes]
            return a * jax.nn.sigmoid(a)

        main = silu(block[:128], slice(0, 128)).astype(bf16)
        tail = silu(block[128:], slice(128, 256))
        for g in range(4):
            low = pltpu.roll(tail, (128 - 32 * g) % 128, 1).astype(bf16)
            for h in range(2):
                r = 2 * g + h
                at = pl.ds(pl.multiple_of((y * TR + r) * 128 + xx * 32 + side * TC, TC), TC)
                hid[at, 0:128] = main[r * TC : (r + 1) * TC]
                hid[at, 128:256] = low[h * TC : (h + 1) * TC]

    for peer in range(PEERS):
        put(own_ref[peer, :F_ROWS], peer, core)
        y, xx = peer // NX, peer % NX
        tail = own_ref[peer, 288:320].astype(f32)
        for g in range(4):
            main = own_ref[peer, 160 + 32 * g : 192 + 32 * g].astype(f32)
            for side in range(2):
                value = cot_rows(main, tail, g, side).astype(bf16)
                for h in range(2):
                    at = (y * TR + 2 * g + h + 1) * 128 + xx * 32 + side * TC
                    strips[at : at + TC] = value[h * TC : (h + 1) * TC]
    copies[0].wait()
    for peer in range(PEERS):
        put(other_ref[peer], peer, 1 - core)
    z = z_ref[0]
    for start, peer, there in ((0, jnp.maximum(z - 1, 0), z > 0),
                               ((ROWS + 1) * 128, jnp.minimum(z + 1, NZ - 1), z < NZ - 1)):
        got = jnp.where(there, edge_ref[peer].astype(f32), 0.0)
        for xx in range(NX):
            for side in range(2):
                at = start + xx * 32 + side * TC
                value = cot_rows(got[16 + 16 * xx : 32 + 16 * xx], got[80:], xx, side)
                strips[at : at + TC] = value.astype(bf16)
    lane = lax.broadcasted_iota(jnp.int32, (NQ, 128), 1)
    for row in range(ROWS + 2):
        at = slice(row * 128, (row + 1) * 128)
        turned = strips[at].astype(f32).T[:NQ]
        before = jnp.where(lane == 0, 0.0, pltpu.roll(turned, 1, 1))
        after = jnp.where(lane == 127, 0.0, pltpu.roll(turned, 127, 1))
        cot3[0:NQ, at] = after.astype(bf16)
        cot3[NQ : 2 * NQ, at] = turned.astype(bf16)
        cot3[2 * NQ : 3 * NQ, at] = before.astype(bf16)
    cot3[3 * NQ :] = jnp.zeros((16, (ROWS + 2) * 128), bf16)
    rest[...] = jnp.zeros_like(rest)
    for i in range(3):
        lhs = cot3[:, (2 - i) * 128 : (2 - i) * 128 + ROWS * 128]
        turned = jnp.dot(lhs, hid[...], preferred_element_type=f32).T
        for z in range(NZ):
            out_ref[z, 16 * i : 16 * i + 16] = turned[16 * z : 16 * z + 16].astype(bf16)
            rest[z, 4 * i : 4 * i + 4] = turned[128 + 4 * z : 132 + 4 * z]
    for z in range(NZ):
        out_ref[z, 48:64] = rest[z].astype(bf16)


def join_kernel(sums_ref, terms_ref, out_ref):
    value = sums_ref[0]
    for p in range(1, 2 * PEERS):
        value = value + sums_ref[p]
    high, middle, low = three(value)
    block = jnp.concatenate(
        [jnp.concatenate([high, middle], axis=1), jnp.concatenate([low, jnp.zeros_like(low)], axis=1)], axis=0
    ).astype(bf16)
    for z in range(NZ):
        out_ref[z, :W_ROWS] = terms_ref[z]
        out_ref[z, W_ROWS:] = block


def final_kernel(core_ref, got_ref, other_ref, both_ref, da_ref, row_ref, gain_ref,
                 grad_ref, gain_grad_ref, shift_grad_ref, bias_ref):

    def half(ref):
        total = jnp.zeros((8, 128), f32)
        for z in range(NZ):
            part = ref[z, W_ROWS:].astype(f32)
            total = total + (part[:8, :128] + part[:8, 128:] + part[8:, :128])
        return total

    own, other = half(got_ref), half(other_ref)
    lower = core_ref[0] == 0
    total = jnp.concatenate([jnp.where(lower, own, other), jnp.where(lower, other, own)], axis=0)
    sums = [jnp.concatenate([total[5 * s + t : 5 * s + t + 1] for t in range(5)], axis=1) for s in range(3)]
    shift_grad_ref[...], gain_grad_ref[...], bias_ref[...] = [value.reshape(C) for value in sums]
    groups = group_matrix()
    gain, mean, rstd = gain_ref[...], row_ref[0:1], row_ref[1:2]

    both = jnp.concatenate([gain * sums[0], gain * sums[1], jnp.zeros((6, C), f32)], axis=0)
    both = exact_dot(exact_dot(both, groups, 0), groups, 1) / TOTAL
    first, second = both[0:1], both[1:2]
    xhat = (both_ref[:PIX].astype(f32) - mean) * rstd
    grad_ref[...] = (rstd * (da_ref[...] * gain - first - xhat * second)).astype(bf16)


def gather_kernel(got_ref, weight_ref):
    weight = got_ref[0, :W_ROWS].astype(f32)
    for z in range(1, NZ):
        weight = weight + got_ref[z, :W_ROWS].astype(f32)
    for i in range(3):
        for j in range(3):
            at = slice(j * NQ, (j + 1) * NQ)
            weight_ref[i, j, 0:16] = weight[16 * i : 16 * i + 16, at]
            weight_ref[i, j, 16:20] = weight[48 + 4 * i : 52 + 4 * i, at]


def flip(value):
    return lax.ppermute(value, "core", [(0, 1), (1, 0)])


def shape(dims, dtype):
    return jax.ShapeDtypeStruct(dims, dtype)


def body(features, cotangent, conv_weight, gain, shift):
    core, y, z = lax.axis_index("core"), lax.axis_index("y"), lax.axis_index("z")
    at_core, at_y, at_z = core.reshape(1), y.reshape(1), z.reshape(1)
    feat, cot = features.reshape(PIX, C), cotangent.reshape(PIX, C)
    gain, shift = gain.reshape(1, C), shift.reshape(1, C)
    cot2, feat2 = flip(cot), flip(feat)
    both = jnp.concatenate([feat, cot])
    edge = jnp.where(
        core == 0,
        jnp.concatenate([cot[PIX - TC :], cot2[PIX - TC :]]),
        jnp.concatenate([cot2[:TC], cot[:TC]]),
    )
    count = NZ * NY
    ways = [(2 * k, 2 * k + 2) for k in range(count - 1)] + [(2 * k + 3, 2 * k + 1) for k in range(count - 1)]
    mine = lax.ppermute(edge, ("z", "y", "core"), ways)

    packed, bias = pl.pallas_call(
        pack_kernel,
        out_shape=(shape((PEERS, G_ROWS, 128), bf16), shape((8, C), f32)),
        in_specs=[smem()] + [vmem()] * 3,
        out_specs=(hbm(), vmem()),
        scratch_shapes=[pltpu.VMEM((PEERS, G_ROWS, 128), bf16), pltpu.SemaphoreType.DMA((2,))],
        compiler_params=params(),
        cost_estimate=pl.CostEstimate(flops=1 << 28, bytes_accessed=2 << 20, transcendentals=0),
        name="pack",
    )(at_core, both, feat2, cot2)
    slab = lax.all_to_all(packed, ("y", "x"), 0, 0)
    theirs = flip(mine)
    side = pl.pallas_call(
        side_kernel,
        out_shape=shape((TR, C), f32),
        in_specs=[smem()] + [vmem()] * 3 + [hbm()],
        out_specs=vmem(),
        scratch_shapes=[pltpu.VMEM((3, C, C), bf16), pltpu.SemaphoreType.DMA((3,))],
        compiler_params=params(),
        name="side",
    )(at_core, both, mine, theirs, conv_weight)
    slab, side = lax.optimization_barrier((slab, side))
    pairs = [(2 * k + 1, 2 * k + 2) for k in range(NX - 1)]
    side = lax.ppermute(side, ("x", "core"), pairs + [(b, a) for a, b in pairs])
    edges = pl.pallas_call(
        split_kernel,
        out_shape=shape((NZ, E_ROWS, 128), bf16),
        in_specs=[smem(), vmem()],
        out_specs=vmem(),
        compiler_params=params(),
        name="split",
    )(at_z, slab)
    slab_other = flip(slab)
    edges = lax.all_to_all(edges, "z", 0, 0)
    back = pl.pallas_call(
        back_kernel,
        out_shape=shape((PIX, C), f32),
        in_specs=[smem()] + [vmem()] * 4 + [hbm()],
        out_specs=vmem(),
        scratch_shapes=[
            pltpu.VMEM((3, (TR + 2) * TC, C), bf16),
            pltpu.VMEM((9, C, C), bf16),
            pltpu.SemaphoreType.DMA((9,)),
        ],
        compiler_params=params(),
        cost_estimate=pl.CostEstimate(flops=2 * PIX * 9 * C * C, bytes_accessed=18 * C * C, transcendentals=0),
        name="back",
    )(at_core, both, cot2, mine, theirs, conv_weight)


    row, da, table, sums = pl.pallas_call(
        sums_kernel,
        out_shape=(shape((8, C), f32), shape((PIX, C), f32), shape((8, 256), f32), shape((2 * PEERS, 8, 128), f32)),
        in_specs=[smem()] * 2 + [vmem()] * 7,
        out_specs=(vmem(), vmem(), vmem(), vmem()),
        scratch_shapes=[pltpu.VMEM((16, 128), f32)],
        compiler_params=params(),
        name="sums",
    )(at_core, at_y, edges, both, back, side, gain, shift, bias)
    sums = lax.all_to_all(sums, ("y", "x", "core"), 0, 0)

    terms = pl.pallas_call(
        terms_kernel,
        out_shape=shape((NZ, W_ROWS, 256), bf16),
        in_specs=[smem()] * 2 + [vmem(), hbm(), vmem(), vmem()],
        out_specs=vmem(),
        scratch_shapes=[
            pltpu.VMEM((ROWS * 128, 256), bf16),
            pltpu.VMEM(((ROWS + 2) * 128, 128), bf16),
            pltpu.VMEM((256, (ROWS + 2) * 128), bf16),
            pltpu.VMEM((NZ, 16, 256), f32),
            pltpu.VMEM((PEERS, F_ROWS, 128), bf16),
            pltpu.SemaphoreType.DMA((1,)),
        ],
        compiler_params=params(),
        cost_estimate=pl.CostEstimate(
            flops=2 * PIX * 9 * C * C, bytes_accessed=4 << 20, transcendentals=ROWS * 128 * 256
        ),
        name="terms",
    )(at_core, at_z, slab, slab_other, edges, table)

    joined = pl.pallas_call(
        join_kernel,
        out_shape=shape((NZ, W_ROWS + V_ROWS, 256), bf16),
        in_specs=[vmem()] * 2,
        out_specs=vmem(),
        compiler_params=params(),
        name="join",
    )(sums, terms)
    joined = lax.all_to_all(joined, "z", 0, 0)
    weight_grad = pl.pallas_call(
        gather_kernel,
        out_shape=shape((3, 3, 20, NQ), f32),
        in_specs=[vmem()],
        out_specs=vmem(),
        compiler_params=params(),
        cost_estimate=pl.CostEstimate(flops=1 << 22, bytes_accessed=1 << 20, transcendentals=0),
        name="gather",
    )(joined)
    grad, gain_grad, shift_grad, bias_grad = pl.pallas_call(
        final_kernel,
        out_shape=(shape((PIX, C), bf16),) + (shape((C,), f32),) * 3,
        in_specs=[smem()] + [vmem()] * 6,
        out_specs=(vmem(),) * 4,
        compiler_params=params(),
        name="final",
    )(at_core, joined, flip(joined), both, da, row, gain)
    return grad.reshape(features.shape), weight_grad, gain_grad, shift_grad, bias_grad


def solution(mesh):
    grid = Mesh(mesh.devices.reshape(NZ, NY, NX, 2), ("z", "y", "x", "core"))
    rows, cols = ("z", "y"), ("x", "core")
    tiled = P(rows, cols, None)
    return jax.shard_map(
        body,
        mesh=grid,
        in_specs=(tiled, tiled, P(), P(), P()),
        out_specs=(tiled, P(None, None, rows, cols), P(), P(), P()),
        check_vma=False,
    )
```

```python
import jax
import jax.numpy as jnp
from jax import lax
from jax.experimental import pallas as pl
from jax.experimental.pallas import tpu as pltpu
from jax.sharding import Mesh
from jax.sharding import PartitionSpec as P

C = 640
GW = 40
TR, TC = 8, 16
PIX = TR * TC
NZ, NY, NX = 8, 4, 4
PEERS = NY * NX
ROWS = NY * TR
NQ = 80
CHIP = float(2 * PIX * GW)
TOTAL = float(NZ * PEERS) * CHIP
VMEM_LIMIT = 48 * 1024 * 1024
F_ROWS, C_ROWS, S_ROWS = 160, 160, 16
S_AT = F_ROWS + C_ROWS
G_ROWS = S_AT + S_ROWS
E_ROWS = 96
W_ROWS = 64
f32, bf16 = jnp.float32, jnp.bfloat16


def lanes(count):
    return lax.broadcasted_iota(jnp.int32, (1, count), 1)


def slab_channel(main, at):
    z = jnp.where(main, at >> 4, at >> 2)
    return z * 80 + jnp.where(main, at & 15, 16 + (at & 3))


def feature_columns():
    lane = lanes(C)
    main = lane < 512
    y = jnp.where(main, lane >> 7, (lane - 512) >> 5)
    return slab_channel(main, jnp.where(main, lane & 127, lane & 31)) + y * 20


def cotangent_columns(core, side):
    lane = lanes(C)
    main = lane < 512
    x = jnp.where(main, lane >> 7, (lane - 512) >> 5)
    at = jnp.where(main, lane & 127, lane & 31)
    q = jnp.where(main, at & 63, 64 + (at & 15))
    mine = jnp.where(main, at >> 6, at >> 4) == side
    return jnp.where(mine, x * 160 + core * NQ + q, -1)


def term_columns(y):
    lane = lanes(256)
    main = lane < 128
    return slab_channel(main, jnp.where(main, lane, lane & 31)) + y * 20


def vmem():
    return pl.BlockSpec(memory_space=pltpu.VMEM)


def smem():
    return pl.BlockSpec(memory_space=pltpu.SMEM)


def hbm():
    return pl.BlockSpec(memory_space=pltpu.HBM)


def fetch(pairs, sem):
    copies = [pltpu.make_async_copy(src, dst, sem.at[k]) for k, (src, dst) in enumerate(pairs)]
    for copy in copies:
        copy.start()
    return copies


def params(**kw):
    return pltpu.CompilerParams(vmem_limit_bytes=VMEM_LIMIT, **kw)


def group_matrix():
    chan = lax.broadcasted_iota(jnp.int32, (C, 128), 0)
    low = lax.broadcasted_iota(jnp.int32, (C, 128), 1) * GW
    return jnp.where((chan >= low) & (chan < low + GW), 1.0, 0.0).astype(bf16)


def exact_dot(value, matrix, over):
    high, middle, low = three(value)
    stacked = jnp.concatenate([high, middle, low, jnp.zeros_like(low)], axis=0).astype(bf16)
    out = lax.dot_general(stacked, matrix, (((1,), (over,)), ((), ())), preferred_element_type=f32)
    return out[0:8] + out[8:16] + out[16:24]


def rows8(row):
    return jnp.broadcast_to(row, (8, row.shape[1]))


def pick(columns):
    rows = lax.broadcasted_iota(jnp.int32, (C, columns.shape[1]), 0)
    return (rows == columns).astype(f32).astype(bf16)


def sigmoid(value):
    return 0.5 * jnp.tanh(0.5 * value) + 0.5


def fold(row):
    return jnp.concatenate([row[:, 128 * t : 128 * t + 128] for t in range(5)], axis=0)


def unfold(rows):
    return jnp.concatenate([rows[t : t + 1] for t in range(5)], axis=1)


def three(value):
    high = value.astype(bf16).astype(f32)
    rest = value - high
    middle = rest.astype(bf16).astype(f32)
    return high, middle, rest - middle


def lanes32(value, height):
    group = lax.broadcasted_iota(jnp.int32, (height, 128), 1) // 32
    out = []
    for a in range(4):
        acc = jnp.zeros((height, 128), f32)
        for g in range(4):
            moved = pltpu.roll(value[height * g : height * (g + 1)], (32 * (g - a)) % 128, 1)
            acc = jnp.where(group == g, moved, acc)
        out.append(acc)
    return out


def put_pieces(mean, squares, bias):
    high, middle, _ = three(bias)
    rows = three(mean) + three(squares) + (high, middle)
    return jnp.concatenate(list(rows), axis=0).astype(bf16)


def merge_pieces(got, count):
    got = got.astype(f32)
    mean, squares = merge(got[:, 0] + got[:, 1] + got[:, 2], got[:, 3] + got[:, 4] + got[:, 5], count)
    total = got[0]
    for p in range(1, got.shape[0]):
        total = total + got[p]
    return mean, squares, total[6:11] + total[11:16]


def in_order(core, own, other):
    a, b = own[...].astype(f32), other[...].astype(f32)
    return jnp.where(core == 0, a, b).astype(bf16), jnp.where(core == 0, b, a).astype(bf16)


def blocks(core, first, second):
    return jnp.dot(first, pick(cotangent_columns(core, 0)), preferred_element_type=f32) + jnp.dot(
        second, pick(cotangent_columns(core, 1)), preferred_element_type=f32
    )


def pack_kernel(core_ref, both_ref, feat2_ref, cot2_ref, out_hbm, out_ref, sem):
    core = core_ref[0]
    feat_ref, cot_ref = both_ref.at[:PIX], both_ref.at[PIX:]
    x, x2 = feat_ref[...].astype(f32), feat2_ref[...].astype(f32)
    groups = group_matrix()
    total = x.sum(0, keepdims=True) + x2.sum(0, keepdims=True)
    mean = exact_dot(rows8(total), groups, 0) / CHIP
    wide = exact_dot(mean, groups, 1)[:1]
    squares = ((x - wide) ** 2).sum(0, keepdims=True) + ((x2 - wide) ** 2).sum(0, keepdims=True)
    bias = cot_ref[...].astype(f32).sum(0, keepdims=True) + cot2_ref[...].astype(f32).sum(0, keepdims=True)
    stats = put_pieces(mean[:1], exact_dot(rows8(squares), groups, 0)[:1], fold(bias))
    moved = jnp.dot(feat_ref[...], pick(feature_columns()), preferred_element_type=f32)
    moved_rest = lanes32(moved[:, 512:], 32)
    for p in range(PEERS):
        y = p // NX
        out_ref[p, 0:128] = moved[:, y * 128 : (y + 1) * 128].astype(bf16)
        out_ref[p, 128:160] = moved_rest[y].astype(bf16)
    copies = fetch(((out_ref.at[:, :F_ROWS, :], out_hbm.at[:, :F_ROWS, :]),), sem.at[0:1])
    first, second = in_order(core, cot_ref, cot2_ref)
    terms = blocks(core, first, second)
    terms_rest = lanes32(terms[:, 512:], 32)
    for p in range(PEERS):
        xx = p % NX
        out_ref[p, 160:288] = terms[:, xx * 128 : (xx + 1) * 128].astype(bf16)
        out_ref[p, 288:320] = terms_rest[xx].astype(bf16)
        out_ref[p, S_AT:] = stats
    copies += fetch(((out_ref.at[:, F_ROWS:, :], out_hbm.at[:, F_ROWS:, :]),), sem.at[1:2])
    for copy in copies:
        copy.wait()


def merge(means, squares, count):
    n = means.shape[0]
    mean = means.sum(0, keepdims=True) / n
    return mean, squares.sum(0, keepdims=True) + count * ((means - mean) ** 2).sum(0, keepdims=True)


def cot_rows(main, rest, g, side):
    lane = lax.broadcasted_iota(jnp.int32, main.shape, 1)
    main = pltpu.roll(main, 64, 1) if side else main
    return jnp.where(lane < 64, main, pltpu.roll(rest, (64 - 32 * g - 16 * side) % 128, 1))


def split_kernel(z_ref, slab_ref, out_ref):
    stats = put_pieces(*merge_pieces(slab_ref[:, S_AT:], CHIP))
    group = lax.broadcasted_iota(jnp.int32, (TC, 128), 1) // 32
    first, last = jnp.zeros((TC, 128), f32), jnp.zeros((TC, 128), f32)
    for xx in range(NX):
        tail = slab_ref[xx, 288:304].astype(f32)
        first = jnp.where(group == xx, pltpu.roll(tail, 32 * xx, 1) if xx else tail, first)
        tail = slab_ref[(NY - 1) * NX + xx, 304:320].astype(f32)
        last = jnp.where(group == xx, pltpu.roll(tail, (32 * xx + 32) % 128, 1) if xx < 3 else tail, last)
    first, last = first.astype(bf16), last.astype(bf16)
    for p in range(NZ):
        out_ref[p, :S_ROWS] = stats

        @pl.when(z_ref[0] < p)
        def _():
            for xx in range(NX):
                out_ref[p, 16 + 16 * xx : 32 + 16 * xx] = slab_ref[(NY - 1) * NX + xx, 272:288]
            out_ref[p, 80:] = last

        @pl.when(z_ref[0] >= p)
        def _():
            for xx in range(NX):
                out_ref[p, 16 + 16 * xx : 32 + 16 * xx] = slab_ref[xx, 160:176]
            out_ref[p, 80:] = first


def back_kernel(core_ref, both_ref, cot2_ref, mine_ref, theirs_ref, w_hbm, out_ref, shifted, w_ref, sem):
    copies = fetch([(w_hbm.at[t // 3, t % 3], w_ref.at[t]) for t in range(9)], sem)
    rows = (TR + 2) * TC
    lower = core_ref[0] == 0
    mine, theirs = mine_ref[...].astype(f32), theirs_ref[...].astype(f32)
    top, bottom = jnp.where(lower, mine, theirs), jnp.where(lower, theirs, mine)
    own_top, other_top = jnp.where(lower, top[:TC], top[TC:]), jnp.where(lower, top[TC:], top[:TC])
    own_bot, other_bot = jnp.where(lower, bottom[:TC], bottom[TC:]), jnp.where(lower, bottom[TC:], bottom[:TC])
    wide = jnp.concatenate([own_top, both_ref[PIX:].astype(f32), own_bot], axis=0)
    near = jnp.concatenate([other_top, cot2_ref[...].astype(f32), other_bot], axis=0)
    near = near.reshape(TR + 2, TC, C)
    inner = jnp.where(lower, near[:, :1], near[:, TC - 1 :])
    left, right = jnp.where(lower, 0.0, inner), jnp.where(lower, inner, 0.0)
    left = jnp.broadcast_to(left, (TR + 2, TC, C)).reshape(rows, C)
    right = jnp.broadcast_to(right, (TR + 2, TC, C)).reshape(rows, C)
    col = lax.broadcasted_iota(jnp.int32, (rows, C), 0) % TC
    shifted[0] = jnp.where(col == 0, left, pltpu.roll(wide, 1, 0)).astype(bf16)
    shifted[1] = wide.astype(bf16)
    shifted[2] = jnp.where(col == TC - 1, right, pltpu.roll(wide, rows - 1, 0)).astype(bf16)
    total = jnp.zeros((C, PIX), f32)
    for t in range(9):
        i, j = t // 3, t % 3
        copies[t].wait()
        pixels = shifted[2 - j, (2 - i) * TC : (2 - i) * TC + PIX]
        total = total + lax.dot_general(
            w_ref[t], pixels, (((1,), (1,)), ((), ())), preferred_element_type=f32
        )
    out_ref[...] = total.T


def side_kernel(core_ref, both_ref, mine_ref, theirs_ref, w_hbm, out_ref, w_ref, sem):
    j = 2 * core_ref[0]
    copies = fetch([(w_hbm.at[i, j], w_ref.at[i]) for i in range(3)], sem)
    lower = core_ref[0] == 0
    tile = both_ref[PIX:].astype(f32).reshape(TR, TC, C)
    tile = jnp.where(lower, tile[:, :1], tile[:, TC - 1 :])
    mine, theirs = mine_ref[...].astype(f32), theirs_ref[...].astype(f32)
    mine = jnp.where(lower, mine[:1], mine[2 * TC - 1 :])
    theirs = jnp.where(lower, theirs[:1], theirs[2 * TC - 1 :])
    top, bottom = jnp.where(lower, mine, theirs), jnp.where(lower, theirs, mine)
    column = jnp.concatenate([top[None], tile, bottom[None]], axis=0)
    total = jnp.zeros((TR, C), f32)
    for i in range(3):
        copies[i].wait()
        pixels = column[2 - i : 2 - i + TR].reshape(TR, C).astype(bf16)
        total = total + lax.dot_general(
            pixels, w_ref[i], (((1,), (1,)), ((), ())), preferred_element_type=f32
        )
    out_ref[...] = total


def sums_kernel(core_ref, y_ref, stat_ref, both_ref, back_ref, side_ref, gain_ref, shift_ref,
                row_ref, da_ref, par_ref, out_ref, bias_ref):
    mean, squares, bias = merge_pieces(stat_ref[:, :S_ROWS], PEERS * CHIP)
    bias_ref[...] = unfold(bias).reshape(C)
    groups = group_matrix()
    both = jnp.concatenate([mean, lax.rsqrt(squares / TOTAL + 1e-05), jnp.zeros((6, 128), f32)], axis=0)
    both = exact_dot(both, groups, 1)
    mean, rstd = both[0:1], both[1:2]
    gain, shift = gain_ref[...], shift_ref[...]
    row = lax.broadcasted_iota(jnp.int32, (8, C), 0)
    row_ref[...] = jnp.where(row == 0, mean, rstd)
    table = jnp.where(row == 0, mean, jnp.where(row == 1, rstd * gain, jnp.where(row == 2, shift, 0.0)))
    par_ref[...] = exact_dot(table, pick(term_columns(y_ref[0])), 0)
    xhat = (both_ref[:PIX].astype(f32) - mean) * rstd
    act = xhat * gain + shift
    sig = sigmoid(act)
    column = lax.broadcasted_iota(jnp.int32, (TR, TC, C), 1)
    side = jnp.broadcast_to(side_ref[...][:, None, :], (TR, TC, C))
    side = jnp.where(column == core_ref[0] * (TC - 1), side, 0.0).reshape(PIX, C)
    da = (back_ref[...] + side) * sig * (1.0 + act * (1.0 - sig))
    da_ref[...] = da
    empty = jnp.zeros((3, 128), f32)
    for side, value in enumerate((da, da * xhat)):
        block = jnp.concatenate([fold(value.sum(0, keepdims=True)), empty], axis=0)
        for p in range(side, 2 * PEERS, 2):
            out_ref[p] = block


def terms_kernel(core_ref, z_ref, own_ref, other_hbm, edge_ref, par_ref, out_ref,
                 hid, strips, cot3, rest, other_ref, sem):
    copies = fetch(((other_hbm.at[:, :F_ROWS, :], other_ref),), sem)
    core = core_ref[0]

    def put(block, peer, side):
        y, xx = peer // NX, peer % NX

        def silu(x, lanes):
            a = (x.astype(f32) - par_ref[0:1, lanes]) * par_ref[1:2, lanes] + par_ref[2:3, lanes]
            return a * sigmoid(a)

        main = silu(block[:128], slice(0, 128)).astype(bf16)
        tail = silu(block[128:], slice(128, 256))
        for g in range(4):
            low = pltpu.roll(tail, (128 - 32 * g) % 128, 1).astype(bf16)
            for h in range(2):
                r = 2 * g + h
                at = pl.ds(pl.multiple_of((y * TR + r) * 128 + xx * 32 + side * TC, TC), TC)
                hid[at, 0:128] = main[r * TC : (r + 1) * TC]
                hid[at, 128:256] = low[h * TC : (h + 1) * TC]

    for peer in range(PEERS):
        put(own_ref[peer, :F_ROWS], peer, core)
        y, xx = peer // NX, peer % NX
        tail = own_ref[peer, 288:320].astype(f32)
        for g in range(4):
            main = own_ref[peer, 160 + 32 * g : 192 + 32 * g].astype(f32)
            for side in range(2):
                value = cot_rows(main, tail, g, side).astype(bf16)
                for h in range(2):
                    at = (y * TR + 2 * g + h + 1) * 128 + xx * 32 + side * TC
                    strips[at : at + TC] = value[h * TC : (h + 1) * TC]
    copies[0].wait()
    for peer in range(PEERS):
        put(other_ref[peer], peer, 1 - core)
    z = z_ref[0]
    for start, peer, there in ((0, jnp.maximum(z - 1, 0), z > 0),
                               ((ROWS + 1) * 128, jnp.minimum(z + 1, NZ - 1), z < NZ - 1)):
        got = jnp.where(there, edge_ref[peer].astype(f32), 0.0)
        for xx in range(NX):
            for side in range(2):
                at = start + xx * 32 + side * TC
                value = cot_rows(got[16 + 16 * xx : 32 + 16 * xx], got[80:], xx, side)
                strips[at : at + TC] = value.astype(bf16)
    lane = lax.broadcasted_iota(jnp.int32, (NQ, 128), 1)
    for row in range(ROWS + 2):
        at = slice(row * 128, (row + 1) * 128)
        turned = strips[at].astype(f32).T[:NQ]
        before = jnp.where(lane == 0, 0.0, pltpu.roll(turned, 1, 1))
        after = jnp.where(lane == 127, 0.0, pltpu.roll(turned, 127, 1))
        cot3[0:NQ, at] = after.astype(bf16)
        cot3[NQ : 2 * NQ, at] = turned.astype(bf16)
        cot3[2 * NQ : 3 * NQ, at] = before.astype(bf16)
    cot3[3 * NQ :] = jnp.zeros((16, (ROWS + 2) * 128), bf16)
    rest[...] = jnp.zeros_like(rest)
    for i in range(3):
        lhs = cot3[:, (2 - i) * 128 : (2 - i) * 128 + ROWS * 128]
        turned = jnp.dot(lhs, hid[...], preferred_element_type=f32).T
        for z in range(NZ):
            out_ref[z, 16 * i : 16 * i + 16] = turned[16 * z : 16 * z + 16].astype(bf16)
            rest[z, 4 * i : 4 * i + 4] = turned[128 + 4 * z : 132 + 4 * z]
    for z in range(NZ):
        out_ref[z, 48:64] = rest[z].astype(bf16)


def join_kernel(sums_ref, terms_ref, out_ref):
    value = sums_ref[0]
    for p in range(1, 2 * PEERS):
        value = value + sums_ref[p]
    high, middle, _ = three(value)
    lane = lax.broadcasted_iota(jnp.int32, (16, 128), 1)
    row = lax.broadcasted_iota(jnp.int32, (16, 128), 0)
    tails = [
        jnp.concatenate([pltpu.roll(middle, (112 - 16 * c) % 128, 1) for c in (2 * k, 2 * k + 1)], axis=0)
        for k in range(4)
    ]
    for z in range(NZ):
        for k in range(4):
            at = slice(16 * k, 16 * k + 16)
            block = terms_ref[z, at].astype(f32)
            left, right = block[:, :128], block[:, 128:]
            right = jnp.where(lane >= 112, tails[k], right)
            if k == 3:
                left = jnp.concatenate([left[:12], high[:4]], axis=0)
                right = jnp.where(row == 13, high[4:5], right)
            out_ref[z, at] = jnp.concatenate([left, right], axis=1).astype(bf16)


def final_kernel(core_ref, got_ref, other_ref, both_ref, da_ref, row_ref, gain_ref,
                 grad_ref, gain_grad_ref, shift_grad_ref):
    lane = lax.broadcasted_iota(jnp.int32, (8, 128), 1)

    def total(ref):
        out = ref[0].astype(f32)
        for z in range(1, NZ):
            out = out + ref[z].astype(f32)
        high = jnp.concatenate([out[60:64, :128], out[61:62, 128:]], axis=0)
        middle = jnp.zeros((8, 128), f32)
        for c in range(8):
            part = pltpu.roll(out[8 * c : 8 * c + 8, 128:], (16 * c - 112) % 128, 1)
            middle = jnp.where(lane // 16 == c, part, middle)
        return unfold(high + middle[:5])

    own, other = total(got_ref), total(other_ref)
    lower = core_ref[0] == 0
    sums = (jnp.where(lower, own, other), jnp.where(lower, other, own))
    shift_grad_ref[...], gain_grad_ref[...] = [value.reshape(C) for value in sums]
    groups = group_matrix()
    gain, mean, rstd = gain_ref[...], row_ref[0:1], row_ref[1:2]

    both = jnp.concatenate([gain * sums[0], gain * sums[1], jnp.zeros((6, C), f32)], axis=0)
    both = exact_dot(exact_dot(both, groups, 0), groups, 1) / TOTAL
    first, second = both[0:1], both[1:2]
    xhat = (both_ref[:PIX].astype(f32) - mean) * rstd
    grad_ref[...] = (rstd * (da_ref[...] * gain - first - xhat * second)).astype(bf16)


def gather_kernel(got_ref, weight_ref):
    weight = got_ref[0].astype(f32)
    for z in range(1, NZ):
        weight = weight + got_ref[z].astype(f32)
    for i in range(3):
        for j in range(3):
            at = slice(j * NQ, (j + 1) * NQ)
            weight_ref[i, j, 0:16] = weight[16 * i : 16 * i + 16, at]
            weight_ref[i, j, 16:20] = weight[48 + 4 * i : 52 + 4 * i, at]


def flip(value):
    return lax.ppermute(value, "core", [(0, 1), (1, 0)])


def shape(dims, dtype):
    return jax.ShapeDtypeStruct(dims, dtype)


def body(features, cotangent, conv_weight, gain, shift):
    core, y, z = lax.axis_index("core"), lax.axis_index("y"), lax.axis_index("z")
    at_core, at_y, at_z = core.reshape(1), y.reshape(1), z.reshape(1)
    feat, cot = features.reshape(PIX, C), cotangent.reshape(PIX, C)
    gain, shift = gain.reshape(1, C), shift.reshape(1, C)
    cot2, feat2 = flip(cot), flip(feat)
    both = jnp.concatenate([feat, cot])
    edge = jnp.where(
        core == 0,
        jnp.concatenate([cot[PIX - TC :], cot2[PIX - TC :]]),
        jnp.concatenate([cot2[:TC], cot[:TC]]),
    )
    count = NZ * NY
    ways = [(2 * k, 2 * k + 2) for k in range(count - 1)] + [(2 * k + 3, 2 * k + 1) for k in range(count - 1)]
    mine = lax.ppermute(edge, ("z", "y", "core"), ways)

    packed = pl.pallas_call(
        pack_kernel,
        out_shape=shape((PEERS, G_ROWS, 128), bf16),
        in_specs=[smem()] + [vmem()] * 3,
        out_specs=hbm(),
        scratch_shapes=[pltpu.VMEM((PEERS, G_ROWS, 128), bf16), pltpu.SemaphoreType.DMA((2,))],
        compiler_params=params(),
        cost_estimate=pl.CostEstimate(flops=1 << 28, bytes_accessed=2 << 20, transcendentals=0),
        name="pack",
    )(at_core, both, feat2, cot2)
    slab = lax.all_to_all(packed, ("y", "x"), 0, 0)
    theirs = flip(mine)
    side = pl.pallas_call(
        side_kernel,
        out_shape=shape((TR, C), f32),
        in_specs=[smem()] + [vmem()] * 3 + [hbm()],
        out_specs=vmem(),
        scratch_shapes=[pltpu.VMEM((3, C, C), bf16), pltpu.SemaphoreType.DMA((3,))],
        compiler_params=params(),
        name="side",
    )(at_core, both, mine, theirs, conv_weight)
    slab, side = lax.optimization_barrier((slab, side))
    pairs = [(2 * k + 1, 2 * k + 2) for k in range(NX - 1)]
    side = lax.ppermute(side, ("x", "core"), pairs + [(b, a) for a, b in pairs])
    edges = pl.pallas_call(
        split_kernel,
        out_shape=shape((NZ, E_ROWS, 128), bf16),
        in_specs=[smem(), vmem()],
        out_specs=vmem(),
        compiler_params=params(),
        name="split",
    )(at_z, slab)
    slab_other = flip(slab)
    edges = lax.all_to_all(edges, "z", 0, 0)
    back = pl.pallas_call(
        back_kernel,
        out_shape=shape((PIX, C), f32),
        in_specs=[smem()] + [vmem()] * 4 + [hbm()],
        out_specs=vmem(),
        scratch_shapes=[
            pltpu.VMEM((3, (TR + 2) * TC, C), bf16),
            pltpu.VMEM((9, C, C), bf16),
            pltpu.SemaphoreType.DMA((9,)),
        ],
        compiler_params=params(),
        cost_estimate=pl.CostEstimate(flops=2 * PIX * 9 * C * C, bytes_accessed=18 * C * C, transcendentals=0),
        name="back",
    )(at_core, both, cot2, mine, theirs, conv_weight)


    row, da, table, sums, bias_grad = pl.pallas_call(
        sums_kernel,
        out_shape=(
            shape((8, C), f32),
            shape((PIX, C), f32),
            shape((8, 256), f32),
            shape((2 * PEERS, 8, 128), f32),
            shape((C,), f32),
        ),
        in_specs=[smem()] * 2 + [vmem()] * 6,
        out_specs=(vmem(),) * 5,
        compiler_params=params(),
        name="sums",
    )(at_core, at_y, edges, both, back, side, gain, shift)
    sums = lax.all_to_all(sums, ("y", "x", "core"), 0, 0)

    terms = pl.pallas_call(
        terms_kernel,
        out_shape=shape((NZ, W_ROWS, 256), bf16),
        in_specs=[smem()] * 2 + [vmem(), hbm(), vmem(), vmem()],
        out_specs=vmem(),
        scratch_shapes=[
            pltpu.VMEM((ROWS * 128, 256), bf16),
            pltpu.VMEM(((ROWS + 2) * 128, 128), bf16),
            pltpu.VMEM((256, (ROWS + 2) * 128), bf16),
            pltpu.VMEM((NZ, 16, 256), f32),
            pltpu.VMEM((PEERS, F_ROWS, 128), bf16),
            pltpu.SemaphoreType.DMA((1,)),
        ],
        compiler_params=params(),
        cost_estimate=pl.CostEstimate(
            flops=2 * PIX * 9 * C * C, bytes_accessed=4 << 20, transcendentals=ROWS * 128 * 256
        ),
        name="terms",
    )(at_core, at_z, slab, slab_other, edges, table)

    joined = pl.pallas_call(
        join_kernel,
        out_shape=shape((NZ, W_ROWS, 256), bf16),
        in_specs=[vmem()] * 2,
        out_specs=vmem(),
        compiler_params=params(),
        name="join",
    )(sums, terms)
    joined = lax.all_to_all(joined, "z", 0, 0)
    weight_grad = pl.pallas_call(
        gather_kernel,
        out_shape=shape((3, 3, 20, NQ), f32),
        in_specs=[vmem()],
        out_specs=vmem(),
        compiler_params=params(),
        cost_estimate=pl.CostEstimate(flops=1 << 22, bytes_accessed=1 << 20, transcendentals=0),
        name="gather",
    )(joined)
    grad, gain_grad, shift_grad = pl.pallas_call(
        final_kernel,
        out_shape=(shape((PIX, C), bf16),) + (shape((C,), f32),) * 2,
        in_specs=[smem()] + [vmem()] * 6,
        out_specs=(vmem(),) * 3,
        compiler_params=params(),
        name="final",
    )(at_core, joined, flip(joined), both, da, row, gain)
    return grad.reshape(features.shape), weight_grad, gain_grad, shift_grad, bias_grad


def solution(mesh):
    grid = Mesh(mesh.devices.reshape(NZ, NY, NX, 2), ("z", "y", "x", "core"))
    rows, cols = ("z", "y"), ("x", "core")
    tiled = P(rows, cols, None)
    return jax.shard_map(
        body,
        mesh=grid,
        in_specs=(tiled, tiled, P(), P(), P()),
        out_specs=(tiled, P(None, None, rows, cols), P(), P(), P()),
        check_vma=False,
    )
```

```python
import jax
import jax.numpy as jnp
from jax import lax
from jax.experimental import pallas as pl
from jax.experimental.pallas import tpu as pltpu
from jax.sharding import Mesh
from jax.sharding import PartitionSpec as P

C = 640
GW = 40
TR, TC = 8, 16
PIX = TR * TC
NZ, NY, NX = 8, 4, 4
PEERS = NY * NX
ROWS = NY * TR
NQ = 80
CHIP = float(2 * PIX * GW)
TOTAL = float(NZ * PEERS) * CHIP
VMEM_LIMIT = 48 * 1024 * 1024
F_ROWS, C_ROWS, S_ROWS = 160, 160, 16
S_AT = F_ROWS + C_ROWS
G_ROWS = S_AT + S_ROWS
E_ROWS = 96
W_ROWS = 64
f32, bf16 = jnp.float32, jnp.bfloat16


def lanes(count):
    return lax.broadcasted_iota(jnp.int32, (1, count), 1)


def slab_channel(main, at):
    z = jnp.where(main, at >> 4, at >> 2)
    return z * 80 + jnp.where(main, at & 15, 16 + (at & 3))


def feature_columns():
    lane = lanes(C)
    main = lane < 512
    y = jnp.where(main, lane >> 7, (lane - 512) >> 5)
    return slab_channel(main, jnp.where(main, lane & 127, lane & 31)) + y * 20


def cotangent_columns(core, side):
    lane = lanes(C)
    main = lane < 512
    x = jnp.where(main, lane >> 7, (lane - 512) >> 5)
    at = jnp.where(main, lane & 127, lane & 31)
    q = jnp.where(main, at & 63, 64 + (at & 15))
    mine = jnp.where(main, at >> 6, at >> 4) == side
    return jnp.where(mine, x * 160 + core * NQ + q, -1)


def term_columns(y):
    lane = lanes(256)
    main = lane < 128
    return slab_channel(main, jnp.where(main, lane, lane & 31)) + y * 20


def vmem():
    return pl.BlockSpec(memory_space=pltpu.VMEM)


def smem():
    return pl.BlockSpec(memory_space=pltpu.SMEM)


def hbm():
    return pl.BlockSpec(memory_space=pltpu.HBM)


def fetch(pairs, sem):
    copies = [pltpu.make_async_copy(src, dst, sem.at[k]) for k, (src, dst) in enumerate(pairs)]
    for copy in copies:
        copy.start()
    return copies


def params(**kw):
    return pltpu.CompilerParams(vmem_limit_bytes=VMEM_LIMIT, **kw)


def group_matrix():
    chan = lax.broadcasted_iota(jnp.int32, (C, 128), 0)
    low = lax.broadcasted_iota(jnp.int32, (C, 128), 1) * GW
    return jnp.where((chan >= low) & (chan < low + GW), 1.0, 0.0).astype(bf16)


def exact_dot(value, matrix, over):
    high, middle, low = three(value)
    stacked = jnp.concatenate([high, middle, low, jnp.zeros_like(low)], axis=0).astype(bf16)
    out = lax.dot_general(stacked, matrix, (((1,), (over,)), ((), ())), preferred_element_type=f32)
    return out[0:8] + out[8:16] + out[16:24]


def rows8(row):
    return jnp.broadcast_to(row, (8, row.shape[1]))


def pick(columns):
    rows = lax.broadcasted_iota(jnp.int32, (C, columns.shape[1]), 0)
    return (rows == columns).astype(f32).astype(bf16)


def sigmoid(value):
    return 0.5 * jnp.tanh(0.5 * value) + 0.5


def fold(row):
    return jnp.concatenate([row[:, 128 * t : 128 * t + 128] for t in range(5)], axis=0)


def unfold(rows):
    return jnp.concatenate([rows[t : t + 1] for t in range(5)], axis=1)


def three(value):
    high = value.astype(bf16).astype(f32)
    rest = value - high
    middle = rest.astype(bf16).astype(f32)
    return high, middle, rest - middle


def lanes32(value, height):
    group = lax.broadcasted_iota(jnp.int32, (height, 128), 1) // 32
    out = []
    for a in range(4):
        acc = jnp.zeros((height, 128), f32)
        for g in range(4):
            moved = pltpu.roll(value[height * g : height * (g + 1)], (32 * (g - a)) % 128, 1)
            acc = jnp.where(group == g, moved, acc)
        out.append(acc)
    return out


def put_pieces(mean, squares, bias):
    high, middle, _ = three(bias)
    rows = three(mean) + three(squares) + (high, middle)
    return jnp.concatenate(list(rows), axis=0).astype(bf16)


def merge_pieces(got, count):
    got = got.astype(f32)
    mean, squares = merge(got[:, 0] + got[:, 1] + got[:, 2], got[:, 3] + got[:, 4] + got[:, 5], count)
    total = got[0]
    for p in range(1, got.shape[0]):
        total = total + got[p]
    return mean, squares, total[6:11] + total[11:16]


def in_order(core, own, other):
    a, b = own[...].astype(f32), other[...].astype(f32)
    return jnp.where(core == 0, a, b).astype(bf16), jnp.where(core == 0, b, a).astype(bf16)


def blocks(core, first, second):
    return jnp.dot(first, pick(cotangent_columns(core, 0)), preferred_element_type=f32) + jnp.dot(
        second, pick(cotangent_columns(core, 1)), preferred_element_type=f32
    )


def pack_kernel(core_ref, both_ref, feat2_ref, cot2_ref, out_hbm, out_ref, sem):
    core = core_ref[0]
    feat_ref, cot_ref = both_ref.at[:PIX], both_ref.at[PIX:]
    x, x2 = feat_ref[...].astype(f32), feat2_ref[...].astype(f32)
    groups = group_matrix()
    total = x.sum(0, keepdims=True) + x2.sum(0, keepdims=True)
    mean = exact_dot(rows8(total), groups, 0) / CHIP
    wide = exact_dot(mean, groups, 1)[:1]
    squares = ((x - wide) ** 2).sum(0, keepdims=True) + ((x2 - wide) ** 2).sum(0, keepdims=True)
    bias = cot_ref[...].astype(f32).sum(0, keepdims=True) + cot2_ref[...].astype(f32).sum(0, keepdims=True)
    stats = put_pieces(mean[:1], exact_dot(rows8(squares), groups, 0)[:1], fold(bias))
    moved = jnp.dot(feat_ref[...], pick(feature_columns()), preferred_element_type=f32)
    moved_rest = lanes32(moved[:, 512:], 32)
    for p in range(PEERS):
        y = p // NX
        out_ref[p, 0:128] = moved[:, y * 128 : (y + 1) * 128].astype(bf16)
        out_ref[p, 128:160] = moved_rest[y].astype(bf16)
    copies = fetch(((out_ref.at[:, :F_ROWS, :], out_hbm.at[:, :F_ROWS, :]),), sem.at[0:1])
    first, second = in_order(core, cot_ref, cot2_ref)
    terms = blocks(core, first, second)
    terms_rest = lanes32(terms[:, 512:], 32)
    for p in range(PEERS):
        xx = p % NX
        out_ref[p, 160:288] = terms[:, xx * 128 : (xx + 1) * 128].astype(bf16)
        out_ref[p, 288:320] = terms_rest[xx].astype(bf16)
        out_ref[p, S_AT:] = stats
    copies += fetch(((out_ref.at[:, F_ROWS:, :], out_hbm.at[:, F_ROWS:, :]),), sem.at[1:2])
    for copy in copies:
        copy.wait()


def merge(means, squares, count):
    n = means.shape[0]
    mean = means.sum(0, keepdims=True) / n
    return mean, squares.sum(0, keepdims=True) + count * ((means - mean) ** 2).sum(0, keepdims=True)


def cot_rows(main, rest, g, side):
    lane = lax.broadcasted_iota(jnp.int32, main.shape, 1)
    main = pltpu.roll(main, 64, 1) if side else main
    return jnp.where(lane < 64, main, pltpu.roll(rest, (64 - 32 * g - 16 * side) % 128, 1))


def split_kernel(z_ref, slab_ref, out_ref):
    stats = put_pieces(*merge_pieces(slab_ref[:, S_AT:], CHIP))
    group = lax.broadcasted_iota(jnp.int32, (TC, 128), 1) // 32
    first, last = jnp.zeros((TC, 128), f32), jnp.zeros((TC, 128), f32)
    for xx in range(NX):
        tail = slab_ref[xx, 288:304].astype(f32)
        first = jnp.where(group == xx, pltpu.roll(tail, 32 * xx, 1) if xx else tail, first)
        tail = slab_ref[(NY - 1) * NX + xx, 304:320].astype(f32)
        last = jnp.where(group == xx, pltpu.roll(tail, (32 * xx + 32) % 128, 1) if xx < 3 else tail, last)
    first, last = first.astype(bf16), last.astype(bf16)
    for p in range(NZ):
        out_ref[p, :S_ROWS] = stats

        @pl.when(z_ref[0] < p)
        def _():
            for xx in range(NX):
                out_ref[p, 16 + 16 * xx : 32 + 16 * xx] = slab_ref[(NY - 1) * NX + xx, 272:288]
            out_ref[p, 80:] = last

        @pl.when(z_ref[0] >= p)
        def _():
            for xx in range(NX):
                out_ref[p, 16 + 16 * xx : 32 + 16 * xx] = slab_ref[xx, 160:176]
            out_ref[p, 80:] = first


def back_kernel(shifted, w_hbm, out_ref, w_ref, sem):
    copies = fetch([(w_hbm.at[t // 3, t % 3], w_ref.at[t]) for t in range(9)], sem)
    total = None
    for i in range(3):
        for copy in copies[3 * i : 3 * i + 3]:
            copy.wait()
        for j in range(3):
            pixels = shifted[2 - j, (2 - i) * TC : (2 - i) * TC + PIX]
            part = lax.dot_general(w_ref[3 * i + j], pixels, (((1,), (1,)), ((), ())), preferred_element_type=f32)
            total = part if total is None else total + part
    out_ref[...] = total.T


def side_kernel(core_ref, both_ref, cot2_ref, mine_ref, theirs_ref, w_hbm, out_ref, shifted, w_ref, sem):
    j = 2 * core_ref[0]
    copies = fetch([(w_hbm.at[i, j], w_ref.at[i]) for i in range(3)], sem)
    lower = core_ref[0] == 0
    rows = (TR + 2) * TC
    mine, theirs = mine_ref[...].astype(f32), theirs_ref[...].astype(f32)
    top, bottom = jnp.where(lower, mine, theirs), jnp.where(lower, theirs, mine)
    own_top, other_top = jnp.where(lower, top[:TC], top[TC:]), jnp.where(lower, top[TC:], top[:TC])
    own_bot, other_bot = jnp.where(lower, bottom[:TC], bottom[TC:]), jnp.where(lower, bottom[TC:], bottom[:TC])
    wide = jnp.concatenate([own_top, both_ref[PIX:].astype(f32), own_bot], axis=0)
    near = jnp.concatenate([other_top, cot2_ref[...].astype(f32), other_bot], axis=0)
    near = near.reshape(TR + 2, TC, C)
    inner = jnp.where(lower, near[:, :1], near[:, TC - 1 :])
    left, right = jnp.where(lower, 0.0, inner), jnp.where(lower, inner, 0.0)
    left = jnp.broadcast_to(left, (TR + 2, TC, C)).reshape(rows, C)
    right = jnp.broadcast_to(right, (TR + 2, TC, C)).reshape(rows, C)
    col = lax.broadcasted_iota(jnp.int32, (rows, C), 0) % TC
    shifted[0] = jnp.where(col == 0, left, pltpu.roll(wide, 1, 0)).astype(bf16)
    shifted[1] = wide.astype(bf16)
    shifted[2] = jnp.where(col == TC - 1, right, pltpu.roll(wide, rows - 1, 0)).astype(bf16)
    column = wide.reshape(TR + 2, TC, C)
    column = jnp.where(lower, column[:, :1], column[:, TC - 1 :])
    total = jnp.zeros((TR, C), f32)
    for i in range(3):
        copies[i].wait()
        pixels = column[2 - i : 2 - i + TR].reshape(TR, C).astype(bf16)
        total = total + lax.dot_general(
            pixels, w_ref[i], (((1,), (1,)), ((), ())), preferred_element_type=f32
        )
    out_ref[...] = total


def sums_kernel(core_ref, y_ref, stat_ref, both_ref, back_ref, side_ref, gain_ref, shift_ref,
                row_ref, da_ref, par_ref, out_ref, bias_ref):
    mean, squares, bias = merge_pieces(stat_ref[:, :S_ROWS], PEERS * CHIP)
    bias_ref[...] = unfold(bias).reshape(C)
    groups = group_matrix()
    both = jnp.concatenate([mean, lax.rsqrt(squares / TOTAL + 1e-05), jnp.zeros((6, 128), f32)], axis=0)
    both = exact_dot(both, groups, 1)
    mean, rstd = both[0:1], both[1:2]
    gain, shift = gain_ref[...], shift_ref[...]
    row = lax.broadcasted_iota(jnp.int32, (8, C), 0)
    row_ref[...] = jnp.where(row == 0, mean, rstd)
    table = jnp.where(row == 0, mean, jnp.where(row == 1, rstd * gain, jnp.where(row == 2, shift, 0.0)))
    par_ref[...] = exact_dot(table, pick(term_columns(y_ref[0])), 0)
    xhat = (both_ref[:PIX].astype(f32) - mean) * rstd
    act = xhat * gain + shift
    sig = sigmoid(act)
    column = lax.broadcasted_iota(jnp.int32, (TR, TC, C), 1)
    side = jnp.broadcast_to(side_ref[...][:, None, :], (TR, TC, C))
    side = jnp.where(column == core_ref[0] * (TC - 1), side, 0.0).reshape(PIX, C)
    da = (back_ref[...] + side) * sig * (1.0 + act * (1.0 - sig))
    da_ref[...] = da
    empty = jnp.zeros((3, 128), f32)
    for side, value in enumerate((da, da * xhat)):
        block = jnp.concatenate([fold(value.sum(0, keepdims=True)), empty], axis=0)
        for p in range(side, 2 * PEERS, 2):
            out_ref[p] = block


def terms_kernel(core_ref, z_ref, own_ref, other_hbm, edge_ref, par_ref, out_ref,
                 hid0, hid1, hid2, hid3, strips, cot3, rest, totals, other_ref, sem):
    hidden = (hid0, hid1, hid2, hid3)
    copies = fetch(((other_hbm.at[:, :F_ROWS, :], other_ref),), sem)
    core = core_ref[0]

    def put(block, peer, side):
        y, xx = peer // NX, peer % NX

        def silu(x, lanes):
            a = (x.astype(f32) - par_ref[0:1, lanes]) * par_ref[1:2, lanes] + par_ref[2:3, lanes]
            return a * sigmoid(a)

        main = silu(block[:128], slice(0, 128)).astype(bf16)
        tail = silu(block[128:], slice(128, 256))
        for g in range(4):
            low = pltpu.roll(tail, (128 - 32 * g) % 128, 1).astype(bf16)
            for h in range(2):
                r = 2 * g + h
                at = pl.ds(pl.multiple_of(r * 128 + xx * 32 + side * TC, TC), TC)
                hidden[y][at, 0:128] = main[r * TC : (r + 1) * TC]
                hidden[y][at, 128:256] = low[h * TC : (h + 1) * TC]

    for peer in range(PEERS):
        y, xx = peer // NX, peer % NX
        tail = own_ref[peer, 288:320].astype(f32)
        for g in range(4):
            main = own_ref[peer, 160 + 32 * g : 192 + 32 * g].astype(f32)
            for side in range(2):
                value = cot_rows(main, tail, g, side).astype(bf16)
                for h in range(2):
                    at = (y * TR + 2 * g + h + 1) * 128 + xx * 32 + side * TC
                    strips[at : at + TC] = value[h * TC : (h + 1) * TC]
    z = z_ref[0]
    for start, peer, there in ((0, jnp.maximum(z - 1, 0), z > 0),
                               ((ROWS + 1) * 128, jnp.minimum(z + 1, NZ - 1), z < NZ - 1)):
        got = jnp.where(there, edge_ref[peer].astype(f32), 0.0)
        for xx in range(NX):
            for side in range(2):
                at = start + xx * 32 + side * TC
                value = cot_rows(got[16 + 16 * xx : 32 + 16 * xx], got[80:], xx, side)
                strips[at : at + TC] = value.astype(bf16)
    lane = lax.broadcasted_iota(jnp.int32, (NQ, 128), 1)
    for row in range(ROWS + 2):
        at = slice(row * 128, (row + 1) * 128)
        turned = strips[at].astype(f32).T[:NQ]
        before = jnp.where(lane == 0, 0.0, pltpu.roll(turned, 1, 1))
        after = jnp.where(lane == 127, 0.0, pltpu.roll(turned, 127, 1))
        cot3[0:NQ, at] = after.astype(bf16)
        cot3[NQ : 2 * NQ, at] = turned.astype(bf16)
        cot3[2 * NQ : 3 * NQ, at] = before.astype(bf16)
    cot3[3 * NQ :] = jnp.zeros((16, (ROWS + 2) * 128), bf16)
    copies[0].wait()
    for y in range(NY):
        for peer in range(y * NX, (y + 1) * NX):
            put(own_ref[peer, :F_ROWS], peer, core)
            put(other_ref[peer], peer, 1 - core)
        for i in range(3):
            at = (2 - i + y * TR) * 128
            part = jnp.dot(cot3[:, at : at + TR * 128], hidden[y][...], preferred_element_type=f32)
            if y == 0:
                totals[i] = part
            else:
                totals[i] += part
    rest[...] = jnp.zeros_like(rest)
    for i in range(3):
        turned = totals[i].T
        for z in range(NZ):
            out_ref[z, 16 * i : 16 * i + 16] = turned[16 * z : 16 * z + 16].astype(bf16)
            rest[z, 4 * i : 4 * i + 4] = turned[128 + 4 * z : 132 + 4 * z]
    for z in range(NZ):
        out_ref[z, 48:64] = rest[z].astype(bf16)


def join_kernel(sums_ref, terms_ref, out_ref):
    value = sums_ref[0]
    for p in range(1, 2 * PEERS):
        value = value + sums_ref[p]
    high, middle, _ = three(value)
    lane = lax.broadcasted_iota(jnp.int32, (16, 128), 1)
    row = lax.broadcasted_iota(jnp.int32, (16, 128), 0)
    tails = [
        jnp.concatenate([pltpu.roll(middle, (112 - 16 * c) % 128, 1) for c in (2 * k, 2 * k + 1)], axis=0)
        for k in range(4)
    ]
    for z in range(NZ):
        for k in range(4):
            at = slice(16 * k, 16 * k + 16)
            block = terms_ref[z, at].astype(f32)
            left, right = block[:, :128], block[:, 128:]
            right = jnp.where(lane >= 112, tails[k], right)
            if k == 3:
                left = jnp.concatenate([left[:12], high[:4]], axis=0)
                right = jnp.where(row == 13, high[4:5], right)
            out_ref[z, at] = jnp.concatenate([left, right], axis=1).astype(bf16)


def final_kernel(core_ref, got_ref, other_ref, both_ref, da_ref, row_ref, gain_ref,
                 grad_ref, gain_grad_ref, shift_grad_ref):
    lane = lax.broadcasted_iota(jnp.int32, (8, 128), 1)

    def total(ref):
        out = ref[0].astype(f32)
        for z in range(1, NZ):
            out = out + ref[z].astype(f32)
        high = jnp.concatenate([out[60:64, :128], out[61:62, 128:]], axis=0)
        middle = jnp.zeros((8, 128), f32)
        for c in range(8):
            part = pltpu.roll(out[8 * c : 8 * c + 8, 128:], (16 * c - 112) % 128, 1)
            middle = jnp.where(lane // 16 == c, part, middle)
        return unfold(high + middle[:5])

    own, other = total(got_ref), total(other_ref)
    lower = core_ref[0] == 0
    sums = (jnp.where(lower, own, other), jnp.where(lower, other, own))
    shift_grad_ref[...], gain_grad_ref[...] = [value.reshape(C) for value in sums]
    groups = group_matrix()
    gain, mean, rstd = gain_ref[...], row_ref[0:1], row_ref[1:2]

    both = jnp.concatenate([gain * sums[0], gain * sums[1], jnp.zeros((6, C), f32)], axis=0)
    both = exact_dot(exact_dot(both, groups, 0), groups, 1) / TOTAL
    first, second = both[0:1], both[1:2]
    xhat = (both_ref[:PIX].astype(f32) - mean) * rstd
    grad_ref[...] = (rstd * (da_ref[...] * gain - first - xhat * second)).astype(bf16)


def gather_kernel(got_ref, weight_ref):
    weight = got_ref[0].astype(f32)
    for z in range(1, NZ):
        weight = weight + got_ref[z].astype(f32)
    for i in range(3):
        for j in range(3):
            at = slice(j * NQ, (j + 1) * NQ)
            weight_ref[i, j, 0:16] = weight[16 * i : 16 * i + 16, at]
            weight_ref[i, j, 16:20] = weight[48 + 4 * i : 52 + 4 * i, at]


def flip(value):
    return lax.ppermute(value, "core", [(0, 1), (1, 0)])


def shape(dims, dtype):
    return jax.ShapeDtypeStruct(dims, dtype)


def body(features, cotangent, conv_weight, gain, shift):
    core, y, z = lax.axis_index("core"), lax.axis_index("y"), lax.axis_index("z")
    at_core, at_y, at_z = core.reshape(1), y.reshape(1), z.reshape(1)
    feat, cot = features.reshape(PIX, C), cotangent.reshape(PIX, C)
    gain, shift = gain.reshape(1, C), shift.reshape(1, C)
    cot2, feat2 = flip(cot), flip(feat)
    both = jnp.concatenate([feat, cot])
    edge = jnp.where(
        core == 0,
        jnp.concatenate([cot[PIX - TC :], cot2[PIX - TC :]]),
        jnp.concatenate([cot2[:TC], cot[:TC]]),
    )
    count = NZ * NY
    ways = [(2 * k, 2 * k + 2) for k in range(count - 1)] + [(2 * k + 3, 2 * k + 1) for k in range(count - 1)]
    mine = lax.ppermute(edge, ("z", "y", "core"), ways)

    packed = pl.pallas_call(
        pack_kernel,
        out_shape=shape((PEERS, G_ROWS, 128), bf16),
        in_specs=[smem()] + [vmem()] * 3,
        out_specs=hbm(),
        scratch_shapes=[pltpu.VMEM((PEERS, G_ROWS, 128), bf16), pltpu.SemaphoreType.DMA((2,))],
        compiler_params=params(),
        cost_estimate=pl.CostEstimate(flops=1 << 28, bytes_accessed=2 << 20, transcendentals=0),
        name="pack",
    )(at_core, both, feat2, cot2)
    slab = lax.all_to_all(packed, ("y", "x"), 0, 0)
    theirs = flip(mine)
    side, shifted = pl.pallas_call(
        side_kernel,
        out_shape=(shape((TR, C), f32), shape((3, (TR + 2) * TC, C), bf16)),
        in_specs=[smem()] + [vmem()] * 4 + [hbm()],
        out_specs=(vmem(), vmem()),
        scratch_shapes=[pltpu.VMEM((3, C, C), bf16), pltpu.SemaphoreType.DMA((3,))],
        compiler_params=params(),
        name="side",
    )(at_core, both, cot2, mine, theirs, conv_weight)
    slab, side = lax.optimization_barrier((slab, side))
    pairs = [(2 * k + 1, 2 * k + 2) for k in range(NX - 1)]
    side = lax.ppermute(side, ("x", "core"), pairs + [(b, a) for a, b in pairs])
    edges = pl.pallas_call(
        split_kernel,
        out_shape=shape((NZ, E_ROWS, 128), bf16),
        in_specs=[smem(), vmem()],
        out_specs=vmem(),
        compiler_params=params(),
        name="split",
    )(at_z, slab)
    slab_other = flip(slab)
    edges = lax.all_to_all(edges, "z", 0, 0)
    back = pl.pallas_call(
        back_kernel,
        out_shape=shape((PIX, C), f32),
        in_specs=[vmem(), hbm()],
        out_specs=vmem(),
        scratch_shapes=[pltpu.VMEM((9, C, C), bf16), pltpu.SemaphoreType.DMA((9,))],
        compiler_params=params(),
        cost_estimate=pl.CostEstimate(flops=2 * PIX * 9 * C * C, bytes_accessed=18 * C * C, transcendentals=0),
        name="back",
    )(shifted, conv_weight)
    row, da, table, sums, bias_grad = pl.pallas_call(
        sums_kernel,
        out_shape=(
            shape((8, C), f32),
            shape((PIX, C), f32),
            shape((8, 256), f32),
            shape((2 * PEERS, 8, 128), f32),
            shape((C,), f32),
        ),
        in_specs=[smem()] * 2 + [vmem()] * 6,
        out_specs=(vmem(),) * 5,
        compiler_params=params(),
        name="sums",
    )(at_core, at_y, edges, both, back, side, gain, shift)
    sums = lax.all_to_all(sums, ("y", "x", "core"), 0, 0)

    terms = pl.pallas_call(
        terms_kernel,
        out_shape=shape((NZ, W_ROWS, 256), bf16),
        in_specs=[smem()] * 2 + [vmem(), hbm(), vmem(), vmem()],
        out_specs=vmem(),
        scratch_shapes=[
            pltpu.VMEM((TR * 128, 256), bf16),
            pltpu.VMEM((TR * 128, 256), bf16),
            pltpu.VMEM((TR * 128, 256), bf16),
            pltpu.VMEM((TR * 128, 256), bf16),
            pltpu.VMEM(((ROWS + 2) * 128, 128), bf16),
            pltpu.VMEM((256, (ROWS + 2) * 128), bf16),
            pltpu.VMEM((NZ, 16, 256), f32),
            pltpu.VMEM((3, 256, 256), f32),
            pltpu.VMEM((PEERS, F_ROWS, 128), bf16),
            pltpu.SemaphoreType.DMA((1,)),
        ],
        compiler_params=params(),
        cost_estimate=pl.CostEstimate(
            flops=2 * PIX * 9 * C * C, bytes_accessed=4 << 20, transcendentals=ROWS * 128 * 256
        ),
        name="terms",
    )(at_core, at_z, slab, slab_other, edges, table)

    joined = pl.pallas_call(
        join_kernel,
        out_shape=shape((NZ, W_ROWS, 256), bf16),
        in_specs=[vmem()] * 2,
        out_specs=vmem(),
        compiler_params=params(),
        name="join",
    )(sums, terms)
    joined = lax.all_to_all(joined, "z", 0, 0)
    weight_grad = pl.pallas_call(
        gather_kernel,
        out_shape=shape((3, 3, 20, NQ), f32),
        in_specs=[vmem()],
        out_specs=vmem(),
        compiler_params=params(),
        cost_estimate=pl.CostEstimate(flops=1 << 22, bytes_accessed=1 << 20, transcendentals=0),
        name="gather",
    )(joined)
    grad, gain_grad, shift_grad = pl.pallas_call(
        final_kernel,
        out_shape=(shape((PIX, C), bf16),) + (shape((C,), f32),) * 2,
        in_specs=[smem()] + [vmem()] * 6,
        out_specs=(vmem(),) * 3,
        compiler_params=params(),
        name="final",
    )(at_core, joined, flip(joined), both, da, row, gain)
    return grad.reshape(features.shape), weight_grad, gain_grad, shift_grad, bias_grad


def solution(mesh):
    grid = Mesh(mesh.devices.reshape(NZ, NY, NX, 2), ("z", "y", "x", "core"))
    rows, cols = ("z", "y"), ("x", "core")
    tiled = P(rows, cols, None)
    return jax.shard_map(
        body,
        mesh=grid,
        in_specs=(tiled, tiled, P(), P(), P()),
        out_specs=(tiled, P(None, None, rows, cols), P(), P(), P()),
        check_vma=False,
    )
```

```python
import jax
import jax.numpy as jnp
from jax import lax
from jax.experimental import pallas as pl
from jax.experimental.pallas import tpu as pltpu
from jax.sharding import Mesh
from jax.sharding import PartitionSpec as P

C = 640
GW = 40
TR, TC = 8, 16
PIX = TR * TC
NZ, NY, NX = 8, 4, 4
PEERS = NY * NX
ROWS = NY * TR
NQ = 80
CHIP = float(2 * PIX * GW)
TOTAL = float(NZ * PEERS) * CHIP
VMEM_LIMIT = 48 * 1024 * 1024
F_ROWS, C_ROWS, S_ROWS = 160, 160, 16
S_AT = F_ROWS + C_ROWS
G_ROWS = S_AT + S_ROWS
E_ROWS = 96
W_ROWS = 64
f32, bf16 = jnp.float32, jnp.bfloat16


def lanes(count):
    return lax.broadcasted_iota(jnp.int32, (1, count), 1)


def slab_channel(main, at):
    z = jnp.where(main, at >> 4, at >> 2)
    return z * 80 + jnp.where(main, at & 15, 16 + (at & 3))


def feature_columns():
    lane = lanes(C)
    main = lane < 512
    y = jnp.where(main, lane >> 7, (lane - 512) >> 5)
    return slab_channel(main, jnp.where(main, lane & 127, lane & 31)) + y * 20


def cotangent_columns(core, side):
    lane = lanes(C)
    main = lane < 512
    x = jnp.where(main, lane >> 7, (lane - 512) >> 5)
    at = jnp.where(main, lane & 127, lane & 31)
    q = jnp.where(main, at & 63, 64 + (at & 15))
    mine = jnp.where(main, at >> 6, at >> 4) == side
    return jnp.where(mine, x * 160 + core * NQ + q, -1)


def term_columns(y):
    lane = lanes(256)
    main = lane < 128
    return slab_channel(main, jnp.where(main, lane, lane & 31)) + y * 20


def vmem():
    return pl.BlockSpec(memory_space=pltpu.VMEM)


def smem():
    return pl.BlockSpec(memory_space=pltpu.SMEM)


def hbm():
    return pl.BlockSpec(memory_space=pltpu.HBM)


def fetch(pairs, sem):
    copies = [pltpu.make_async_copy(src, dst, sem.at[k]) for k, (src, dst) in enumerate(pairs)]
    for copy in copies:
        copy.start()
    return copies


def params(**kw):
    return pltpu.CompilerParams(vmem_limit_bytes=VMEM_LIMIT, **kw)


def group_matrix():
    chan = lax.broadcasted_iota(jnp.int32, (C, 128), 0)
    low = lax.broadcasted_iota(jnp.int32, (C, 128), 1) * GW
    return jnp.where((chan >= low) & (chan < low + GW), 1.0, 0.0).astype(bf16)


def exact_dot(value, matrix, over):
    high, middle, low = three(value)
    stacked = jnp.concatenate([high, middle, low, jnp.zeros_like(low)], axis=0).astype(bf16)
    out = lax.dot_general(stacked, matrix, (((1,), (over,)), ((), ())), preferred_element_type=f32)
    return out[0:8] + out[8:16] + out[16:24]


def rows8(row):
    return jnp.broadcast_to(row, (8, row.shape[1]))


def pick(columns):
    rows = lax.broadcasted_iota(jnp.int32, (C, columns.shape[1]), 0)
    return (rows == columns).astype(f32).astype(bf16)


def sigmoid(value):
    return 0.5 * jnp.tanh(0.5 * value) + 0.5


def fold(row):
    return jnp.concatenate([row[:, 128 * t : 128 * t + 128] for t in range(5)], axis=0)


def unfold(rows):
    return jnp.concatenate([rows[t : t + 1] for t in range(5)], axis=1)


def three(value):
    high = value.astype(bf16).astype(f32)
    rest = value - high
    middle = rest.astype(bf16).astype(f32)
    return high, middle, rest - middle


def lanes32(value, height):
    group = lax.broadcasted_iota(jnp.int32, (height, 128), 1) // 32
    out = []
    for a in range(4):
        acc = jnp.zeros((height, 128), f32)
        for g in range(4):
            moved = pltpu.roll(value[height * g : height * (g + 1)], (32 * (g - a)) % 128, 1)
            acc = jnp.where(group == g, moved, acc)
        out.append(acc)
    return out


def put_pieces(mean, squares, bias):
    high, middle, _ = three(bias)
    rows = three(mean) + three(squares) + (high, middle)
    return jnp.concatenate(list(rows), axis=0).astype(bf16)


def merge_pieces(got, count):
    got = got.astype(f32)
    mean, squares = merge(got[:, 0] + got[:, 1] + got[:, 2], got[:, 3] + got[:, 4] + got[:, 5], count)
    total = got[0]
    for p in range(1, got.shape[0]):
        total = total + got[p]
    return mean, squares, total[6:11] + total[11:16]


def in_order(core, own, other):
    a, b = own[...].astype(f32), other[...].astype(f32)
    return jnp.where(core == 0, a, b).astype(bf16), jnp.where(core == 0, b, a).astype(bf16)


def blocks(core, first, second):
    return jnp.dot(first, pick(cotangent_columns(core, 0)), preferred_element_type=f32) + jnp.dot(
        second, pick(cotangent_columns(core, 1)), preferred_element_type=f32
    )


def pack_kernel(core_ref, both_ref, feat2_ref, cot2_ref, out_hbm, out_ref, sem):
    core = core_ref[0]
    feat_ref, cot_ref = both_ref.at[:PIX], both_ref.at[PIX:]
    x, x2 = feat_ref[...].astype(f32), feat2_ref[...].astype(f32)
    groups = group_matrix()
    total = x.sum(0, keepdims=True) + x2.sum(0, keepdims=True)
    mean = exact_dot(rows8(total), groups, 0) / CHIP
    wide = exact_dot(mean, groups, 1)[:1]
    squares = ((x - wide) ** 2).sum(0, keepdims=True) + ((x2 - wide) ** 2).sum(0, keepdims=True)
    bias = cot_ref[...].astype(f32).sum(0, keepdims=True) + cot2_ref[...].astype(f32).sum(0, keepdims=True)
    stats = put_pieces(mean[:1], exact_dot(rows8(squares), groups, 0)[:1], fold(bias))
    moved = jnp.dot(feat_ref[...], pick(feature_columns()), preferred_element_type=f32)
    moved_rest = lanes32(moved[:, 512:], 32)
    for p in range(PEERS):
        y = p % NY
        out_ref[p, 0:128] = moved[:, y * 128 : (y + 1) * 128].astype(bf16)
        out_ref[p, 128:160] = moved_rest[y].astype(bf16)
    copies = fetch(((out_ref.at[:, :F_ROWS, :], out_hbm.at[:, :F_ROWS, :]),), sem.at[0:1])
    first, second = in_order(core, cot_ref, cot2_ref)
    terms = blocks(core, first, second)
    terms_rest = lanes32(terms[:, 512:], 32)
    for p in range(PEERS):
        xx = p // NY
        out_ref[p, 160:288] = terms[:, xx * 128 : (xx + 1) * 128].astype(bf16)
        out_ref[p, 288:320] = terms_rest[xx].astype(bf16)
        out_ref[p, S_AT:] = stats
    copies += fetch(((out_ref.at[:, F_ROWS:, :], out_hbm.at[:, F_ROWS:, :]),), sem.at[1:2])
    for copy in copies:
        copy.wait()


def merge(means, squares, count):
    n = means.shape[0]
    mean = means.sum(0, keepdims=True) / n
    return mean, squares.sum(0, keepdims=True) + count * ((means - mean) ** 2).sum(0, keepdims=True)


def cot_rows(main, rest, g, side):
    lane = lax.broadcasted_iota(jnp.int32, main.shape, 1)
    main = pltpu.roll(main, 64, 1) if side else main
    return jnp.where(lane < 64, main, pltpu.roll(rest, (64 - 32 * g - 16 * side) % 128, 1))


def split_kernel(z_ref, slab_ref, out_ref):
    stats = put_pieces(*merge_pieces(slab_ref[:, S_AT:], CHIP))
    group = lax.broadcasted_iota(jnp.int32, (TC, 128), 1) // 32
    first, last = jnp.zeros((TC, 128), f32), jnp.zeros((TC, 128), f32)
    for xx in range(NX):
        tail = slab_ref[xx * NY, 288:304].astype(f32)
        first = jnp.where(group == xx, pltpu.roll(tail, 32 * xx, 1) if xx else tail, first)
        tail = slab_ref[xx * NY + NY - 1, 304:320].astype(f32)
        last = jnp.where(group == xx, pltpu.roll(tail, (32 * xx + 32) % 128, 1) if xx < 3 else tail, last)
    first, last = first.astype(bf16), last.astype(bf16)
    for p in range(NZ):
        out_ref[p, :S_ROWS] = stats

        @pl.when(z_ref[0] < p)
        def _():
            for xx in range(NX):
                out_ref[p, 16 + 16 * xx : 32 + 16 * xx] = slab_ref[xx * NY + NY - 1, 272:288]
            out_ref[p, 80:] = last

        @pl.when(z_ref[0] >= p)
        def _():
            for xx in range(NX):
                out_ref[p, 16 + 16 * xx : 32 + 16 * xx] = slab_ref[xx * NY, 160:176]
            out_ref[p, 80:] = first


def back_kernel(shifted, w_hbm, out_ref, w_ref, sem):
    copies = fetch([(w_hbm.at[t // 3, t % 3], w_ref.at[t]) for t in range(9)], sem)
    total = None
    for i in range(3):
        for copy in copies[3 * i : 3 * i + 3]:
            copy.wait()
        for j in range(3):
            pixels = shifted[2 - j, (2 - i) * TC : (2 - i) * TC + PIX]
            part = lax.dot_general(w_ref[3 * i + j], pixels, (((1,), (1,)), ((), ())), preferred_element_type=f32)
            total = part if total is None else total + part
    out_ref[...] = total.T


def side_kernel(core_ref, both_ref, cot2_ref, mine_ref, theirs_ref, w_hbm, out_ref, shifted, w_ref, sem):
    j = 2 * core_ref[0]
    copies = fetch([(w_hbm.at[i, j], w_ref.at[i]) for i in range(3)], sem)
    lower = core_ref[0] == 0
    rows = (TR + 2) * TC
    mine, theirs = mine_ref[...].astype(f32), theirs_ref[...].astype(f32)
    top, bottom = jnp.where(lower, mine, theirs), jnp.where(lower, theirs, mine)
    own_top, other_top = jnp.where(lower, top[:TC], top[TC:]), jnp.where(lower, top[TC:], top[:TC])
    own_bot, other_bot = jnp.where(lower, bottom[:TC], bottom[TC:]), jnp.where(lower, bottom[TC:], bottom[:TC])
    wide = jnp.concatenate([own_top, both_ref[PIX:].astype(f32), own_bot], axis=0)
    near = jnp.concatenate([other_top, cot2_ref[...].astype(f32), other_bot], axis=0)
    near = near.reshape(TR + 2, TC, C)
    inner = jnp.where(lower, near[:, :1], near[:, TC - 1 :])
    left, right = jnp.where(lower, 0.0, inner), jnp.where(lower, inner, 0.0)
    left = jnp.broadcast_to(left, (TR + 2, TC, C)).reshape(rows, C)
    right = jnp.broadcast_to(right, (TR + 2, TC, C)).reshape(rows, C)
    col = lax.broadcasted_iota(jnp.int32, (rows, C), 0) % TC
    shifted[0] = jnp.where(col == 0, left, pltpu.roll(wide, 1, 0)).astype(bf16)
    shifted[1] = wide.astype(bf16)
    shifted[2] = jnp.where(col == TC - 1, right, pltpu.roll(wide, rows - 1, 0)).astype(bf16)
    column = wide.reshape(TR + 2, TC, C)
    column = jnp.where(lower, column[:, :1], column[:, TC - 1 :])
    total = jnp.zeros((TR, C), f32)
    for i in range(3):
        copies[i].wait()
        pixels = column[2 - i : 2 - i + TR].reshape(TR, C).astype(bf16)
        total = total + lax.dot_general(
            pixels, w_ref[i], (((1,), (1,)), ((), ())), preferred_element_type=f32
        )
    out_ref[...] = total


def sums_kernel(core_ref, y_ref, stat_ref, both_ref, back_ref, side_ref, gain_ref, shift_ref,
                row_ref, da_ref, par_ref, out_ref, bias_ref):
    mean, squares, bias = merge_pieces(stat_ref[:, :S_ROWS], PEERS * CHIP)
    bias_ref[...] = unfold(bias).reshape(C)
    groups = group_matrix()
    both = jnp.concatenate([mean, lax.rsqrt(squares / TOTAL + 1e-05), jnp.zeros((6, 128), f32)], axis=0)
    both = exact_dot(both, groups, 1)
    mean, rstd = both[0:1], both[1:2]
    gain, shift = gain_ref[...], shift_ref[...]
    row = lax.broadcasted_iota(jnp.int32, (8, C), 0)
    row_ref[...] = jnp.where(row == 0, mean, rstd)
    table = jnp.where(row == 0, mean, jnp.where(row == 1, rstd * gain, jnp.where(row == 2, shift, 0.0)))
    par_ref[...] = exact_dot(table, pick(term_columns(y_ref[0])), 0)
    xhat = (both_ref[:PIX].astype(f32) - mean) * rstd
    act = xhat * gain + shift
    sig = sigmoid(act)
    column = lax.broadcasted_iota(jnp.int32, (TR, TC, C), 1)
    side = jnp.broadcast_to(side_ref[...][:, None, :], (TR, TC, C))
    side = jnp.where(column == core_ref[0] * (TC - 1), side, 0.0).reshape(PIX, C)
    da = (back_ref[...] + side) * sig * (1.0 + act * (1.0 - sig))
    da_ref[...] = da
    empty = jnp.zeros((3, 128), f32)
    for side, value in enumerate((da, da * xhat)):
        block = jnp.concatenate([fold(value.sum(0, keepdims=True)), empty], axis=0)
        for p in range(side, 2 * PEERS, 2):
            out_ref[p] = block


def terms_kernel(core_ref, z_ref, own_ref, other_hbm, edge_ref, par_ref, out_ref,
                 hid0, hid1, hid2, hid3, strips, cot3, rest, totals, other_ref, sem):
    hidden = (hid0, hid1, hid2, hid3)
    copies = fetch(((other_hbm.at[:, :F_ROWS, :], other_ref),), sem)
    core = core_ref[0]

    def put(block, peer, side):
        xx, y = peer // NY, peer % NY

        def silu(x, lanes):
            a = (x.astype(f32) - par_ref[0:1, lanes]) * par_ref[1:2, lanes] + par_ref[2:3, lanes]
            return a * sigmoid(a)

        main = silu(block[:128], slice(0, 128)).astype(bf16)
        tail = silu(block[128:], slice(128, 256))
        for g in range(4):
            low = pltpu.roll(tail, (128 - 32 * g) % 128, 1).astype(bf16)
            for h in range(2):
                r = 2 * g + h
                at = pl.ds(pl.multiple_of(r * 128 + xx * 32 + side * TC, TC), TC)
                hidden[y][at, 0:128] = main[r * TC : (r + 1) * TC]
                hidden[y][at, 128:256] = low[h * TC : (h + 1) * TC]

    for peer in range(PEERS):
        xx, y = peer // NY, peer % NY
        tail = own_ref[peer, 288:320].astype(f32)
        for g in range(4):
            main = own_ref[peer, 160 + 32 * g : 192 + 32 * g].astype(f32)
            for side in range(2):
                value = cot_rows(main, tail, g, side).astype(bf16)
                for h in range(2):
                    at = (y * TR + 2 * g + h + 1) * 128 + xx * 32 + side * TC
                    strips[at : at + TC] = value[h * TC : (h + 1) * TC]
    z = z_ref[0]
    for start, peer, there in ((0, jnp.maximum(z - 1, 0), z > 0),
                               ((ROWS + 1) * 128, jnp.minimum(z + 1, NZ - 1), z < NZ - 1)):
        got = jnp.where(there, edge_ref[peer].astype(f32), 0.0)
        for xx in range(NX):
            for side in range(2):
                at = start + xx * 32 + side * TC
                value = cot_rows(got[16 + 16 * xx : 32 + 16 * xx], got[80:], xx, side)
                strips[at : at + TC] = value.astype(bf16)
    lane = lax.broadcasted_iota(jnp.int32, (NQ, 128), 1)
    for row in range(ROWS + 2):
        at = slice(row * 128, (row + 1) * 128)
        turned = strips[at].astype(f32).T[:NQ]
        before = jnp.where(lane == 0, 0.0, pltpu.roll(turned, 1, 1))
        after = jnp.where(lane == 127, 0.0, pltpu.roll(turned, 127, 1))
        cot3[0:NQ, at] = after.astype(bf16)
        cot3[NQ : 2 * NQ, at] = turned.astype(bf16)
        cot3[2 * NQ : 3 * NQ, at] = before.astype(bf16)
    cot3[3 * NQ :] = jnp.zeros((16, (ROWS + 2) * 128), bf16)
    copies[0].wait()
    for y in range(NY):
        for peer in range(y, PEERS, NY):
            put(own_ref[peer, :F_ROWS], peer, core)
            put(other_ref[peer], peer, 1 - core)
        for i in range(3):
            at = (2 - i + y * TR) * 128
            part = jnp.dot(cot3[:, at : at + TR * 128], hidden[y][...], preferred_element_type=f32)
            if y == 0:
                totals[i] = part
            else:
                totals[i] += part
    rest[...] = jnp.zeros_like(rest)
    for i in range(3):
        turned = totals[i].T
        for z in range(NZ):
            out_ref[z, 16 * i : 16 * i + 16] = turned[16 * z : 16 * z + 16].astype(bf16)
            rest[z, 4 * i : 4 * i + 4] = turned[128 + 4 * z : 132 + 4 * z]
    for z in range(NZ):
        out_ref[z, 48:64] = rest[z].astype(bf16)


def join_kernel(sums_ref, terms_ref, out_ref):
    value = sums_ref[0]
    for p in range(1, 2 * PEERS):
        value = value + sums_ref[p]
    high, middle, _ = three(value)
    lane = lax.broadcasted_iota(jnp.int32, (16, 128), 1)
    row = lax.broadcasted_iota(jnp.int32, (16, 128), 0)
    tails = [
        jnp.concatenate([pltpu.roll(middle, (112 - 16 * c) % 128, 1) for c in (2 * k, 2 * k + 1)], axis=0)
        for k in range(4)
    ]
    for z in range(NZ):
        for k in range(4):
            at = slice(16 * k, 16 * k + 16)
            block = terms_ref[z, at].astype(f32)
            left, right = block[:, :128], block[:, 128:]
            right = jnp.where(lane >= 112, tails[k], right)
            if k == 3:
                left = jnp.concatenate([left[:12], high[:4]], axis=0)
                right = jnp.where(row == 13, high[4:5], right)
            out_ref[z, at] = jnp.concatenate([left, right], axis=1).astype(bf16)


def final_kernel(core_ref, got_ref, other_ref, both_ref, da_ref, row_ref, gain_ref,
                 grad_ref, gain_grad_ref, shift_grad_ref):
    lane = lax.broadcasted_iota(jnp.int32, (8, 128), 1)

    def total(ref):
        out = ref[0].astype(f32)
        for z in range(1, NZ):
            out = out + ref[z].astype(f32)
        high = jnp.concatenate([out[60:64, :128], out[61:62, 128:]], axis=0)
        middle = jnp.zeros((8, 128), f32)
        for c in range(8):
            part = pltpu.roll(out[8 * c : 8 * c + 8, 128:], (16 * c - 112) % 128, 1)
            middle = jnp.where(lane // 16 == c, part, middle)
        return unfold(high + middle[:5])

    own, other = total(got_ref), total(other_ref)
    lower = core_ref[0] == 0
    sums = (jnp.where(lower, own, other), jnp.where(lower, other, own))
    shift_grad_ref[...], gain_grad_ref[...] = [value.reshape(C) for value in sums]
    groups = group_matrix()
    gain, mean, rstd = gain_ref[...], row_ref[0:1], row_ref[1:2]

    both = jnp.concatenate([gain * sums[0], gain * sums[1], jnp.zeros((6, C), f32)], axis=0)
    both = exact_dot(exact_dot(both, groups, 0), groups, 1) / TOTAL
    first, second = both[0:1], both[1:2]
    xhat = (both_ref[:PIX].astype(f32) - mean) * rstd
    grad_ref[...] = (rstd * (da_ref[...] * gain - first - xhat * second)).astype(bf16)


def gather_kernel(got_ref, weight_ref):
    weight = got_ref[0].astype(f32)
    for z in range(1, NZ):
        weight = weight + got_ref[z].astype(f32)
    for i in range(3):
        for j in range(3):
            at = slice(j * NQ, (j + 1) * NQ)
            weight_ref[i, j, 0:16] = weight[16 * i : 16 * i + 16, at]
            weight_ref[i, j, 16:20] = weight[48 + 4 * i : 52 + 4 * i, at]


def flip(value):
    return lax.ppermute(value, "core", [(0, 1), (1, 0)])


def shape(dims, dtype):
    return jax.ShapeDtypeStruct(dims, dtype)


def body(features, cotangent, conv_weight, gain, shift):
    core, y, z = lax.axis_index("core"), lax.axis_index("y"), lax.axis_index("z")
    at_core, at_y, at_z = core.reshape(1), y.reshape(1), z.reshape(1)
    feat, cot = features.reshape(PIX, C), cotangent.reshape(PIX, C)
    gain, shift = gain.reshape(1, C), shift.reshape(1, C)
    cot2, feat2 = flip(cot), flip(feat)
    both = jnp.concatenate([feat, cot])
    edge = jnp.where(
        core == 0,
        jnp.concatenate([cot[PIX - TC :], cot2[PIX - TC :]]),
        jnp.concatenate([cot2[:TC], cot[:TC]]),
    )
    count = NZ * NY
    ways = [(2 * k, 2 * k + 2) for k in range(count - 1)] + [(2 * k + 3, 2 * k + 1) for k in range(count - 1)]
    mine = lax.ppermute(edge, ("z", "y", "core"), ways)

    packed = pl.pallas_call(
        pack_kernel,
        out_shape=shape((PEERS, G_ROWS, 128), bf16),
        in_specs=[smem()] + [vmem()] * 3,
        out_specs=hbm(),
        scratch_shapes=[pltpu.VMEM((PEERS, G_ROWS, 128), bf16), pltpu.SemaphoreType.DMA((2,))],
        compiler_params=params(),
        cost_estimate=pl.CostEstimate(flops=1 << 28, bytes_accessed=2 << 20, transcendentals=0),
        name="pack",
    )(at_core, both, feat2, cot2)
    slab = lax.all_to_all(packed, ("x", "y"), 0, 0)
    theirs = flip(mine)
    side, shifted = pl.pallas_call(
        side_kernel,
        out_shape=(shape((TR, C), f32), shape((3, (TR + 2) * TC, C), bf16)),
        in_specs=[smem()] + [vmem()] * 4 + [hbm()],
        out_specs=(vmem(), vmem()),
        scratch_shapes=[pltpu.VMEM((3, C, C), bf16), pltpu.SemaphoreType.DMA((3,))],
        compiler_params=params(),
        name="side",
    )(at_core, both, cot2, mine, theirs, conv_weight)
    slab, side = lax.optimization_barrier((slab, side))
    pairs = [(2 * k + 1, 2 * k + 2) for k in range(NX - 1)]
    side = lax.ppermute(side, ("x", "core"), pairs + [(b, a) for a, b in pairs])
    edges = pl.pallas_call(
        split_kernel,
        out_shape=shape((NZ, E_ROWS, 128), bf16),
        in_specs=[smem(), vmem()],
        out_specs=vmem(),
        compiler_params=params(),
        name="split",
    )(at_z, slab)
    late, edges = lax.optimization_barrier((slab, edges))
    slab_other = flip(late)
    edges = lax.all_to_all(edges, "z", 0, 0)
    back = pl.pallas_call(
        back_kernel,
        out_shape=shape((PIX, C), f32),
        in_specs=[vmem(), hbm()],
        out_specs=vmem(),
        scratch_shapes=[pltpu.VMEM((9, C, C), bf16), pltpu.SemaphoreType.DMA((9,))],
        compiler_params=params(),
        cost_estimate=pl.CostEstimate(flops=2 * PIX * 9 * C * C, bytes_accessed=18 * C * C, transcendentals=0),
        name="back",
    )(shifted, conv_weight)
    row, da, table, sums, bias_grad = pl.pallas_call(
        sums_kernel,
        out_shape=(
            shape((8, C), f32),
            shape((PIX, C), f32),
            shape((8, 256), f32),
            shape((2 * PEERS, 8, 128), f32),
            shape((C,), f32),
        ),
        in_specs=[smem()] * 2 + [vmem()] * 6,
        out_specs=(vmem(),) * 5,
        compiler_params=params(),
        name="sums",
    )(at_core, at_y, edges, both, back, side, gain, shift)
    sums = lax.all_to_all(sums, ("y", "x", "core"), 0, 0)

    terms = pl.pallas_call(
        terms_kernel,
        out_shape=shape((NZ, W_ROWS, 256), bf16),
        in_specs=[smem()] * 2 + [vmem(), hbm(), vmem(), vmem()],
        out_specs=vmem(),
        scratch_shapes=[
            pltpu.VMEM((TR * 128, 256), bf16),
            pltpu.VMEM((TR * 128, 256), bf16),
            pltpu.VMEM((TR * 128, 256), bf16),
            pltpu.VMEM((TR * 128, 256), bf16),
            pltpu.VMEM(((ROWS + 2) * 128, 128), bf16),
            pltpu.VMEM((256, (ROWS + 2) * 128), bf16),
            pltpu.VMEM((NZ, 16, 256), f32),
            pltpu.VMEM((3, 256, 256), f32),
            pltpu.VMEM((PEERS, F_ROWS, 128), bf16),
            pltpu.SemaphoreType.DMA((1,)),
        ],
        compiler_params=params(),
        cost_estimate=pl.CostEstimate(
            flops=2 * PIX * 9 * C * C, bytes_accessed=4 << 20, transcendentals=ROWS * 128 * 256
        ),
        name="terms",
    )(at_core, at_z, slab, slab_other, edges, table)

    joined = pl.pallas_call(
        join_kernel,
        out_shape=shape((NZ, W_ROWS, 256), bf16),
        in_specs=[vmem()] * 2,
        out_specs=vmem(),
        compiler_params=params(),
        name="join",
    )(sums, terms)
    joined = lax.all_to_all(joined, "z", 0, 0)
    weight_grad = pl.pallas_call(
        gather_kernel,
        out_shape=shape((3, 3, 20, NQ), f32),
        in_specs=[vmem()],
        out_specs=vmem(),
        compiler_params=params(),
        cost_estimate=pl.CostEstimate(flops=1 << 22, bytes_accessed=1 << 20, transcendentals=0),
        name="gather",
    )(joined)
    grad, gain_grad, shift_grad = pl.pallas_call(
        final_kernel,
        out_shape=(shape((PIX, C), bf16),) + (shape((C,), f32),) * 2,
        in_specs=[smem()] + [vmem()] * 6,
        out_specs=(vmem(),) * 3,
        compiler_params=params(),
        name="final",
    )(at_core, joined, flip(joined), both, da, row, gain)
    return grad.reshape(features.shape), weight_grad, gain_grad, shift_grad, bias_grad


def solution(mesh):
    grid = Mesh(mesh.devices.reshape(NZ, NY, NX, 2), ("z", "y", "x", "core"))
    rows, cols = ("z", "y"), ("x", "core")
    tiled = P(rows, cols, None)
    return jax.shard_map(
        body,
        mesh=grid,
        in_specs=(tiled, tiled, P(), P(), P()),
        out_specs=(tiled, P(None, None, rows, cols), P(), P(), P()),
        check_vma=False,
    )
```

```python
import jax
import jax.numpy as jnp
from jax import lax
from jax.experimental import pallas as pl
from jax.experimental.pallas import tpu as pltpu
from jax.sharding import Mesh
from jax.sharding import PartitionSpec as P

C = 640
GW = 40
TR, TC = 8, 16
PIX = TR * TC
NZ, NY, NX = 8, 4, 4
PEERS = NY * NX
ROWS = NY * TR
NQ = 80
CHIP = float(2 * PIX * GW)
TOTAL = float(NZ * PEERS) * CHIP
VMEM_LIMIT = 48 * 1024 * 1024
F_ROWS, C_ROWS, S_ROWS = 160, 160, 16
S_AT = F_ROWS + C_ROWS
G_ROWS = S_AT + S_ROWS
E_ROWS = 96
W_ROWS = 64
f32, bf16 = jnp.float32, jnp.bfloat16


def lanes(count):
    return lax.broadcasted_iota(jnp.int32, (1, count), 1)


def slab_channel(main, at):
    z = jnp.where(main, at >> 4, at >> 2)
    return z * 80 + jnp.where(main, at & 15, 16 + (at & 3))


def feature_columns():
    lane = lanes(C)
    main = lane < 512
    y = jnp.where(main, lane >> 7, (lane - 512) >> 5)
    return slab_channel(main, jnp.where(main, lane & 127, lane & 31)) + y * 20


def cotangent_columns(core, side):
    lane = lanes(C)
    main = lane < 512
    x = jnp.where(main, lane >> 7, (lane - 512) >> 5)
    at = jnp.where(main, lane & 127, lane & 31)
    q = jnp.where(main, at & 63, 64 + (at & 15))
    mine = jnp.where(main, at >> 6, at >> 4) == side
    return jnp.where(mine, x * 160 + core * NQ + q, -1)


def term_columns(y):
    lane = lanes(256)
    main = lane < 128
    return slab_channel(main, jnp.where(main, lane, lane & 31)) + y * 20


def vmem():
    return pl.BlockSpec(memory_space=pltpu.VMEM)


def smem():
    return pl.BlockSpec(memory_space=pltpu.SMEM)


def hbm():
    return pl.BlockSpec(memory_space=pltpu.HBM)


def fetch(pairs, sem):
    copies = [pltpu.make_async_copy(src, dst, sem.at[k]) for k, (src, dst) in enumerate(pairs)]
    for copy in copies:
        copy.start()
    return copies


def params(**kw):
    return pltpu.CompilerParams(vmem_limit_bytes=VMEM_LIMIT, **kw)


def group_matrix():
    chan = lax.broadcasted_iota(jnp.int32, (C, 128), 0)
    low = lax.broadcasted_iota(jnp.int32, (C, 128), 1) * GW
    return jnp.where((chan >= low) & (chan < low + GW), 1.0, 0.0).astype(bf16)


def exact_dot(value, matrix, over):
    high, middle, low = three(value)
    stacked = jnp.concatenate([high, middle, low, jnp.zeros_like(low)], axis=0).astype(bf16)
    out = lax.dot_general(stacked, matrix, (((1,), (over,)), ((), ())), preferred_element_type=f32)
    return out[0:8] + out[8:16] + out[16:24]


def rows8(row):
    return jnp.broadcast_to(row, (8, row.shape[1]))


def pick(columns):
    rows = lax.broadcasted_iota(jnp.int32, (C, columns.shape[1]), 0)
    return (rows == columns).astype(f32).astype(bf16)


def sigmoid(value):
    return 0.5 * jnp.tanh(0.5 * value) + 0.5


def fold(row):
    return jnp.concatenate([row[:, 128 * t : 128 * t + 128] for t in range(5)], axis=0)


def unfold(rows):
    return jnp.concatenate([rows[t : t + 1] for t in range(5)], axis=1)


def three(value):
    high = value.astype(bf16).astype(f32)
    rest = value - high
    middle = rest.astype(bf16).astype(f32)
    return high, middle, rest - middle


def lanes32(value, height):
    group = lax.broadcasted_iota(jnp.int32, (height, 128), 1) // 32
    out = []
    for a in range(4):
        acc = jnp.zeros((height, 128), f32)
        for g in range(4):
            moved = pltpu.roll(value[height * g : height * (g + 1)], (32 * (g - a)) % 128, 1)
            acc = jnp.where(group == g, moved, acc)
        out.append(acc)
    return out


def put_pieces(mean, squares, bias):
    high, middle, _ = three(bias)
    rows = three(mean) + three(squares) + (high, middle)
    return jnp.concatenate(list(rows), axis=0).astype(bf16)


def merge_pieces(got, count):
    got = got.astype(f32)
    mean, squares = merge(got[:, 0] + got[:, 1] + got[:, 2], got[:, 3] + got[:, 4] + got[:, 5], count)
    total = got[0]
    for p in range(1, got.shape[0]):
        total = total + got[p]
    return mean, squares, total[6:11] + total[11:16]


def in_order(core, own, other):
    a, b = own[...].astype(f32), other[...].astype(f32)
    return jnp.where(core == 0, a, b).astype(bf16), jnp.where(core == 0, b, a).astype(bf16)


def blocks(core, first, second):
    return jnp.dot(first, pick(cotangent_columns(core, 0)), preferred_element_type=f32) + jnp.dot(
        second, pick(cotangent_columns(core, 1)), preferred_element_type=f32
    )


def pack_kernel(core_ref, both_ref, feat2_ref, cot2_ref, out_hbm, out_ref, sem):
    core = core_ref[0]
    feat_ref, cot_ref = both_ref.at[:PIX], both_ref.at[PIX:]
    x, x2 = feat_ref[...].astype(f32), feat2_ref[...].astype(f32)
    groups = group_matrix()
    total = x.sum(0, keepdims=True) + x2.sum(0, keepdims=True)
    mean = exact_dot(rows8(total), groups, 0) / CHIP
    wide = exact_dot(mean, groups, 1)[:1]
    squares = ((x - wide) ** 2).sum(0, keepdims=True) + ((x2 - wide) ** 2).sum(0, keepdims=True)
    bias = cot_ref[...].astype(f32).sum(0, keepdims=True) + cot2_ref[...].astype(f32).sum(0, keepdims=True)
    stats = put_pieces(mean[:1], exact_dot(rows8(squares), groups, 0)[:1], fold(bias))
    moved = jnp.dot(feat_ref[...], pick(feature_columns()), preferred_element_type=f32)
    moved_rest = lanes32(moved[:, 512:], 32)
    for p in range(PEERS):
        y = p % NY
        out_ref[p, 0:128] = moved[:, y * 128 : (y + 1) * 128].astype(bf16)
        out_ref[p, 128:160] = moved_rest[y].astype(bf16)
    copies = fetch(((out_ref.at[:, :F_ROWS, :], out_hbm.at[:, :F_ROWS, :]),), sem.at[0:1])
    first, second = in_order(core, cot_ref, cot2_ref)
    terms = blocks(core, first, second)
    terms_rest = lanes32(terms[:, 512:], 32)
    for p in range(PEERS):
        xx = p // NY
        out_ref[p, 160:288] = terms[:, xx * 128 : (xx + 1) * 128].astype(bf16)
        out_ref[p, 288:320] = terms_rest[xx].astype(bf16)
        out_ref[p, S_AT:] = stats
    copies += fetch(((out_ref.at[:, F_ROWS:, :], out_hbm.at[:, F_ROWS:, :]),), sem.at[1:2])
    for copy in copies:
        copy.wait()


def merge(means, squares, count):
    n = means.shape[0]
    mean = means.sum(0, keepdims=True) / n
    return mean, squares.sum(0, keepdims=True) + count * ((means - mean) ** 2).sum(0, keepdims=True)


def cot_rows(main, rest, g, side):
    lane = lax.broadcasted_iota(jnp.int32, main.shape, 1)
    main = pltpu.roll(main, 64, 1) if side else main
    return jnp.where(lane < 64, main, pltpu.roll(rest, (64 - 32 * g - 16 * side) % 128, 1))


def split_kernel(z_ref, slab_ref, out_ref):
    stats = put_pieces(*merge_pieces(slab_ref[:, S_AT:], CHIP))
    group = lax.broadcasted_iota(jnp.int32, (TC, 128), 1) // 32
    first, last = jnp.zeros((TC, 128), f32), jnp.zeros((TC, 128), f32)
    for xx in range(NX):
        tail = slab_ref[xx * NY, 288:304].astype(f32)
        first = jnp.where(group == xx, pltpu.roll(tail, 32 * xx, 1) if xx else tail, first)
        tail = slab_ref[xx * NY + NY - 1, 304:320].astype(f32)
        last = jnp.where(group == xx, pltpu.roll(tail, (32 * xx + 32) % 128, 1) if xx < 3 else tail, last)
    first = jnp.concatenate([slab_ref[xx * NY, 160:176].astype(f32) for xx in range(NX)] + [first], axis=0)
    last = jnp.concatenate(
        [slab_ref[xx * NY + NY - 1, 272:288].astype(f32) for xx in range(NX)] + [last], axis=0
    )
    for p in range(NZ):
        out_ref[p, :S_ROWS] = stats
        out_ref[p, S_ROWS:] = jnp.where(z_ref[0] < p, last, first).astype(bf16)


def back_kernel(shifted, w_hbm, out_ref, w_ref, sem):
    copies = fetch([(w_hbm.at[t // 3, t % 3], w_ref.at[t]) for t in range(9)], sem)
    total = None
    for i in range(3):
        for copy in copies[3 * i : 3 * i + 3]:
            copy.wait()
        for j in range(3):
            pixels = shifted[2 - j, (2 - i) * TC : (2 - i) * TC + PIX]
            part = lax.dot_general(w_ref[3 * i + j], pixels, (((1,), (1,)), ((), ())), preferred_element_type=f32)
            total = part if total is None else total + part
    out_ref[...] = total.T


def side_kernel(core_ref, both_ref, cot2_ref, mine_ref, theirs_ref, w_hbm, out_ref, shifted, w_ref, sem):
    j = 2 * core_ref[0]
    copies = fetch([(w_hbm.at[i, j], w_ref.at[i]) for i in range(3)], sem)
    lower = core_ref[0] == 0
    rows = (TR + 2) * TC
    mine, theirs = mine_ref[...].astype(f32), theirs_ref[...].astype(f32)
    top, bottom = jnp.where(lower, mine, theirs), jnp.where(lower, theirs, mine)
    own_top, other_top = jnp.where(lower, top[:TC], top[TC:]), jnp.where(lower, top[TC:], top[:TC])
    own_bot, other_bot = jnp.where(lower, bottom[:TC], bottom[TC:]), jnp.where(lower, bottom[TC:], bottom[:TC])
    wide = jnp.concatenate([own_top, both_ref[PIX:].astype(f32), own_bot], axis=0)
    near = jnp.concatenate([other_top, cot2_ref[...].astype(f32), other_bot], axis=0)
    near = near.reshape(TR + 2, TC, C)
    inner = jnp.where(lower, near[:, :1], near[:, TC - 1 :])
    left, right = jnp.where(lower, 0.0, inner), jnp.where(lower, inner, 0.0)
    left = jnp.broadcast_to(left, (TR + 2, TC, C)).reshape(rows, C)
    right = jnp.broadcast_to(right, (TR + 2, TC, C)).reshape(rows, C)
    col = lax.broadcasted_iota(jnp.int32, (rows, C), 0) % TC
    shifted[0] = jnp.where(col == 0, left, pltpu.roll(wide, 1, 0)).astype(bf16)
    shifted[1] = wide.astype(bf16)
    shifted[2] = jnp.where(col == TC - 1, right, pltpu.roll(wide, rows - 1, 0)).astype(bf16)
    column = wide.reshape(TR + 2, TC, C)
    column = jnp.where(lower, column[:, :1], column[:, TC - 1 :])
    total = jnp.zeros((TR, C), f32)
    for i in range(3):
        copies[i].wait()
        pixels = column[2 - i : 2 - i + TR].reshape(TR, C).astype(bf16)
        total = total + lax.dot_general(
            pixels, w_ref[i], (((1,), (1,)), ((), ())), preferred_element_type=f32
        )
    out_ref[...] = total


def sums_kernel(core_ref, y_ref, stat_ref, both_ref, back_ref, side_ref, gain_ref, shift_ref,
                row_ref, da_ref, par_ref, out_ref, bias_ref):
    mean, squares, bias = merge_pieces(stat_ref[:, :S_ROWS], PEERS * CHIP)
    bias_ref[...] = unfold(bias).reshape(C)
    groups = group_matrix()
    both = jnp.concatenate([mean, lax.rsqrt(squares / TOTAL + 1e-05), jnp.zeros((6, 128), f32)], axis=0)
    both = exact_dot(both, groups, 1)
    mean, rstd = both[0:1], both[1:2]
    gain, shift = gain_ref[...], shift_ref[...]
    row = lax.broadcasted_iota(jnp.int32, (8, C), 0)
    row_ref[...] = jnp.where(row == 0, mean, rstd)
    table = jnp.where(row == 0, mean, jnp.where(row == 1, rstd * gain, jnp.where(row == 2, shift, 0.0)))
    par_ref[...] = exact_dot(table, pick(term_columns(y_ref[0])), 0)
    xhat = (both_ref[:PIX].astype(f32) - mean) * rstd
    act = xhat * gain + shift
    sig = sigmoid(act)
    column = lax.broadcasted_iota(jnp.int32, (TR, TC, C), 1)
    side = jnp.broadcast_to(side_ref[...][:, None, :], (TR, TC, C))
    side = jnp.where(column == core_ref[0] * (TC - 1), side, 0.0).reshape(PIX, C)
    da = (back_ref[...] + side) * sig * (1.0 + act * (1.0 - sig))
    da_ref[...] = da
    empty = jnp.zeros((3, 128), f32)
    for side, value in enumerate((da, da * xhat)):
        block = jnp.concatenate([fold(value.sum(0, keepdims=True)), empty], axis=0)
        for p in range(side, 2 * PEERS, 2):
            out_ref[p] = block


def terms_kernel(core_ref, z_ref, own_ref, other_hbm, edge_ref, par_ref, out_ref,
                 hid0, hid1, hid2, hid3, strips, cot3, rest, totals, other_ref, sem):
    hidden = (hid0, hid1, hid2, hid3)
    copies = fetch(((other_hbm.at[:, :F_ROWS, :], other_ref),), sem)
    core = core_ref[0]

    def put(block, peer, side):
        xx, y = peer // NY, peer % NY

        def silu(x, lanes):
            a = (x.astype(f32) - par_ref[0:1, lanes]) * par_ref[1:2, lanes] + par_ref[2:3, lanes]
            return a * sigmoid(a)

        main = silu(block[:128], slice(0, 128)).astype(bf16)
        tail = silu(block[128:], slice(128, 256))
        for g in range(4):
            low = pltpu.roll(tail, (128 - 32 * g) % 128, 1).astype(bf16)
            for h in range(2):
                r = 2 * g + h
                at = pl.ds(pl.multiple_of(r * 128 + xx * 32 + side * TC, TC), TC)
                hidden[y][at, 0:128] = main[r * TC : (r + 1) * TC]
                hidden[y][at, 128:256] = low[h * TC : (h + 1) * TC]

    for peer in range(PEERS):
        xx, y = peer // NY, peer % NY
        tail = own_ref[peer, 288:320].astype(f32)
        for g in range(4):
            main = own_ref[peer, 160 + 32 * g : 192 + 32 * g].astype(f32)
            for side in range(2):
                value = cot_rows(main, tail, g, side).astype(bf16)
                for h in range(2):
                    at = (y * TR + 2 * g + h + 1) * 128 + xx * 32 + side * TC
                    strips[at : at + TC] = value[h * TC : (h + 1) * TC]
    z = z_ref[0]
    for start, peer, there in ((0, jnp.maximum(z - 1, 0), z > 0),
                               ((ROWS + 1) * 128, jnp.minimum(z + 1, NZ - 1), z < NZ - 1)):
        got = jnp.where(there, edge_ref[peer].astype(f32), 0.0)
        for xx in range(NX):
            for side in range(2):
                at = start + xx * 32 + side * TC
                value = cot_rows(got[16 + 16 * xx : 32 + 16 * xx], got[80:], xx, side)
                strips[at : at + TC] = value.astype(bf16)
    lane = lax.broadcasted_iota(jnp.int32, (NQ, 128), 1)
    for row in range(ROWS + 2):
        at = slice(row * 128, (row + 1) * 128)
        turned = strips[at].astype(f32).T[:NQ]
        before = jnp.where(lane == 0, 0.0, pltpu.roll(turned, 1, 1))
        after = jnp.where(lane == 127, 0.0, pltpu.roll(turned, 127, 1))
        cot3[0:NQ, at] = after.astype(bf16)
        cot3[NQ : 2 * NQ, at] = turned.astype(bf16)
        cot3[2 * NQ : 3 * NQ, at] = before.astype(bf16)
    cot3[3 * NQ :] = jnp.zeros((16, (ROWS + 2) * 128), bf16)
    copies[0].wait()
    for y in range(NY):
        for peer in range(y, PEERS, NY):
            put(own_ref[peer, :F_ROWS], peer, core)
            put(other_ref[peer], peer, 1 - core)
        for i in range(3):
            at = (2 - i + y * TR) * 128
            part = jnp.dot(cot3[:, at : at + TR * 128], hidden[y][...], preferred_element_type=f32)
            if y == 0:
                totals[i] = part
            else:
                totals[i] += part
    rest[...] = jnp.zeros_like(rest)
    for i in range(3):
        turned = totals[i].T
        for z in range(NZ):
            out_ref[z, 16 * i : 16 * i + 16] = turned[16 * z : 16 * z + 16].astype(bf16)
            rest[z, 4 * i : 4 * i + 4] = turned[128 + 4 * z : 132 + 4 * z]
    for z in range(NZ):
        out_ref[z, 48:64] = rest[z].astype(bf16)


def join_kernel(sums_ref, terms_ref, out_ref):
    value = sums_ref[0]
    for p in range(1, 2 * PEERS):
        value = value + sums_ref[p]
    high, middle, _ = three(value)
    lane = lax.broadcasted_iota(jnp.int32, (16, 128), 1)
    row = lax.broadcasted_iota(jnp.int32, (16, 128), 0)
    tails = [
        jnp.concatenate([pltpu.roll(middle, (112 - 16 * c) % 128, 1) for c in (2 * k, 2 * k + 1)], axis=0)
        for k in range(4)
    ]
    for z in range(NZ):
        for k in range(4):
            at = slice(16 * k, 16 * k + 16)
            block = terms_ref[z, at].astype(f32)
            left, right = block[:, :128], block[:, 128:]
            right = jnp.where(lane >= 112, tails[k], right)
            if k == 3:
                left = jnp.concatenate([left[:12], high[:4]], axis=0)
                right = jnp.where(row == 13, high[4:5], right)
            out_ref[z, at] = jnp.concatenate([left, right], axis=1).astype(bf16)


def total_kernel(got_ref, out_ref):
    lane = lax.broadcasted_iota(jnp.int32, (8, 128), 1)
    middle = jnp.zeros((8, 128), f32)
    upper, right = got_ref[0, 48:].astype(f32), got_ref[0, :, 128:].astype(f32)
    for z in range(1, NZ):
        upper = upper + got_ref[z, 48:].astype(f32)
        right = right + got_ref[z, :, 128:].astype(f32)
    high = jnp.concatenate([upper[12:16, :128], upper[13:14, 128:]], axis=0)
    for c in range(8):
        part = pltpu.roll(right[8 * c : 8 * c + 8], (16 * c - 112) % 128, 1)
        middle = jnp.where(lane // 16 == c, part, middle)
    out_ref[...] = rows8(unfold(high + middle[:5]))


def final_kernel(core_ref, own_ref, other_ref, both_ref, da_ref, row_ref, gain_ref,
                 grad_ref, gain_grad_ref, shift_grad_ref):
    own, other = own_ref[0:1], other_ref[0:1]
    lower = core_ref[0] == 0
    sums = (jnp.where(lower, own, other), jnp.where(lower, other, own))
    shift_grad_ref[...], gain_grad_ref[...] = [value.reshape(C) for value in sums]
    groups = group_matrix()
    gain, mean, rstd = gain_ref[...], row_ref[0:1], row_ref[1:2]

    both = jnp.concatenate([gain * sums[0], gain * sums[1], jnp.zeros((6, C), f32)], axis=0)
    both = exact_dot(exact_dot(both, groups, 0), groups, 1) / TOTAL
    first, second = both[0:1], both[1:2]
    xhat = (both_ref[:PIX].astype(f32) - mean) * rstd
    grad_ref[...] = (rstd * (da_ref[...] * gain - first - xhat * second)).astype(bf16)


def gather_kernel(got_ref, weight_ref):
    weight = got_ref[0].astype(f32)
    for z in range(1, NZ):
        weight = weight + got_ref[z].astype(f32)
    for i in range(3):
        for j in range(3):
            at = slice(j * NQ, (j + 1) * NQ)
            weight_ref[i, j, 0:16] = weight[16 * i : 16 * i + 16, at]
            weight_ref[i, j, 16:20] = weight[48 + 4 * i : 52 + 4 * i, at]


def flip(value):
    return lax.ppermute(value, "core", [(0, 1), (1, 0)])


def shape(dims, dtype):
    return jax.ShapeDtypeStruct(dims, dtype)


def body(features, cotangent, conv_weight, gain, shift):
    core, y, z = lax.axis_index("core"), lax.axis_index("y"), lax.axis_index("z")
    at_core, at_y, at_z = core.reshape(1), y.reshape(1), z.reshape(1)
    feat, cot = features.reshape(PIX, C), cotangent.reshape(PIX, C)
    gain, shift = gain.reshape(1, C), shift.reshape(1, C)
    cot2, feat2 = flip(cot), flip(feat)
    both = jnp.concatenate([feat, cot])
    edge = jnp.where(
        core == 0,
        jnp.concatenate([cot[PIX - TC :], cot2[PIX - TC :]]),
        jnp.concatenate([cot2[:TC], cot[:TC]]),
    )
    count = NZ * NY
    ways = [(2 * k, 2 * k + 2) for k in range(count - 1)] + [(2 * k + 3, 2 * k + 1) for k in range(count - 1)]
    mine = lax.ppermute(edge, ("z", "y", "core"), ways)

    packed = pl.pallas_call(
        pack_kernel,
        out_shape=shape((PEERS, G_ROWS, 128), bf16),
        in_specs=[smem()] + [vmem()] * 3,
        out_specs=hbm(),
        scratch_shapes=[pltpu.VMEM((PEERS, G_ROWS, 128), bf16), pltpu.SemaphoreType.DMA((2,))],
        compiler_params=params(),
        cost_estimate=pl.CostEstimate(flops=1 << 28, bytes_accessed=2 << 20, transcendentals=0),
        name="pack",
    )(at_core, both, feat2, cot2)
    slab = lax.all_to_all(packed, ("x", "y"), 0, 0)
    theirs = flip(mine)
    side, shifted = pl.pallas_call(
        side_kernel,
        out_shape=(shape((TR, C), f32), shape((3, (TR + 2) * TC, C), bf16)),
        in_specs=[smem()] + [vmem()] * 4 + [hbm()],
        out_specs=(vmem(), vmem()),
        scratch_shapes=[pltpu.VMEM((3, C, C), bf16), pltpu.SemaphoreType.DMA((3,))],
        compiler_params=params(),
        name="side",
    )(at_core, both, cot2, mine, theirs, conv_weight)
    slab, side = lax.optimization_barrier((slab, side))
    pairs = [(2 * k + 1, 2 * k + 2) for k in range(NX - 1)]
    side = lax.ppermute(side, ("x", "core"), pairs + [(b, a) for a, b in pairs])
    edges = pl.pallas_call(
        split_kernel,
        out_shape=shape((NZ, E_ROWS, 128), bf16),
        in_specs=[smem(), vmem()],
        out_specs=vmem(),
        compiler_params=params(),
        name="split",
    )(at_z, slab)
    late, edges = lax.optimization_barrier((slab, edges))
    slab_other = flip(late)
    edges = lax.all_to_all(edges, "z", 0, 0)
    back = pl.pallas_call(
        back_kernel,
        out_shape=shape((PIX, C), f32),
        in_specs=[vmem(), hbm()],
        out_specs=vmem(),
        scratch_shapes=[pltpu.VMEM((9, C, C), bf16), pltpu.SemaphoreType.DMA((9,))],
        compiler_params=params(),
        cost_estimate=pl.CostEstimate(flops=2 * PIX * 9 * C * C, bytes_accessed=18 * C * C, transcendentals=0),
        name="back",
    )(shifted, conv_weight)
    row, da, table, sums, bias_grad = pl.pallas_call(
        sums_kernel,
        out_shape=(
            shape((8, C), f32),
            shape((PIX, C), f32),
            shape((8, 256), f32),
            shape((2 * PEERS, 8, 128), f32),
            shape((C,), f32),
        ),
        in_specs=[smem()] * 2 + [vmem()] * 6,
        out_specs=(vmem(),) * 5,
        compiler_params=params(),
        name="sums",
    )(at_core, at_y, edges, both, back, side, gain, shift)
    sums = lax.all_to_all(sums, ("y", "x", "core"), 0, 0)

    terms = pl.pallas_call(
        terms_kernel,
        out_shape=shape((NZ, W_ROWS, 256), bf16),
        in_specs=[smem()] * 2 + [vmem(), hbm(), vmem(), vmem()],
        out_specs=vmem(),
        scratch_shapes=[
            pltpu.VMEM((TR * 128, 256), bf16),
            pltpu.VMEM((TR * 128, 256), bf16),
            pltpu.VMEM((TR * 128, 256), bf16),
            pltpu.VMEM((TR * 128, 256), bf16),
            pltpu.VMEM(((ROWS + 2) * 128, 128), bf16),
            pltpu.VMEM((256, (ROWS + 2) * 128), bf16),
            pltpu.VMEM((NZ, 16, 256), f32),
            pltpu.VMEM((3, 256, 256), f32),
            pltpu.VMEM((PEERS, F_ROWS, 128), bf16),
            pltpu.SemaphoreType.DMA((1,)),
        ],
        compiler_params=params(),
        cost_estimate=pl.CostEstimate(
            flops=2 * PIX * 9 * C * C, bytes_accessed=4 << 20, transcendentals=ROWS * 128 * 256
        ),
        name="terms",
    )(at_core, at_z, slab, slab_other, edges, table)

    joined = pl.pallas_call(
        join_kernel,
        out_shape=shape((NZ, W_ROWS, 256), bf16),
        in_specs=[vmem()] * 2,
        out_specs=vmem(),
        compiler_params=params(),
        name="join",
    )(sums, terms)
    joined = lax.all_to_all(joined, "z", 0, 0)
    total = pl.pallas_call(
        total_kernel,
        out_shape=shape((8, C), f32),
        in_specs=[vmem()],
        out_specs=vmem(),
        compiler_params=params(),
        name="total",
    )(joined)
    weight_grad = pl.pallas_call(
        gather_kernel,
        out_shape=shape((3, 3, 20, NQ), f32),
        in_specs=[vmem()],
        out_specs=vmem(),
        compiler_params=params(),
        cost_estimate=pl.CostEstimate(flops=1 << 22, bytes_accessed=1 << 20, transcendentals=0),
        name="gather",
    )(joined)
    grad, gain_grad, shift_grad = pl.pallas_call(
        final_kernel,
        out_shape=(shape((PIX, C), bf16),) + (shape((C,), f32),) * 2,
        in_specs=[smem()] + [vmem()] * 6,
        out_specs=(vmem(),) * 3,
        compiler_params=params(),
        name="final",
    )(at_core, total, flip(total), both, da, row, gain)
    return grad.reshape(features.shape), weight_grad, gain_grad, shift_grad, bias_grad


def solution(mesh):
    grid = Mesh(mesh.devices.reshape(NZ, NY, NX, 2), ("z", "y", "x", "core"))
    rows, cols = ("z", "y"), ("x", "core")
    tiled = P(rows, cols, None)
    return jax.shard_map(
        body,
        mesh=grid,
        in_specs=(tiled, tiled, P(), P(), P()),
        out_specs=(tiled, P(None, None, rows, cols), P(), P(), P()),
        check_vma=False,
    )
```

```python
import jax
import jax.numpy as jnp
from jax import lax
from jax.experimental import pallas as pl
from jax.experimental.pallas import tpu as pltpu
from jax.sharding import Mesh
from jax.sharding import PartitionSpec as P

C = 640
GW = 40
TR, TC = 8, 16
PIX = TR * TC
NZ, NY, NX = 8, 4, 4
PEERS = NY * NX
ROWS = NY * TR
NQ = 80
CHIP = float(2 * PIX * GW)
TOTAL = float(NZ * PEERS) * CHIP
VMEM_LIMIT = 48 * 1024 * 1024
F_ROWS, C_ROWS, S_ROWS = 160, 160, 16
S_AT = F_ROWS + C_ROWS
G_ROWS = S_AT + S_ROWS
E_ROWS = 96
W_ROWS = 64
f32, bf16 = jnp.float32, jnp.bfloat16


def lanes(count):
    return lax.broadcasted_iota(jnp.int32, (1, count), 1)


def slab_channel(main, at):
    z = jnp.where(main, at >> 4, at >> 2)
    return z * 80 + jnp.where(main, at & 15, 16 + (at & 3))


def feature_columns():
    lane = lanes(C)
    main = lane < 512
    y = jnp.where(main, lane >> 7, (lane - 512) >> 5)
    return slab_channel(main, jnp.where(main, lane & 127, lane & 31)) + y * 20


def cotangent_columns(core, side):
    lane = lanes(C)
    main = lane < 512
    x = jnp.where(main, lane >> 7, (lane - 512) >> 5)
    at = jnp.where(main, lane & 127, lane & 31)
    q = jnp.where(main, at & 63, 64 + (at & 15))
    mine = jnp.where(main, at >> 6, at >> 4) == side
    return jnp.where(mine, x * 160 + core * NQ + q, -1)


def term_columns(y):
    lane = lanes(256)
    main = lane < 128
    return slab_channel(main, jnp.where(main, lane, lane & 31)) + y * 20


def vmem():
    return pl.BlockSpec(memory_space=pltpu.VMEM)


def smem():
    return pl.BlockSpec(memory_space=pltpu.SMEM)


def hbm():
    return pl.BlockSpec(memory_space=pltpu.HBM)


def fetch(pairs, sem):
    copies = [pltpu.make_async_copy(src, dst, sem.at[k]) for k, (src, dst) in enumerate(pairs)]
    for copy in copies:
        copy.start()
    return copies


def params(**kw):
    return pltpu.CompilerParams(vmem_limit_bytes=VMEM_LIMIT, **kw)


def group_matrix():
    chan = lax.broadcasted_iota(jnp.int32, (C, 128), 0)
    low = lax.broadcasted_iota(jnp.int32, (C, 128), 1) * GW
    return jnp.where((chan >= low) & (chan < low + GW), 1.0, 0.0).astype(bf16)


def exact_dot(value, matrix, over):
    high, middle, low = three(value)
    stacked = jnp.concatenate([high, middle, low, jnp.zeros_like(low)], axis=0).astype(bf16)
    out = lax.dot_general(stacked, matrix, (((1,), (over,)), ((), ())), preferred_element_type=f32)
    return out[0:8] + out[8:16] + out[16:24]


def rows8(row):
    return jnp.broadcast_to(row, (8, row.shape[1]))


def pick(columns):
    rows = lax.broadcasted_iota(jnp.int32, (C, columns.shape[1]), 0)
    return (rows == columns).astype(f32).astype(bf16)


def sigmoid(value):
    return 0.5 * jnp.tanh(0.5 * value) + 0.5


def fold(row):
    return jnp.concatenate([row[:, 128 * t : 128 * t + 128] for t in range(5)], axis=0)


def unfold(rows):
    return jnp.concatenate([rows[t : t + 1] for t in range(5)], axis=1)


def three(value):
    high = value.astype(bf16).astype(f32)
    rest = value - high
    middle = rest.astype(bf16).astype(f32)
    return high, middle, rest - middle


def lanes32(value, height):
    group = lax.broadcasted_iota(jnp.int32, (height, 128), 1) // 32
    out = []
    for a in range(4):
        acc = jnp.zeros((height, 128), f32)
        for g in range(4):
            moved = pltpu.roll(value[height * g : height * (g + 1)], (32 * (g - a)) % 128, 1)
            acc = jnp.where(group == g, moved, acc)
        out.append(acc)
    return out


def put_pieces(mean, squares, bias):
    high, middle, _ = three(bias)
    rows = three(mean) + three(squares) + (high, middle)
    return jnp.concatenate(list(rows), axis=0).astype(bf16)


def merge_pieces(got, count):
    got = got.astype(f32)
    mean, squares = merge(got[:, 0] + got[:, 1] + got[:, 2], got[:, 3] + got[:, 4] + got[:, 5], count)
    total = got[0]
    for p in range(1, got.shape[0]):
        total = total + got[p]
    return mean, squares, total[6:11] + total[11:16]


def in_order(core, own, other):
    a, b = own[...].astype(f32), other[...].astype(f32)
    return jnp.where(core == 0, a, b).astype(bf16), jnp.where(core == 0, b, a).astype(bf16)


def blocks(core, first, second):
    return jnp.dot(first, pick(cotangent_columns(core, 0)), preferred_element_type=f32) + jnp.dot(
        second, pick(cotangent_columns(core, 1)), preferred_element_type=f32
    )


def pack_kernel(core_ref, both_ref, feat2_ref, cot2_ref, out_hbm, out_ref, sem):
    core = core_ref[0]
    feat_ref, cot_ref = both_ref.at[:PIX], both_ref.at[PIX:]
    x, x2 = feat_ref[...].astype(f32), feat2_ref[...].astype(f32)
    groups = group_matrix()
    total = x.sum(0, keepdims=True) + x2.sum(0, keepdims=True)
    mean = exact_dot(rows8(total), groups, 0) / CHIP
    wide = exact_dot(mean, groups, 1)[:1]
    squares = ((x - wide) ** 2).sum(0, keepdims=True) + ((x2 - wide) ** 2).sum(0, keepdims=True)
    bias = cot_ref[...].astype(f32).sum(0, keepdims=True) + cot2_ref[...].astype(f32).sum(0, keepdims=True)
    stats = put_pieces(mean[:1], exact_dot(rows8(squares), groups, 0)[:1], fold(bias))
    moved = jnp.dot(feat_ref[...], pick(feature_columns()), preferred_element_type=f32)
    moved_rest = lanes32(moved[:, 512:], 32)
    for p in range(PEERS):
        y = p % NY
        out_ref[p, 0:128] = moved[:, y * 128 : (y + 1) * 128].astype(bf16)
        out_ref[p, 128:160] = moved_rest[y].astype(bf16)
    copies = fetch(((out_ref.at[:, :F_ROWS, :], out_hbm.at[:, :F_ROWS, :]),), sem.at[0:1])
    first, second = in_order(core, cot_ref, cot2_ref)
    terms = blocks(core, first, second)
    terms_rest = lanes32(terms[:, 512:], 32)
    for p in range(PEERS):
        xx = p // NY
        out_ref[p, 160:288] = terms[:, xx * 128 : (xx + 1) * 128].astype(bf16)
        out_ref[p, 288:320] = terms_rest[xx].astype(bf16)
        out_ref[p, S_AT:] = stats
    copies += fetch(((out_ref.at[:, F_ROWS:, :], out_hbm.at[:, F_ROWS:, :]),), sem.at[1:2])
    for copy in copies:
        copy.wait()


def merge(means, squares, count):
    n = means.shape[0]
    mean = means.sum(0, keepdims=True) / n
    return mean, squares.sum(0, keepdims=True) + count * ((means - mean) ** 2).sum(0, keepdims=True)


def cot_rows(main, rest, g, side):
    lane = lax.broadcasted_iota(jnp.int32, main.shape, 1)
    main = pltpu.roll(main, 64, 1) if side else main
    return jnp.where(lane < 64, main, pltpu.roll(rest, (64 - 32 * g - 16 * side) % 128, 1))


def split_kernel(z_ref, slab_ref, out_ref):
    stats = put_pieces(*merge_pieces(slab_ref[:, S_AT:], CHIP))
    group = lax.broadcasted_iota(jnp.int32, (TC, 128), 1) // 32
    first, last = jnp.zeros((TC, 128), f32), jnp.zeros((TC, 128), f32)
    for xx in range(NX):
        tail = slab_ref[xx * NY, 288:304].astype(f32)
        first = jnp.where(group == xx, pltpu.roll(tail, 32 * xx, 1) if xx else tail, first)
        tail = slab_ref[xx * NY + NY - 1, 304:320].astype(f32)
        last = jnp.where(group == xx, pltpu.roll(tail, (32 * xx + 32) % 128, 1) if xx < 3 else tail, last)
    first = jnp.concatenate([slab_ref[xx * NY, 160:176].astype(f32) for xx in range(NX)] + [first], axis=0)
    last = jnp.concatenate(
        [slab_ref[xx * NY + NY - 1, 272:288].astype(f32) for xx in range(NX)] + [last], axis=0
    )
    for p in range(NZ):
        out_ref[p, :S_ROWS] = stats
        out_ref[p, S_ROWS:] = jnp.where(z_ref[0] < p, last, first).astype(bf16)


def back_kernel(shifted, w_hbm, out_ref, w_ref, sem):
    copies = fetch([(w_hbm.at[t // 3, t % 3], w_ref.at[t]) for t in range(9)], sem)
    total = None
    for i in range(3):
        for copy in copies[3 * i : 3 * i + 3]:
            copy.wait()
        for j in range(3):
            pixels = shifted[2 - j, (2 - i) * TC : (2 - i) * TC + PIX]
            part = lax.dot_general(w_ref[3 * i + j], pixels, (((1,), (1,)), ((), ())), preferred_element_type=f32)
            total = part if total is None else total + part
    out_ref[...] = total.T


def side_kernel(core_ref, both_ref, cot2_ref, mine_ref, theirs_ref, w_hbm, out_ref, shifted, w_ref, sem):
    j = 2 * core_ref[0]
    copies = fetch([(w_hbm.at[i, j], w_ref.at[i]) for i in range(3)], sem)
    lower = core_ref[0] == 0
    rows = (TR + 2) * TC
    mine, theirs = mine_ref[...].astype(f32), theirs_ref[...].astype(f32)
    top, bottom = jnp.where(lower, mine, theirs), jnp.where(lower, theirs, mine)
    own_top, other_top = jnp.where(lower, top[:TC], top[TC:]), jnp.where(lower, top[TC:], top[:TC])
    own_bot, other_bot = jnp.where(lower, bottom[:TC], bottom[TC:]), jnp.where(lower, bottom[TC:], bottom[:TC])
    wide = jnp.concatenate([own_top, both_ref[PIX:].astype(f32), own_bot], axis=0)
    near = jnp.concatenate([other_top, cot2_ref[...].astype(f32), other_bot], axis=0)
    near = near.reshape(TR + 2, TC, C)
    inner = jnp.where(lower, near[:, :1], near[:, TC - 1 :])
    left, right = jnp.where(lower, 0.0, inner), jnp.where(lower, inner, 0.0)
    left = jnp.broadcast_to(left, (TR + 2, TC, C)).reshape(rows, C)
    right = jnp.broadcast_to(right, (TR + 2, TC, C)).reshape(rows, C)
    col = lax.broadcasted_iota(jnp.int32, (rows, C), 0) % TC
    shifted[0] = jnp.where(col == 0, left, pltpu.roll(wide, 1, 0)).astype(bf16)
    shifted[1] = wide.astype(bf16)
    shifted[2] = jnp.where(col == TC - 1, right, pltpu.roll(wide, rows - 1, 0)).astype(bf16)
    column = wide.reshape(TR + 2, TC, C)
    column = jnp.where(lower, column[:, :1], column[:, TC - 1 :])
    total = jnp.zeros((TR, C), f32)
    for i in range(3):
        copies[i].wait()
        pixels = column[2 - i : 2 - i + TR].reshape(TR, C).astype(bf16)
        total = total + lax.dot_general(
            pixels, w_ref[i], (((1,), (1,)), ((), ())), preferred_element_type=f32
        )
    out_ref[...] = total


def sums_kernel(core_ref, stat_ref, both_ref, back_ref, side_ref, gain_ref, shift_ref,
                row_ref, da_ref, out_ref, bias_ref):
    mean, squares, bias = merge_pieces(stat_ref[:, :S_ROWS], PEERS * CHIP)
    bias_ref[...] = unfold(bias).reshape(C)
    groups = group_matrix()
    both = jnp.concatenate([mean, lax.rsqrt(squares / TOTAL + 1e-05), jnp.zeros((6, 128), f32)], axis=0)
    both = exact_dot(both, groups, 1)
    mean, rstd = both[0:1], both[1:2]
    gain, shift = gain_ref[...], shift_ref[...]
    row = lax.broadcasted_iota(jnp.int32, (8, C), 0)
    row_ref[...] = jnp.where(row == 0, mean, jnp.where(row == 1, rstd, jnp.where(row == 2, rstd * gain, shift)))
    xhat = (both_ref[:PIX].astype(f32) - mean) * rstd
    act = xhat * gain + shift
    sig = sigmoid(act)
    column = lax.broadcasted_iota(jnp.int32, (TR, TC, C), 1)
    side = jnp.broadcast_to(side_ref[...][:, None, :], (TR, TC, C))
    side = jnp.where(column == core_ref[0] * (TC - 1), side, 0.0).reshape(PIX, C)
    da = (back_ref[...] + side) * sig * (1.0 + act * (1.0 - sig))
    da_ref[...] = da
    empty = jnp.zeros((3, 128), f32)
    for side, value in enumerate((da, da * xhat)):
        block = jnp.concatenate([fold(value.sum(0, keepdims=True)), empty], axis=0)
        for p in range(side, 2 * PEERS, 2):
            out_ref[p] = block


def terms_kernel(core_ref, y_ref, z_ref, own_ref, other_hbm, edge_ref, row_ref, out_ref,
                 hid0, hid1, hid2, hid3, strips, cot3, rest, totals, other_ref, sem):
    hidden = (hid0, hid1, hid2, hid3)
    table = exact_dot(row_ref[...], pick(term_columns(y_ref[0])), 0)
    copies = fetch(((other_hbm.at[:, :F_ROWS, :], other_ref),), sem)
    core = core_ref[0]

    def put(block, peer, side):
        xx, y = peer // NY, peer % NY

        def silu(x, lanes):
            a = (x.astype(f32) - table[0:1, lanes]) * table[2:3, lanes] + table[3:4, lanes]
            return a * sigmoid(a)

        main = silu(block[:128], slice(0, 128)).astype(bf16)
        tail = silu(block[128:], slice(128, 256))
        for g in range(4):
            low = pltpu.roll(tail, (128 - 32 * g) % 128, 1).astype(bf16)
            for h in range(2):
                r = 2 * g + h
                at = pl.ds(pl.multiple_of(r * 128 + xx * 32 + side * TC, TC), TC)
                hidden[y][at, 0:128] = main[r * TC : (r + 1) * TC]
                hidden[y][at, 128:256] = low[h * TC : (h + 1) * TC]

    for peer in range(PEERS):
        xx, y = peer // NY, peer % NY
        tail = own_ref[peer, 288:320].astype(f32)
        for g in range(4):
            main = own_ref[peer, 160 + 32 * g : 192 + 32 * g].astype(f32)
            for side in range(2):
                value = cot_rows(main, tail, g, side).astype(bf16)
                for h in range(2):
                    at = (y * TR + 2 * g + h + 1) * 128 + xx * 32 + side * TC
                    strips[at : at + TC] = value[h * TC : (h + 1) * TC]
    z = z_ref[0]
    for start, peer, there in ((0, jnp.maximum(z - 1, 0), z > 0),
                               ((ROWS + 1) * 128, jnp.minimum(z + 1, NZ - 1), z < NZ - 1)):
        got = jnp.where(there, edge_ref[peer].astype(f32), 0.0)
        for xx in range(NX):
            for side in range(2):
                at = start + xx * 32 + side * TC
                value = cot_rows(got[16 + 16 * xx : 32 + 16 * xx], got[80:], xx, side)
                strips[at : at + TC] = value.astype(bf16)
    lane = lax.broadcasted_iota(jnp.int32, (NQ, 128), 1)
    for row in range(ROWS + 2):
        at = slice(row * 128, (row + 1) * 128)
        turned = strips[at].astype(f32).T[:NQ]
        before = jnp.where(lane == 0, 0.0, pltpu.roll(turned, 1, 1))
        after = jnp.where(lane == 127, 0.0, pltpu.roll(turned, 127, 1))
        cot3[0:NQ, at] = after.astype(bf16)
        cot3[NQ : 2 * NQ, at] = turned.astype(bf16)
        cot3[2 * NQ : 3 * NQ, at] = before.astype(bf16)
    cot3[3 * NQ :] = jnp.zeros((16, (ROWS + 2) * 128), bf16)
    copies[0].wait()
    for y in range(NY):
        for peer in range(y, PEERS, NY):
            put(own_ref[peer, :F_ROWS], peer, core)
            put(other_ref[peer], peer, 1 - core)
        for i in range(3):
            at = (2 - i + y * TR) * 128
            part = jnp.dot(cot3[:, at : at + TR * 128], hidden[y][...], preferred_element_type=f32)
            if y == 0:
                totals[i] = part
            else:
                totals[i] += part
    rest[...] = jnp.zeros_like(rest)
    for i in range(3):
        turned = totals[i].T
        for z in range(NZ):
            out_ref[z, 16 * i : 16 * i + 16] = turned[16 * z : 16 * z + 16].astype(bf16)
            rest[z, 4 * i : 4 * i + 4] = turned[128 + 4 * z : 132 + 4 * z]
    for z in range(NZ):
        out_ref[z, 48:64] = rest[z].astype(bf16)


def join_kernel(sums_ref, terms_ref, out_ref):
    value = sums_ref[0]
    for p in range(1, 2 * PEERS):
        value = value + sums_ref[p]
    high, middle, _ = three(value)
    lane = lax.broadcasted_iota(jnp.int32, (16, 128), 1)
    row = lax.broadcasted_iota(jnp.int32, (16, 128), 0)
    tails = [
        jnp.concatenate([pltpu.roll(middle, (112 - 16 * c) % 128, 1) for c in (2 * k, 2 * k + 1)], axis=0)
        for k in range(4)
    ]
    for z in range(NZ):
        for k in range(4):
            at = slice(16 * k, 16 * k + 16)
            block = terms_ref[z, at].astype(f32)
            left, right = block[:, :128], block[:, 128:]
            right = jnp.where(lane >= 112, tails[k], right)
            if k == 3:
                left = jnp.concatenate([left[:12], high[:4]], axis=0)
                right = jnp.where(row == 13, high[4:5], right)
            out_ref[z, at] = jnp.concatenate([left, right], axis=1).astype(bf16)


def total_kernel(got_ref, out_ref):
    lane = lax.broadcasted_iota(jnp.int32, (8, 128), 1)
    middle = jnp.zeros((8, 128), f32)
    upper, right = got_ref[0, 48:].astype(f32), got_ref[0, :, 128:].astype(f32)
    for z in range(1, NZ):
        upper = upper + got_ref[z, 48:].astype(f32)
        right = right + got_ref[z, :, 128:].astype(f32)
    high = jnp.concatenate([upper[12:16, :128], upper[13:14, 128:]], axis=0)
    for c in range(8):
        part = pltpu.roll(right[8 * c : 8 * c + 8], (16 * c - 112) % 128, 1)
        middle = jnp.where(lane // 16 == c, part, middle)
    out_ref[...] = rows8(unfold(high + middle[:5]))


def final_kernel(core_ref, own_ref, other_ref, both_ref, da_ref, row_ref, gain_ref,
                 grad_ref, gain_grad_ref, shift_grad_ref):
    own, other = own_ref[0:1], other_ref[0:1]
    lower = core_ref[0] == 0
    sums = (jnp.where(lower, own, other), jnp.where(lower, other, own))
    shift_grad_ref[...], gain_grad_ref[...] = [value.reshape(C) for value in sums]
    groups = group_matrix()
    gain, mean, rstd = gain_ref[...], row_ref[0:1], row_ref[1:2]

    both = jnp.concatenate([gain * sums[0], gain * sums[1], jnp.zeros((6, C), f32)], axis=0)
    both = exact_dot(exact_dot(both, groups, 0), groups, 1) / TOTAL
    first, second = both[0:1], both[1:2]
    xhat = (both_ref[:PIX].astype(f32) - mean) * rstd
    grad_ref[...] = (rstd * (da_ref[...] * gain - first - xhat * second)).astype(bf16)


def gather_kernel(got_ref, weight_ref):
    weight = got_ref[0].astype(f32)
    for z in range(1, NZ):
        weight = weight + got_ref[z].astype(f32)
    for i in range(3):
        for j in range(3):
            at = slice(j * NQ, (j + 1) * NQ)
            weight_ref[i, j, 0:16] = weight[16 * i : 16 * i + 16, at]
            weight_ref[i, j, 16:20] = weight[48 + 4 * i : 52 + 4 * i, at]


def flip(value):
    return lax.ppermute(value, "core", [(0, 1), (1, 0)])


def shape(dims, dtype):
    return jax.ShapeDtypeStruct(dims, dtype)


def body(features, cotangent, conv_weight, gain, shift):
    core, y, z = lax.axis_index("core"), lax.axis_index("y"), lax.axis_index("z")
    at_core, at_y, at_z = core.reshape(1), y.reshape(1), z.reshape(1)
    feat, cot = features.reshape(PIX, C), cotangent.reshape(PIX, C)
    gain, shift = gain.reshape(1, C), shift.reshape(1, C)
    cot2, feat2 = flip(cot), flip(feat)
    both = jnp.concatenate([feat, cot])
    edge = jnp.where(
        core == 0,
        jnp.concatenate([cot[PIX - TC :], cot2[PIX - TC :]]),
        jnp.concatenate([cot2[:TC], cot[:TC]]),
    )
    count = NZ * NY
    ways = [(2 * k, 2 * k + 2) for k in range(count - 1)] + [(2 * k + 3, 2 * k + 1) for k in range(count - 1)]
    mine = lax.ppermute(edge, ("z", "y", "core"), ways)

    packed = pl.pallas_call(
        pack_kernel,
        out_shape=shape((PEERS, G_ROWS, 128), bf16),
        in_specs=[smem()] + [vmem()] * 3,
        out_specs=hbm(),
        scratch_shapes=[pltpu.VMEM((PEERS, G_ROWS, 128), bf16), pltpu.SemaphoreType.DMA((2,))],
        compiler_params=params(),
        cost_estimate=pl.CostEstimate(flops=1 << 28, bytes_accessed=2 << 20, transcendentals=0),
        name="pack",
    )(at_core, both, feat2, cot2)
    slab = lax.all_to_all(packed, ("x", "y"), 0, 0)
    theirs = flip(mine)
    side, shifted = pl.pallas_call(
        side_kernel,
        out_shape=(shape((TR, C), f32), shape((3, (TR + 2) * TC, C), bf16)),
        in_specs=[smem()] + [vmem()] * 4 + [hbm()],
        out_specs=(vmem(), vmem()),
        scratch_shapes=[pltpu.VMEM((3, C, C), bf16), pltpu.SemaphoreType.DMA((3,))],
        compiler_params=params(),
        name="side",
    )(at_core, both, cot2, mine, theirs, conv_weight)
    slab, side = lax.optimization_barrier((slab, side))
    pairs = [(2 * k + 1, 2 * k + 2) for k in range(NX - 1)]
    side = lax.ppermute(side, ("x", "core"), pairs + [(b, a) for a, b in pairs])
    edges = pl.pallas_call(
        split_kernel,
        out_shape=shape((NZ, E_ROWS, 128), bf16),
        in_specs=[smem(), vmem()],
        out_specs=vmem(),
        compiler_params=params(),
        name="split",
    )(at_z, slab)
    late, edges = lax.optimization_barrier((slab, edges))
    slab_other = flip(late)
    edges = lax.all_to_all(edges, "z", 0, 0)
    back = pl.pallas_call(
        back_kernel,
        out_shape=shape((PIX, C), f32),
        in_specs=[vmem(), hbm()],
        out_specs=vmem(),
        scratch_shapes=[pltpu.VMEM((9, C, C), bf16), pltpu.SemaphoreType.DMA((9,))],
        compiler_params=params(),
        cost_estimate=pl.CostEstimate(flops=2 * PIX * 9 * C * C, bytes_accessed=18 * C * C, transcendentals=0),
        name="back",
    )(shifted, conv_weight)
    row, da, sums, bias_grad = pl.pallas_call(
        sums_kernel,
        out_shape=(
            shape((8, C), f32),
            shape((PIX, C), f32),
            shape((2 * PEERS, 8, 128), f32),
            shape((C,), f32),
        ),
        in_specs=[smem()] + [vmem()] * 6,
        out_specs=(vmem(),) * 4,
        compiler_params=params(),
        name="sums",
    )(at_core, edges, both, back, side, gain, shift)
    sums = lax.all_to_all(sums, ("y", "x", "core"), 0, 0)

    terms = pl.pallas_call(
        terms_kernel,
        out_shape=shape((NZ, W_ROWS, 256), bf16),
        in_specs=[smem()] * 3 + [vmem(), hbm(), vmem(), vmem()],
        out_specs=vmem(),
        scratch_shapes=[
            pltpu.VMEM((TR * 128, 256), bf16),
            pltpu.VMEM((TR * 128, 256), bf16),
            pltpu.VMEM((TR * 128, 256), bf16),
            pltpu.VMEM((TR * 128, 256), bf16),
            pltpu.VMEM(((ROWS + 2) * 128, 128), bf16),
            pltpu.VMEM((256, (ROWS + 2) * 128), bf16),
            pltpu.VMEM((NZ, 16, 256), f32),
            pltpu.VMEM((3, 256, 256), f32),
            pltpu.VMEM((PEERS, F_ROWS, 128), bf16),
            pltpu.SemaphoreType.DMA((1,)),
        ],
        compiler_params=params(),
        cost_estimate=pl.CostEstimate(
            flops=2 * PIX * 9 * C * C, bytes_accessed=4 << 20, transcendentals=ROWS * 128 * 256
        ),
        name="terms",
    )(at_core, at_y, at_z, slab, slab_other, edges, row)

    joined = pl.pallas_call(
        join_kernel,
        out_shape=shape((NZ, W_ROWS, 256), bf16),
        in_specs=[vmem()] * 2,
        out_specs=vmem(),
        compiler_params=params(),
        name="join",
    )(sums, terms)
    joined = lax.all_to_all(joined, "z", 0, 0)
    total = pl.pallas_call(
        total_kernel,
        out_shape=shape((8, C), f32),
        in_specs=[vmem()],
        out_specs=vmem(),
        compiler_params=params(),
        name="total",
    )(joined)
    weight_grad = pl.pallas_call(
        gather_kernel,
        out_shape=shape((3, 3, 20, NQ), f32),
        in_specs=[vmem()],
        out_specs=vmem(),
        compiler_params=params(),
        cost_estimate=pl.CostEstimate(flops=1 << 22, bytes_accessed=1 << 20, transcendentals=0),
        name="gather",
    )(joined)
    grad, gain_grad, shift_grad = pl.pallas_call(
        final_kernel,
        out_shape=(shape((PIX, C), bf16),) + (shape((C,), f32),) * 2,
        in_specs=[smem()] + [vmem()] * 6,
        out_specs=(vmem(),) * 3,
        compiler_params=params(),
        name="final",
    )(at_core, total, flip(total), both, da, row, gain)
    return grad.reshape(features.shape), weight_grad, gain_grad, shift_grad, bias_grad


def solution(mesh):
    grid = Mesh(mesh.devices.reshape(NZ, NY, NX, 2), ("z", "y", "x", "core"))
    rows, cols = ("z", "y"), ("x", "core")
    tiled = P(rows, cols, None)
    return jax.shard_map(
        body,
        mesh=grid,
        in_specs=(tiled, tiled, P(), P(), P()),
        out_specs=(tiled, P(None, None, rows, cols), P(), P(), P()),
        check_vma=False,
    )
```
